128 devices in a mesh: enc: 32 (over z, x, core), dec: 4 (over y).
Axes of the slice: x: 4, y: 4, z: 4, core: 2. Of those that a mesh axis runs over, the one named last changes fastest.
Arguments:
- enc_rows: bfloat16 [16384, 4096], P('enc'), may hold values from -6 to 6
- key_weight: bfloat16 [4096, 4096], P('enc', 'dec'), may hold values from -0.09375 to 0.09375
- value_weight: bfloat16 [4096, 4096], P('enc', 'dec'), may hold values from -0.09375 to 0.09375
- queries: bfloat16 [32, 16, 4096], P('enc', None, 'dec'), may hold values from -8 to 8
- ctx_grad: bfloat16 [32, 16, 4096], P('enc', None, 'dec'), may hold values from -6 to 6
- passage_len: int32 [32, 4], P('enc'), may hold values from 1 to 256, 512 in all within a row
- passage_question: int32 [128, 1], P('enc'), may hold values from 0 to 31
Outputs:
- ctx: float32 [32, 16, 4096], P('enc', None, 'dec')
- enc_grad: float32 [16384, 4096], P('enc', 'dec')
The draws below stay inside these ranges and needn't reach their ends.
Inputs may be any that keep to these rules, and one draw needn't show every extreme that they name: Each row of passage_len sums to 512 and its largest entry is 256. `passage_question`: every question has at least one passage.
All inputs are finite; a program needn't handle non-finite values.
Results may differ from the reference program's by a relative error of at most 0.02.
Values may be sent and summed in bfloat16 or wider, within the bound.
No kernel may reach another device: no remote copies, remote signals or barrier semaphores. Data moves between devices by JAX's collectives and lax.ppermute only.
A program may use at most 128 MiB of HBM per device.

```python
import math
import jax
import jax.numpy as jnp
import numpy as np
from jax import lax

D = 4096
HEAD_DIM = 64
TOK_DEV = 512
PASS_DEV = 4
DEC_TOK = 16
HEADS = 64
ENC_DEVS = 32
TOKENS = 16384
PASSAGES = 128
QUESTIONS = 32


def draw_queries(key, part):
    key = jax.random.fold_in(key, 11)
    first = jax.random.fold_in(key, 0)
    shape = (QUESTIONS, DEC_TOK, D)
    values = jnp.clip(jax.random.normal(first, shape, jnp.float32) * 0.125, -0.75, 0.75)
    return values.astype(jnp.bfloat16)


def block_scale(stream_key, extent, cuts, low, top_value):
    loudness, own = 1.0, jax.random.fold_in(stream_key, 6)
    for position, blocks in cuts:
        heights = jnp.exp(jax.random.uniform(jax.random.fold_in(own, position), (blocks,), jnp.float32, low / len(cuts), top_value / len(cuts)))
        loudness = loudness * jnp.repeat(heights, extent[position] // blocks).reshape([-1 if axis == position else 1 for axis in range(len(extent))])
    return loudness


def picks_of(rng, rows, count, top, lift):
    sequence = jax.random.permutation(jax.random.fold_in(rng, 1), count)
    pull = sequence
    for power in range(3):
        pull = pull * pull // count
    pull = pull * lift // count
    tickets = jax.random.randint(jax.random.fold_in(rng, 2), (rows, count), 0, 4096) + pull
    holders = jax.random.permutation(jax.random.fold_in(rng, 3), rows)[jnp.arange(count) % rows]
    tickets = jnp.where(jnp.arange(rows)[:, None] == holders[None, :], 1 << 14, tickets)
    priority = tickets * count + jnp.arange(count)
    return lax.top_k(priority.astype(jnp.int32), top)[1].astype(jnp.int32)


def length_profile(amount, total, reach, lean):
    weights = [(1 << 20) // math.isqrt(standing ** lean) + 1 for standing in range(2, amount + 1)]
    spare, given = total - reach - (amount - 1), [1] * (amount - 1)
    while spare > 0:
        candidates = [i for i in range(amount - 1) if given[i] < reach]
        mass, remaining = sum([weights[i] for i in candidates]), spare
        for i in candidates:
            addition = min(reach - given[i], max(1, remaining * weights[i] // mass), spare)
            given[i] = given[i] + addition
            spare = spare - addition
    return np.array([reach] + given)


def ragged_sizes(stream_key, count, total, bound, skew):
    if count == 2:
        one = jax.random.randint(stream_key, (), max(1, total - bound), min(bound, total - 1) + 1)
        return jnp.stack([one, total - one])
    tallies = jnp.asarray(length_profile(count, total, bound, skew), jnp.int32)
    twos = (count - 1) // 2
    source_of, receiver = tallies[1:1 + 2 * twos:2], tallies[2:2 + 2 * twos:2]
    margin = jnp.minimum(source_of - 1, bound - receiver)
    passed = jax.random.randint(jax.random.fold_in(stream_key, 1), (twos,), 0, 1 << 20) % (margin + 1)
    tallies = tallies.at[1:1 + 2 * twos:2].set(source_of - passed).at[2:2 + 2 * twos:2].set(receiver + passed)
    return tallies[jax.random.permutation(jax.random.fold_in(stream_key, 2), count)]


def centred(own_key, shape, spread, most, cuts=(), kind=jnp.bfloat16):
    level = block_scale(own_key, shape, cuts, -0.22, 0.18) if cuts else 1.0
    values = jax.random.normal(own_key, shape, jnp.float32) * spread * level
    return jnp.minimum(jnp.maximum(values, -most), most).astype(kind)


def setup_inputs(seed: int = 0) -> dict:
    seeds = jax.random.split(jax.random.key(seed), 8)
    enc_rows = centred(seeds[0], (TOKENS, D), 1.0, 6.0, ((0, 32),))
    key_weight = centred(seeds[1], (D, D), D ** -0.5, 0.09375, ((0, 32), (1, 4)))
    value_weight = centred(seeds[2], (D, D), D ** -0.5, 0.09375, ((0, 32), (1, 4)))
    queries = draw_queries(jax.random.fold_in(seeds[7], 71), 0)
    ctx_grad = centred(seeds[4], (QUESTIONS, DEC_TOK, D), 1.0, 6.0, ((0, 32), (2, 4)))
    passage_len = jax.vmap(lambda own: ragged_sizes(own, PASS_DEV, TOK_DEV, TOK_DEV // 2, 1))(jax.random.split(seeds[5], ENC_DEVS)).reshape((ENC_DEVS, PASS_DEV)).astype(jnp.int32)
    passage_question = picks_of(seeds[6], PASSAGES, QUESTIONS, 1, 256)
    return dict(enc_rows=enc_rows, key_weight=key_weight, value_weight=value_weight, queries=queries, ctx_grad=ctx_grad, passage_len=passage_len, passage_question=passage_question)


def reference(enc_rows, key_weight, value_weight, queries, ctx_grad, passage_len, passage_question):
    key_rows = jnp.dot(enc_rows, key_weight, preferred_element_type=jnp.float32).astype(jnp.bfloat16)
    value_rows = jnp.dot(enc_rows, value_weight, preferred_element_type=jnp.float32).astype(jnp.bfloat16)
    passage_ends = jnp.cumsum(passage_len, axis=1)
    positions = jnp.arange(TOK_DEV, dtype=jnp.int32)
    segment = jnp.sum((positions[None, :, None] >= passage_ends[:, None, :]).astype(jnp.int32), axis=2)
    slot_index = segment + (jnp.arange(ENC_DEVS, dtype=jnp.int32) * PASS_DEV)[:, None]
    token_question = passage_question[:, 0][slot_index.reshape(-1)]
    row_question = jnp.repeat(jnp.arange(QUESTIONS, dtype=jnp.int32), DEC_TOK)
    inside = row_question[:, None] == token_question[None, :]
    row_total = QUESTIONS * DEC_TOK
    query_heads = queries.reshape(row_total, HEADS, HEAD_DIM).transpose(1, 0, 2)
    grad_heads = ctx_grad.reshape(row_total, HEADS, HEAD_DIM).transpose(1, 0, 2)
    key_heads = key_rows.reshape(TOKENS, HEADS, HEAD_DIM).transpose(1, 0, 2)
    value_heads = value_rows.reshape(TOKENS, HEADS, HEAD_DIM).transpose(1, 0, 2)

    def one_head(operands):
        query_h, key_h, value_h, grad_h = operands
        scores = jnp.dot(query_h, key_h.T, preferred_element_type=jnp.float32)
        score_top = jnp.max(jnp.where(inside, scores, -1e30), axis=1, keepdims=True)
        unnorm = jnp.where(inside, jnp.exp(scores - score_top), 0.0)
        total = jnp.sum(unnorm, axis=1, keepdims=True)
        context = jnp.dot(unnorm.astype(jnp.bfloat16), value_h, preferred_element_type=jnp.float32) / total
        delta = jnp.sum(grad_h.astype(jnp.float32) * context, axis=1, keepdims=True)
        probs = unnorm / total
        value_grad = jnp.dot(probs.astype(jnp.bfloat16).T, grad_h, preferred_element_type=jnp.float32)
        dprob = jnp.dot(grad_h, value_h.T, preferred_element_type=jnp.float32)
        ds_b = (probs * (dprob - delta)).astype(jnp.bfloat16)
        key_grad = jnp.dot(ds_b.T, query_h, preferred_element_type=jnp.float32)
        return context, key_grad.astype(jnp.bfloat16), value_grad.astype(jnp.bfloat16)

    context, key_grad, value_grad = lax.map(one_head, (query_heads, key_heads, value_heads, grad_heads))
    ctx = context.transpose(1, 0, 2).reshape(QUESTIONS, DEC_TOK, D).astype(jnp.float32)
    key_grad_rows = key_grad.transpose(1, 0, 2).reshape(TOKENS, D)
    value_grad_rows = value_grad.transpose(1, 0, 2).reshape(TOKENS, D)
    enc_grad = jnp.dot(key_grad_rows, key_weight.T, preferred_element_type=jnp.float32)
    enc_grad = enc_grad + jnp.dot(value_grad_rows, value_weight.T, preferred_element_type=jnp.float32)
    return ctx, enc_grad
```

```python
import functools

import jax
import jax.numpy as jnp
from jax import lax
from jax.experimental import pallas as pl
from jax.experimental.pallas import tpu as pltpu
from jax.sharding import Mesh, PartitionSpec as P

BF = jnp.bfloat16
F32 = jnp.float32
NZ, NX, NC, NY = 4, 4, 2, 4
ENC = ("z", "x", "core")
ROWS = 512
D = 4096
HALF = 512
CHUNK = 256
DEC = 16
NPASS = 4
PAIRS = 4
LOW = -1e30
NT = (((1,), (1,)), ((), ()))
TN = (((0,), (0,)), ((), ()))


def perm(v, axis, shift):
    n = {"z": NZ, "x": NX, "core": NC, "dec": NY}[axis]
    return lax.ppermute(v, axis, [(i, (i + shift) % n) for i in range(n)])


def gather4(v, axis):
    return [v] + [perm(v, axis, -o) for o in (1, 2, 3)]


def ring_near(v, axis):
    return perm(v, axis, -1), perm(v, axis, 1)


def ring_far(up, down, axis):
    return perm(up[0], axis, -1), perm(down[1], axis, 1)


def params(mib):
    return pltpu.CompilerParams(vmem_limit_bytes=mib * 1024 * 1024)


def proj_kernel(sizes, has_acc, offs, own_ref, oth_ref, *refs):
    weights = refs[: len(sizes[0]) + len(sizes[1])]
    rest = refs[len(weights) :]
    acc_ref = rest[0] if has_acc else None
    out_ref = rest[-1]
    step = pl.program_id(0)

    def run(enc_ref):
        at = 0
        place = 0
        for side in range(2):
            total = None
            for count in sizes[side]:
                w = weights[place][...].reshape(count * CHUNK, CHUNK)
                place += 1
                parts = []
                for k in range(count):
                    start = pl.multiple_of(offs[at + k] * CHUNK, CHUNK)
                    parts.append(enc_ref[:, pl.ds(start, CHUNK)])
                at += count
                lhs = jnp.concatenate(parts, axis=1)
                term = jnp.dot(lhs, w, preferred_element_type=F32)
                total = term if total is None else total + term
            cols = slice(side * CHUNK, (side + 1) * CHUNK)
            if has_acc:
                total = total + acc_ref[0, :, cols]
            out_ref[0, :, cols] = total.astype(out_ref.dtype)

    pl.when(step < 2)(lambda: run(own_ref))
    pl.when(step >= 2)(lambda: run(oth_ref))


def project(offs, own, other, a_blocks, b_blocks, acc, dtype):
    sizes = tuple(tuple(b.size // (CHUNK * CHUNK) for b in g) for g in (a_blocks, b_blocks))
    blocks = list(a_blocks) + list(b_blocks)
    tile = ROWS // 2

    def whole(b):
        return pl.BlockSpec(b.shape, lambda i, o: (0,) * b.ndim)

    tile_spec = pl.BlockSpec((1, tile, HALF), lambda i, o: (i // 2, i % 2, 0))
    in_specs = [
        pl.BlockSpec((tile, D), lambda i, o: (jnp.minimum(i, 1), 0)),
        pl.BlockSpec((tile, D), lambda i, o: (jnp.maximum(i - 2, 0), 0)),
    ] + [whole(b) for b in blocks]
    args = [offs, own, other] + blocks
    if acc is not None:
        in_specs.append(tile_spec)
        args.append(acc)
    depth = CHUNK * sum(sizes[0])
    return pl.pallas_call(
        functools.partial(proj_kernel, sizes, acc is not None),
        grid_spec=pltpu.PrefetchScalarGridSpec(
            num_scalar_prefetch=1, grid=(4,), in_specs=in_specs, out_specs=tile_spec
        ),
        out_shape=jax.ShapeDtypeStruct((2, ROWS, HALF), dtype),
        compiler_params=params(40),
        cost_estimate=pl.CostEstimate(
            flops=2 * 2 * ROWS * depth * HALF,
            bytes_accessed=2 * 2 * ROWS * D + 2 * depth * HALF + 4 * 2 * ROWS * HALF,
            transcendentals=0,
        ),
    )(*args)


def pair_matrix(meta, qg_ref, side, pair, which):
    low = lax.broadcasted_iota(jnp.int32, (DEC, 128), 1) < 64
    parts = []
    for p in range(NPASS):
        tile = qg_ref[meta[side * NPASS + p], which, :, pair * 128 : (pair + 1) * 128]
        zero = jnp.zeros_like(tile)
        parts += [jnp.where(low, tile, zero), jnp.where(low, zero, tile)]
    return jnp.concatenate(parts, axis=0)


def lane_value(meta, base, side):
    lane = lax.broadcasted_iota(jnp.int32, (1, 128), 1) // 32
    value = jnp.zeros((1, 128), jnp.int32)
    for p in range(NPASS):
        value = jnp.where(lane == p, meta[base + side * NPASS + p], value)
    return value


def inside_mask(meta, side):
    row = lax.broadcasted_iota(jnp.int32, (ROWS, 128), 0)
    return (row >= lane_value(meta, 8, side)) & (row < lane_value(meta, 16, side))


def dot_nt(a, b):
    return lax.dot_general(a, b, NT, preferred_element_type=F32)


def stats_kernel(meta, k_ref, qg_ref, out_ref):
    for side in range(2):
        inside = inside_mask(meta, side)
        question = lane_value(meta, 24, side).astype(F32)
        for pair in range(PAIRS):
            cols = slice(pair * 128, (pair + 1) * 128)
            scores = dot_nt(k_ref[side, :, cols], pair_matrix(meta, qg_ref, side, pair, 0))
            scores = jnp.where(inside, scores, LOW)
            top = jnp.max(scores, axis=0, keepdims=True)
            total = jnp.sum(jnp.exp(scores - top), axis=0, keepdims=True)
            at = side * PAIRS + pair
            out_ref[at : at + 1, :] = top
            out_ref[8 + at : 9 + at, :] = total
            out_ref[16 + at : 17 + at, :] = question


def over_group(own_question, parts, start, combine):
    totals = [None, None]
    for question, value in parts:
        for k in range(NPASS):
            q = pltpu.roll(question, 32 * k, 1) if k else question
            v = pltpu.roll(value, 32 * k, 1) if k else value
            for side in range(2):
                term = jnp.where(q == own_question[side], v, start)
                totals[side] = term if totals[side] is None else combine(totals[side], term)
    return [combine(t[0:PAIRS], t[PAIRS:]) for t in totals]


def forward_kernel(meta, k_ref, v_ref, qg_ref, st_ref, ml_ref, delta_ref, dense_ref):
    own_question = [st_ref[0, 16 + s * PAIRS : 17 + s * PAIRS, :] for s in range(2)]
    n = st_ref.shape[0]
    tops = over_group(
        own_question, [(st_ref[d, 16:24], st_ref[d, 0:8]) for d in range(n)], LOW, jnp.maximum
    )
    both = [jnp.concatenate([t, t], axis=0) for t in tops]
    totals = [None, None]
    for d in range(n):
        question, top, total = st_ref[d, 16:24], st_ref[d, 0:8], st_ref[d, 8:16]
        for k in range(NPASS):
            q = pltpu.roll(question, 32 * k, 1) if k else question
            m = pltpu.roll(top, 32 * k, 1) if k else top
            l = pltpu.roll(total, 32 * k, 1) if k else total
            for side in range(2):
                hit = q == own_question[side]
                scale = jnp.exp(jnp.where(hit, m - both[side], 0.0))
                term = jnp.where(hit, scale * l, 0.0)
                totals[side] = term if totals[side] is None else totals[side] + term
    dense_ref[...] = jnp.zeros_like(dense_ref)
    low = lax.broadcasted_iota(jnp.int32, (DEC, 128), 1) < 64
    for side in range(2):
        inside = inside_mask(meta, side)
        total = totals[side][0:PAIRS] + totals[side][PAIRS:]
        inverse = 1.0 / total
        ml_ref[side * PAIRS : (side + 1) * PAIRS, :] = tops[side]
        ml_ref[8 + side * PAIRS : 8 + (side + 1) * PAIRS, :] = inverse
        for pair in range(PAIRS):
            cols = slice(pair * 128, (pair + 1) * 128)
            scores = dot_nt(k_ref[side, :, cols], pair_matrix(meta, qg_ref, side, pair, 0))
            unnorm = jnp.where(inside, jnp.exp(scores - tops[side][pair : pair + 1]), 0.0)
            unnorm_b = unnorm.astype(BF)
            values = v_ref[side, :, cols]
            dprob = dot_nt(values, pair_matrix(meta, qg_ref, side, pair, 1))
            inv = inverse[pair : pair + 1]
            at = side * PAIRS + pair
            delta_ref[at : at + 1, :] = (
                jnp.sum(unnorm_b.astype(F32) * dprob, axis=0, keepdims=True) * inv
            )
            weighted = lax.dot_general(values, unnorm_b, TN, preferred_element_type=F32)
            context = (weighted * inv).T
            for p in range(NPASS):
                part = jnp.where(
                    low, context[p * 32 : p * 32 + 16], context[p * 32 + 16 : p * 32 + 32]
                )
                q = meta[side * NPASS + p]
                dense_ref[q, :, cols] += part


def backward_kernel(meta, k_ref, v_ref, qg_ref, st_ref, ml_ref, dl_ref, own_ref, oth_ref):
    own_question = [st_ref[0, 16 + s * PAIRS : 17 + s * PAIRS, :] for s in range(2)]
    n = st_ref.shape[0]
    deltas = over_group(
        own_question, [(st_ref[d, 16:24], dl_ref[d]) for d in range(n)], 0.0, jnp.add
    )
    for side in range(2):
        inside = inside_mask(meta, side)
        out_ref = own_ref if side == 0 else oth_ref
        for pair in range(PAIRS):
            cols = slice(pair * 128, (pair + 1) * 128)
            at = side * PAIRS + pair
            queries = pair_matrix(meta, qg_ref, side, pair, 0)
            grads = pair_matrix(meta, qg_ref, side, pair, 1)
            scores = dot_nt(k_ref[side, :, cols], queries)
            unnorm = jnp.where(inside, jnp.exp(scores - ml_ref[at : at + 1, :]), 0.0)
            probs = unnorm * ml_ref[8 + at : 9 + at, :]
            dprob = dot_nt(v_ref[side, :, cols], grads)
            ds = (probs * (dprob - deltas[side][pair : pair + 1])).astype(BF)
            out_ref[0, :, cols] = jnp.dot(ds, queries, preferred_element_type=F32).astype(BF)
            out_ref[1, :, cols] = jnp.dot(
                probs.astype(BF), grads, preferred_element_type=F32
            ).astype(BF)


def small_call(kernel, meta, args, out_shape, name_flops):
    def whole(a):
        return pl.BlockSpec(a.shape, lambda i, m: (0,) * len(a.shape))

    return pl.pallas_call(
        kernel,
        grid_spec=pltpu.PrefetchScalarGridSpec(
            num_scalar_prefetch=1,
            grid=(1,),
            in_specs=[whole(a) for a in args],
            out_specs=jax.tree.map(whole, out_shape),
        ),
        out_shape=out_shape,
        compiler_params=params(40),
        cost_estimate=pl.CostEstimate(
            flops=name_flops, bytes_accessed=4 * 1024 * 1024, transcendentals=512 * 1024
        ),
    )(meta, *args)


def grad_kernel(add, zi, own_ref, got_ref, *refs):
    weights, outs = refs[:8], refs[8:]
    lhs = jnp.concatenate([own_ref[0], got_ref[0], own_ref[1], got_ref[1]], axis=1)
    rhs = jnp.concatenate([w[...].reshape(CHUNK, CHUNK) for w in weights], axis=1)
    total = dot_nt(lhs, rhs)
    if len(outs) == 1:
        outs[0][...] = total.astype(outs[0].dtype)
    else:
        outs[0][...] = total[: ROWS // 2].astype(outs[0].dtype)
        outs[1][...] = total[ROWS // 2 :].astype(outs[1].dtype)


def grad_block(zi, own, got, wk, wk_got, wv, wv_got, dtypes):
    a_spec = pl.BlockSpec((1, 1, 1, CHUNK, CHUNK), lambda n, z: (0, z[0], n, 0, 0))
    b_spec = pl.BlockSpec((1, 1, 1, CHUNK, CHUNK), lambda n, z: (1, n, z[0], 0, 0))
    full = pl.BlockSpec((2, ROWS, HALF), lambda n, z: (0, 0, 0))
    rows = ROWS // len(dtypes)
    out_specs = [pl.BlockSpec((rows, CHUNK), lambda n, z: (0, n)) for _ in dtypes]
    return pl.pallas_call(
        functools.partial(grad_kernel, False),
        grid_spec=pltpu.PrefetchScalarGridSpec(
            num_scalar_prefetch=1,
            grid=(4,),
            in_specs=[full, full] + [a_spec, b_spec] * 4,
            out_specs=out_specs,
        ),
        out_shape=[jax.ShapeDtypeStruct((rows, 4 * CHUNK), t) for t in dtypes],
        compiler_params=params(40),
        cost_estimate=pl.CostEstimate(
            flops=2 * ROWS * 1024 * 2048, bytes_accessed=8 * 1024 * 1024, transcendentals=0
        ),
    )(zi, own, got, wk, wk, wk_got, wk_got, wv, wv, wv_got, wv_got)


def finish_kernel(place, base_ref, plus_top, plus_low, minus_top, minus_low, out_ref):
    half = ROWS // 2
    out_ref[:half] = base_ref[:half] + plus_top[...].astype(F32) + minus_top[...].astype(F32)
    out_ref[half:] = base_ref[half:] + plus_low[...].astype(F32) + minus_low[...].astype(F32)


def finish(place, base, parts):
    half = pl.BlockSpec((ROWS // 2, CHUNK), lambda n, p: (0, n))
    return pl.pallas_call(
        finish_kernel,
        grid_spec=pltpu.PrefetchScalarGridSpec(
            num_scalar_prefetch=1,
            grid=(4,),
            in_specs=[pl.BlockSpec((ROWS, CHUNK), lambda n, p: (0, n))] + [half] * 4,
            out_specs=pl.BlockSpec((ROWS, CHUNK), lambda n, p: (0, p[n])),
        ),
        out_shape=jax.ShapeDtypeStruct((ROWS, 4 * CHUNK), F32),
        cost_estimate=pl.CostEstimate(
            flops=ROWS * 2048, bytes_accessed=6 * 1024 * 1024, transcendentals=0
        ),
    )(place, base, *parts)


def body(enc_rows, key_weight, value_weight, queries, ctx_grad, passage_len, passage_question):
    z, x, core, y = (lax.axis_index(a) for a in ("z", "x", "core", "dec"))
    four = jnp.arange(4, dtype=jnp.int32)

    cat = jnp.concatenate([key_weight, value_weight, queries[0], ctx_grad[0]], axis=0)
    mine = lax.dynamic_slice_in_dim(cat, core * HALF, HALF, 1)
    theirs = lax.dynamic_slice_in_dim(cat, (1 - core) * HALF, HALF, 1)
    got = perm(theirs, "core", 1)
    first = jnp.where(core == 0, mine, got)
    second = jnp.where(core == 0, got, mine)
    chip = jnp.stack(
        [
            jnp.concatenate([first[:128], second[:128]], axis=0),
            jnp.concatenate([first[128:256], second[128:256]], axis=0),
        ]
    )
    qg = jnp.stack([first[256:].reshape(2, DEC, HALF), second[256:].reshape(2, DEC, HALF)])
    numbers = jnp.concatenate([passage_len[0], passage_question[:, 0]])
    other_numbers = perm(numbers, "core", 1)
    enc_other = perm(lax.optimization_barrier((enc_rows, got))[0], "core", 1)

    a_first = gather4(chip[:, :, :CHUNK], "x")
    b_first = gather4(chip[:, :, CHUNK:], "z")
    qg_x = jnp.stack(gather4(qg, "x"))
    qg_all = jnp.stack(gather4(qg_x, "z")).reshape(32, 2, DEC, HALF)
    a_key, a_value = (jnp.stack([p[t] for p in a_first]).reshape(2, 512, CHUNK) for t in (0, 1))
    b_key, b_value = (jnp.stack([p[t] for p in b_first]).reshape(2, 512, CHUNK) for t in (0, 1))
    ak_up, ak_down = ring_near(a_key, "z")
    bk_up, bk_down = ring_near(b_key, "x")
    a_value, b_value, ak_up, ak_down, bk_up, bk_down = lax.optimization_barrier(
        (a_value, b_value, ak_up, ak_down, bk_up, bk_down)
    )
    ak_far = ring_far(ak_up, ak_down, "z")
    bk_far = ring_far(bk_up, bk_down, "x")
    av_up, av_down = ring_near(a_value, "z")
    bv_up, bv_down = ring_near(b_value, "x")
    av_far = ring_far(av_up, av_down, "z")
    bv_far = ring_far(bv_up, bv_down, "x")

    zs, xs = (z + four) % 4, (x + four) % 4
    a_chips = zs[:, None] * 4 + xs[None, :]
    b_chips = zs[None, :] * 4 + xs[:, None]
    near = jnp.array([0, 1, 3])
    offs_near = jnp.concatenate([a_chips[near].reshape(-1), b_chips[near].reshape(-1)])
    offs_far = jnp.concatenate([a_chips[2], b_chips[2]])

    def project_all(a_own, a_up, a_down, a_far, b_own, b_up, b_down, b_far):
        part = project(
            offs_near, enc_rows, enc_other, [a_own, a_up, a_down], [b_own, b_up, b_down], None, F32
        )
        return project(offs_far, enc_rows, enc_other, a_far, b_far, part, BF)

    keys = project_all(a_key, ak_up, ak_down, ak_far, b_key, bk_up, bk_down, bk_far)

    all_numbers = jnp.stack([numbers, other_numbers])
    lengths, questions = all_numbers[:, :4], all_numbers[:, 4:]
    ends = jnp.cumsum(lengths, axis=1)
    qz, qx, qc = questions // 8, (questions // 2) % 4, questions % 2
    place = ((qz - z) % 4) * 8 + ((qx - x) % 4) * 2 + qc
    meta = jnp.concatenate(
        [v.reshape(-1) for v in (place, ends - lengths, ends, questions)]
    ).astype(jnp.int32)
    spread_flops = 2 * 2 * ROWS * 128 * 128 * PAIRS
    stats = small_call(
        stats_kernel, meta, (keys, qg_all), jax.ShapeDtypeStruct((24, 128), F32), spread_flops
    )
    stats_x = jnp.stack(gather4(stats, "x"))
    stats_all = jnp.concatenate(gather4(stats_x, "z"), axis=0)

    values = project_all(a_value, av_up, av_down, av_far, b_value, bv_up, bv_down, bv_far)

    def assemble(a_own, a_up, a_down, a_far, b_own, b_up, b_down, b_far):
        return jnp.concatenate(
            [a_own, a_up, a_far[0][None], a_far[1][None], a_down]
            + [b_own, b_up, b_far[0][None], b_far[1][None], b_down],
            axis=0,
        ).reshape(2, 4, 4, CHUNK, CHUNK)

    wk = assemble(a_key, ak_up, ak_down, ak_far, b_key, bk_up, bk_down, bk_far)
    wk_got = perm(wk, "core", 1)
    wv = assemble(a_value, av_up, av_down, av_far, b_value, bv_up, bv_down, bv_far)
    wv_got = perm(wv, "core", 1)

    ml, delta, dense = small_call(
        forward_kernel,
        meta,
        (keys, values, qg_all, stats_all),
        [
            jax.ShapeDtypeStruct((16, 128), F32),
            jax.ShapeDtypeStruct((8, 128), F32),
            jax.ShapeDtypeStruct((32, DEC, HALF), F32),
        ],
        3 * spread_flops,
    )
    delta_x = jnp.stack(gather4(delta, "x"))
    delta_all = jnp.concatenate(gather4(delta_x, "z"), axis=0)
    own, send = small_call(
        backward_kernel,
        meta,
        (keys, values, qg_all, stats_all, ml, delta_all),
        [jax.ShapeDtypeStruct((2, ROWS, HALF), BF)] * 2,
        4 * spread_flops,
    )
    received = perm(send, "core", 1)

    def block(target, dtypes):
        zi = ((target - z) % 4).astype(jnp.int32).reshape(1)
        return grad_block(zi, own, received, wk, wk_got, wv, wv_got, dtypes)

    far_top, far_low = block(y + 2, [BF, BF])
    from_below = perm(far_top, "dec", 1)
    from_above = perm(far_low, "dec", -1)
    up_top, up_low = block(y + 1, [F32, BF])
    low_below = perm(up_low, "dec", 1)
    down_top, down_low = block(y + 3, [BF, F32])
    top_above = perm(down_top, "dec", -1)
    top_below = perm((up_top + from_below.astype(F32)).astype(BF), "dec", 1)
    low_above = perm((down_low + from_above.astype(F32)).astype(BF), "dec", -1)
    (base,) = block(y, [F32])
    enc_grad = finish(xs.astype(jnp.int32), base, (top_below, low_below, top_above, low_above))

    dense = dense.reshape(4, 4, 2, DEC, HALF)
    by_z = dense[0] + perm(dense[1], "z", 1) + perm(dense[2], "z", 2) + perm(dense[3], "z", 3)
    by_x = by_z[0] + perm(by_z[1], "x", 1) + perm(by_z[2], "x", 2) + perm(by_z[3], "x", 3)
    keep = lax.dynamic_index_in_dim(by_x, core, 0, keepdims=False)
    give = lax.dynamic_index_in_dim(by_x, 1 - core, 0, keepdims=False)
    come = perm(give, "core", 1)
    ctx = jnp.where(
        core == 0,
        jnp.concatenate([keep, come], axis=1),
        jnp.concatenate([come, keep], axis=1),
    )[None]
    return ctx, enc_grad


def solution(mesh):
    grid = Mesh(mesh.devices.reshape(NZ, NX, NC, NY), ("z", "x", "core", "dec"))
    return jax.shard_map(
        body,
        mesh=grid,
        in_specs=(
            P(ENC, None),
            P(ENC, "dec"),
            P(ENC, "dec"),
            P(ENC, None, "dec"),
            P(ENC, None, "dec"),
            P(ENC, None),
            P(ENC, None),
        ),
        out_specs=(P(ENC, None, "dec"), P(ENC, "dec")),
        check_vma=False,
    )
```

```python
import functools

import jax
import jax.numpy as jnp
from jax import lax
from jax.experimental import pallas as pl
from jax.experimental.pallas import tpu as pltpu
from jax.sharding import Mesh, PartitionSpec as P

BF = jnp.bfloat16
F32 = jnp.float32
NZ, NX, NC, NY = 4, 4, 2, 4
ENC = ("z", "x", "core")
ROWS = 512
D = 4096
HALF = 512
CHUNK = 256
PIECE = 576
DEC = 16
NPASS = 4
PAIRS = 4
LOW = -1e30
HIDDEN = pl.CostEstimate(flops=0, bytes_accessed=0, transcendentals=0)
NT = (((1,), (1,)), ((), ()))
TN = (((0,), (0,)), ((), ()))


def perm(v, axis, shift):
    n = {"z": NZ, "x": NX, "core": NC, "dec": NY}[axis]
    return lax.ppermute(v, axis, [(i, (i + shift) % n) for i in range(n)])


def gather4(v, axis):
    return [v] + [perm(v, axis, -o) for o in (1, 2, 3)]


def phase(*values):
    return lax.optimization_barrier(values)


def params(mib):
    return pltpu.CompilerParams(vmem_limit_bytes=mib * 1024 * 1024)


def first_kernel(*refs):
    outs = refs[10:]
    for side in range(2):
        own, up, top, low, down = refs[side * 5 : side * 5 + 5]
        mid = PIECE // 2
        outs[side][0, :PIECE] = own[...]
        outs[side][0, PIECE:] = up[...]
        outs[side][1, :mid] = top[...]
        outs[side][1, mid:PIECE] = low[...]
        outs[side][1, PIECE:] = down[...]


def first_blocks(pieces):
    return pl.pallas_call(
        first_kernel,
        out_shape=[jax.ShapeDtypeStruct((2, 2 * PIECE, CHUNK), BF)] * 2,
        compiler_params=params(16),
        cost_estimate=HIDDEN,
    )(*pieces)


def halves_kernel(a_ref, b_ref, c_ref, d_ref, *outs):
    for ref, out in zip((a_ref, b_ref, c_ref, d_ref), outs):
        out[...] = ref[0]


def take_halves(a_up, a_down, b_up, b_down):
    half = (1, 2 * PIECE, CHUNK)
    first = pl.BlockSpec(half, lambda i: (0, 0, 0))
    second = pl.BlockSpec(half, lambda i: (1, 0, 0))
    return pl.pallas_call(
        halves_kernel,
        grid=(1,),
        in_specs=[first, second, first, second],
        out_specs=[pl.BlockSpec(half[1:], lambda i: (0, 0))] * 4,
        out_shape=[jax.ShapeDtypeStruct(half[1:], BF)] * 4,
        compiler_params=params(16),
        cost_estimate=HIDDEN,
    )(a_up, a_down, b_up, b_down)


def near_kernel(pos, own_ref, oth_ref, *refs):
    blocks, (acc_ref, enc_ref, qa_ref, qb_ref) = refs[:6], refs[6:]
    z, x = pos[0], pos[1]
    step = pl.program_id(0)

    def columns(ref, side, outer, inners):
        parts = []
        for inner in inners:
            zo, xo = (outer, inner) if side == 0 else (inner, outer)
            chip = ((z + zo) & 3) * 4 + ((x + xo) & 3)
            parts.append(ref[:, pl.ds(pl.multiple_of(chip * CHUNK, CHUNK), CHUNK)])
        return jnp.concatenate(parts, axis=1)

    def run(ref):
        for side in range(2):
            totals = [None, None]
            for b, outer in enumerate((0, 1, 3)):
                for h in range(2):
                    lhs = columns(ref, side, outer, (h * 2, h * 2 + 1))
                    block = blocks[side * 3 + b].at[h]
                    for t in range(2):
                        rhs = jnp.concatenate(
                            [block[at + t * 256 : at + t * 256 + 256] for at in (0, PIECE)], axis=0
                        )
                        term = jnp.dot(lhs, rhs, preferred_element_type=F32)
                        totals[t] = term if totals[t] is None else totals[t] + term
            for t in range(2):
                at = t * HALF + side * CHUNK
                acc_ref[0, :, at : at + CHUNK] = totals[t]
            enc_ref[0, :, side * 1024 : (side + 1) * 1024] = columns(ref, side, 2, range(4))

    pl.when(step < 2)(lambda: run(own_ref))
    pl.when(step >= 2)(lambda: run(oth_ref))

    @pl.when(step == 0)
    def questions():
        for side, out in ((0, qa_ref), (1, qb_ref)):
            for b, outer in enumerate((0, 1, 3)):
                for inner in range(4):
                    row = (inner % 2) * PIECE + 512
                    at = (outer * 4 + inner) * 64
                    out[at : at + 64, :] = blocks[side * 3 + b][inner // 2, row : row + 64]
            out[512:768, :] = jnp.zeros((256, CHUNK), BF)


def project_near(pos, own, other, blocks):
    tile = ROWS // 2
    fixed = pl.BlockSpec((1024, CHUNK), lambda i, o: (0, 0))
    return pl.pallas_call(
        near_kernel,
        grid_spec=pltpu.PrefetchScalarGridSpec(
            num_scalar_prefetch=1,
            grid=(4,),
            in_specs=[
                pl.BlockSpec((tile, D), lambda i, o: (jnp.minimum(i, 1), 0)),
                pl.BlockSpec((tile, D), lambda i, o: (jnp.maximum(i - 2, 0), 0)),
            ]
            + [pl.BlockSpec(b.shape, lambda i, o: (0, 0, 0)) for b in blocks],
            out_specs=[
                pl.BlockSpec((1, tile, 2 * HALF), lambda i, o: (i // 2, i % 2, 0)),
                pl.BlockSpec((1, tile, 2048), lambda i, o: (i // 2, i % 2, 0)),
                fixed,
                fixed,
            ],
        ),
        out_shape=[
            jax.ShapeDtypeStruct((2, ROWS, 2 * HALF), F32),
            jax.ShapeDtypeStruct((2, ROWS, 2048), BF),
            jax.ShapeDtypeStruct((1024, CHUNK), BF),
            jax.ShapeDtypeStruct((1024, CHUNK), BF),
        ],
        compiler_params=params(26),
        cost_estimate=HIDDEN,
    )(pos, own, other, *blocks)


class Passages:
    def __init__(self, pos, own, other):
        self.z, self.x = pos[0], pos[1]
        self.numbers = (own, other)

    def question(self, side, p):
        return self.numbers[side][NPASS + p]

    def start(self, side, p):
        at = 0
        for k in range(p):
            at = at + self.numbers[side][k]
        return at

    def chip(self, side, p):
        q = self.question(side, p)
        return ((q >> 3) - self.z) & 3, ((q >> 1) - self.x) & 3, q & 1

    def row(self, half, side, p):
        zo, xo, core = self.chip(side, p)
        outer, inner = (zo, xo) if half == 0 else (xo, zo)
        return (outer * 4 + inner) * 64 + core * 16


def pair_matrix(meta, qg_refs, side, pair, which):
    low = lax.broadcasted_iota(jnp.int32, (DEC, 128), 1) < 64
    half, lane = pair // 2, pair % 2
    parts = []
    for p in range(NPASS):
        row = pl.multiple_of(meta.row(half, side, p) + which * 32, 16)
        tile = qg_refs[half][pl.ds(row, DEC), lane * 128 : (lane + 1) * 128]
        zero = jnp.zeros_like(tile)
        parts += [jnp.where(low, tile, zero), jnp.where(low, zero, tile)]
    return jnp.concatenate(parts, axis=0)


def lane_value(numbers):
    lane = lax.broadcasted_iota(jnp.int32, (1, 128), 1) // 32
    value = jnp.zeros((1, 128), jnp.int32)
    for p in range(NPASS):
        value = jnp.where(lane == p, numbers[p], value)
    return value


def inside_mask(meta, side):
    row = lax.broadcasted_iota(jnp.int32, (ROWS, 128), 0)
    starts = [meta.start(side, p) for p in range(NPASS + 1)]
    return (row >= lane_value(starts[:NPASS])) & (row < lane_value(starts[1:]))


def dot_nt(a, b):
    return lax.dot_general(a, b, NT, preferred_element_type=F32)


def forward_side(side, meta, k, v, qg, st_ref, num_ref):
    inside = inside_mask(meta, side)
    question = lane_value([meta.question(side, p) for p in range(NPASS)]).astype(F32)
    for pair in range(PAIRS):
        cols = slice(pair * 128, (pair + 1) * 128)
        scores = dot_nt(k[side, :, cols], pair_matrix(meta, qg, side, pair, 0))
        scores = jnp.where(inside, scores, LOW)
        top = jnp.max(scores, axis=0, keepdims=True)
        unnorm = jnp.exp(scores - top)
        unnorm_b = unnorm.astype(BF)
        values = v[side, :, cols]
        dprob = dot_nt(values, pair_matrix(meta, qg, side, pair, 1))
        at = side * PAIRS + pair
        st_ref[at : at + 1, :] = top
        st_ref[8 + at : 9 + at, :] = jnp.sum(unnorm, axis=0, keepdims=True)
        st_ref[16 + at : 17 + at, :] = jnp.sum(
            unnorm_b.astype(F32) * dprob, axis=0, keepdims=True
        )
        st_ref[24 + at : 25 + at, :] = question
        num_ref[side, pair] = lax.dot_general(values, unnorm_b, TN, preferred_element_type=F32)


def far_kernel(
    pos, own_numbers, other_numbers, enc_ref, acc_ref, a_top, a_low, b_top, b_low, qa_in, qb_in,
    k_ref, v_ref, qa_ref, qb_ref, st_ref, num_ref,
):
    meta = Passages(pos, own_numbers, other_numbers)
    step = pl.program_id(0)
    far = ((a_top, a_low), (b_top, b_low))

    @pl.when(step == 0)
    def questions():
        for side, source, out in ((0, qa_in, qa_ref), (1, qb_in, qb_ref)):
            out[...] = source[...]
            for inner in range(4):
                row = (inner % 2) * PIECE + 512
                at = (8 + inner) * 64
                out[at : at + 64, :] = far[side][inner // 2][row : row + 64, :]

    row0 = pl.multiple_of((step % 2) * (ROWS // 2), ROWS // 2)
    for side in range(2):
        lhs = enc_ref[0, :, side * 1024 : (side + 1) * 1024]
        for t, out in ((0, k_ref), (1, v_ref)):
            rhs = jnp.concatenate(
                [
                    far[side][inner // 2][(inner % 2) * PIECE + t * 256 : (inner % 2) * PIECE + t * 256 + 256]
                    for inner in range(4)
                ],
                axis=0,
            )
            at = t * HALF + side * CHUNK
            total = acc_ref[0, :, at : at + CHUNK] + jnp.dot(
                lhs, rhs, preferred_element_type=F32
            )
            out[step // 2, pl.ds(row0, ROWS // 2), side * CHUNK : (side + 1) * CHUNK] = total.astype(BF)
    for side in range(2):
        @pl.when(step == side * 2 + 1)
        def attend():
            forward_side(side, meta, k_ref, v_ref, (qa_ref, qb_ref), st_ref, num_ref)


def project_far(meta, enc_far, acc, blocks, qa, qb):
    tile = ROWS // 2

    def whole(shape):
        return pl.BlockSpec(shape, lambda i, *m: (0,) * len(shape))

    shapes = [
        jax.ShapeDtypeStruct((2, ROWS, HALF), BF),
        jax.ShapeDtypeStruct((2, ROWS, HALF), BF),
        jax.ShapeDtypeStruct((1024, CHUNK), BF),
        jax.ShapeDtypeStruct((1024, CHUNK), BF),
        jax.ShapeDtypeStruct((32, 128), F32),
        jax.ShapeDtypeStruct((2, PAIRS, 128, 128), F32),
    ]
    return pl.pallas_call(
        far_kernel,
        grid_spec=pltpu.PrefetchScalarGridSpec(
            num_scalar_prefetch=3,
            grid=(4,),
            in_specs=[
                pl.BlockSpec((1, tile, 2048), lambda i, *m: (i // 2, i % 2, 0)),
                pl.BlockSpec((1, tile, 2 * HALF), lambda i, *m: (i // 2, i % 2, 0)),
            ]
            + [whole(b.shape) for b in blocks]
            + [whole((1024, CHUNK))] * 2,
            out_specs=[whole(s.shape) for s in shapes],
        ),
        out_shape=shapes,
        compiler_params=params(24),
        cost_estimate=HIDDEN,
    )(*meta, enc_far, acc, *blocks, qa, qb)


def combine(st_ref):
    n = st_ref.shape[0]
    own_question = [st_ref[0, 24 + s * PAIRS : 25 + s * PAIRS, :] for s in range(2)]

    def turned(value, k):
        return pltpu.roll(value, 32 * k, 1) if k else value

    tops = [None, None]
    for d in range(n):
        for k in range(NPASS):
            q, m = turned(st_ref[d, 24:32], k), turned(st_ref[d, 0:8], k)
            for s in range(2):
                term = jnp.where(q == own_question[s], m, LOW)
                tops[s] = term if tops[s] is None else jnp.maximum(tops[s], term)
    tops = [jnp.maximum(t[0:PAIRS], t[PAIRS:]) for t in tops]
    both = [jnp.concatenate([t, t], axis=0) for t in tops]
    totals, deltas = [0.0, 0.0], [0.0, 0.0]
    for d in range(n):
        for k in range(NPASS):
            q, m = turned(st_ref[d, 24:32], k), turned(st_ref[d, 0:8], k)
            l, e = turned(st_ref[d, 8:16], k), turned(st_ref[d, 16:24], k)
            for s in range(2):
                hit = q == own_question[s]
                scale = jnp.where(hit, jnp.exp(jnp.where(hit, m - both[s], 0.0)), 0.0)
                totals[s] = totals[s] + scale * l
                deltas[s] = deltas[s] + scale * e
    inverse = [1.0 / (t[0:PAIRS] + t[PAIRS:]) for t in totals]
    deltas = [(t[0:PAIRS] + t[PAIRS:]) * i for t, i in zip(deltas, inverse)]
    return tops, inverse, deltas


def weight_copy(ref, row, w_ref, sems, side, n):
    return pltpu.make_async_copy(
        ref.at[pl.ds(row, 2 * CHUNK)], w_ref.at[side, n], sems.at[side, n]
    )


def wait_copies(sources, w_ref, sems):
    for side in range(2):
        for n in range(4):
            weight_copy(sources[2], 0, w_ref, sems, side, n).wait()


def start_copies(place, sources, w_ref, sems):
    a_own, a_up, a_top, a_low, a_down, b_own, b_up, b_top, b_low, b_down = sources

    def copy(ref, row, side, n):
        return weight_copy(ref, row, w_ref, sems, side, n)

    for outer in range(4):
        @pl.when(place == outer)
        def start_a():
            for n in range(4):
                half = {
                    0: a_own.at[n // 2],
                    1: a_up.at[n // 2],
                    2: (a_top, a_low)[n // 2],
                    3: a_down.at[n // 2],
                }[outer]
                copy(half, (n % 2) * PIECE, 0, n).start()

    upper = place // 2
    row = pl.multiple_of((place % 2) * PIECE, 64)
    for n, ref in ((0, b_own), (1, b_up), (3, b_down)):
        copy(ref.at[upper], row, 1, n).start()
    for h, ref in ((0, b_top), (1, b_low)):
        pl.when(upper == h)(copy(ref, row, 1, 2).start)


def weights_tile(w_ref):
    rows = [
        jnp.concatenate(
            [w_ref[side, n, t * CHUNK : (t + 1) * CHUNK] for t in range(2) for side in range(2)],
            axis=1,
        )
        for n in range(4)
    ]
    return jnp.concatenate(rows, axis=0)


WEIGHT_SPECS = [pl.BlockSpec(memory_space=pltpu.HBM)] * 10


def weight_scratch(count):
    return [
        pltpu.VMEM((count, 2, 4, 2 * CHUNK, CHUNK), BF),
        pltpu.SemaphoreType.DMA((count, 2, 4)),
    ]


def backward_kernel(
    pos, own_numbers, other_numbers, k_ref, v_ref, qa_ref, qb_ref, st_ref, num_ref, *refs
):
    sources, outs = refs[:10], refs[10:]
    kvg_ref, own_ref, oth_ref, c0_ref, c1_ref, c2_ref, c3_ref, ctx_ref, w_ref, sems = outs
    w_ref = w_ref.at[0]
    sems = sems.at[0]
    start_copies(pos[2], sources, w_ref, sems)
    meta = Passages(pos, own_numbers, other_numbers)
    qg = (qa_ref, qb_ref)
    tops, inverses, deltas = combine(st_ref)
    ctx_ref[...] = jnp.zeros_like(ctx_ref)
    low = lax.broadcasted_iota(jnp.int32, (DEC, 128), 1) < 64
    for side in (1, 0):
        inside = inside_mask(meta, side)
        for pair in range(PAIRS):
            cols = slice(pair * 128, (pair + 1) * 128)
            at = side * PAIRS + pair
            top, inverse = tops[side][pair : pair + 1], inverses[side][pair : pair + 1]
            queries = pair_matrix(meta, qg, side, pair, 0)
            grads = pair_matrix(meta, qg, side, pair, 1)
            scores = dot_nt(k_ref[side, :, cols], queries)
            unnorm = jnp.where(inside, jnp.exp(jnp.where(inside, scores - top, 0.0)), 0.0)
            probs = unnorm * inverse
            dprob = dot_nt(v_ref[side, :, cols], grads)
            ds = (probs * (dprob - deltas[side][pair : pair + 1])).astype(BF)
            for t, lanes, weight in ((0, queries, ds), (1, grads, probs.astype(BF))):
                turned = lax.dot_general(
                    lanes, weight, (((0,), (1,)), ((), ())), preferred_element_type=F32
                ).astype(BF)
                for n in range(2):
                    kvg_ref[
                        side * 2 + n, t * HALF + pair * 128 : t * HALF + (pair + 1) * 128, :
                    ] = turned[:, n * 256 : (n + 1) * 256]
            scale = jnp.exp(st_ref[0, at : at + 1, :] - top) * inverse
            context = (num_ref[side, pair] * scale).T
            for p in range(NPASS):
                zo, xo, core = meta.chip(side, p)
                ctx_ref[(zo * 4 + xo) * 2 + core, :, cols] += jnp.where(
                    low, context[p * 32 : p * 32 + 16], context[p * 32 + 16 : p * 32 + 32]
                )
        if side == 1:
            wait_copies(sources, w_ref, sems)
        out = (own_ref, oth_ref)[side]
        for n in range(2):
            out[n] = jnp.dot(
                weights_tile(w_ref), kvg_ref[side * 2 + n], preferred_element_type=F32
            ).astype(BF)
    for o, out in enumerate((c0_ref, c1_ref, c2_ref, c3_ref)):
        out[...] = ctx_ref[o * 8 : o * 8 + 8].astype(out.dtype)


def backward(meta, args, weights):
    def whole(shape):
        return pl.BlockSpec(shape, lambda i, *m: (0,) * len(shape))

    shapes = [
        jax.ShapeDtypeStruct((4, 2 * HALF, ROWS // 2), BF),
        jax.ShapeDtypeStruct((2, 1024, ROWS // 2), BF),
        jax.ShapeDtypeStruct((2, 1024, ROWS // 2), BF),
        jax.ShapeDtypeStruct((8, DEC, HALF), F32),
    ] + [jax.ShapeDtypeStruct((8, DEC, HALF), BF)] * 3
    return pl.pallas_call(
        backward_kernel,
        grid_spec=pltpu.PrefetchScalarGridSpec(
            num_scalar_prefetch=3,
            grid=(1,),
            in_specs=[whole(a.shape) for a in args]
            + WEIGHT_SPECS,
            out_specs=[whole(s.shape) for s in shapes],
            scratch_shapes=[pltpu.VMEM((32, DEC, HALF), F32)] + weight_scratch(1),
        ),
        out_shape=shapes,
        compiler_params=params(24),
        cost_estimate=HIDDEN,
    )(*meta, *args, *weights)


def grad_kernel(count, places, kvg_ref, *refs):
    sources, (own_ref, oth_ref, w_ref, sems) = refs[:10], refs[10:]
    step = pl.program_id(0)
    for k in range(count):
        @pl.when(step == 4 * k)
        def load():
            first = range(count) if k == 0 else ()
            for n in first:
                start_copies(places[n], sources, w_ref.at[n], sems.at[n])
            wait_copies(sources, w_ref.at[k], sems.at[k])

    total = jnp.dot(weights_tile(w_ref.at[step // 4]), kvg_ref[0], preferred_element_type=F32)

    @pl.when(step % 4 < 2)
    def other():
        oth_ref[0, 0] = total.astype(oth_ref.dtype)

    @pl.when(step % 4 >= 2)
    def own():
        own_ref[0, 0] = total.astype(own_ref.dtype)


def grad_blocks(places, kvg, weights, dtype):
    tile = ROWS // 2
    count = places.shape[0]
    return pl.pallas_call(
        functools.partial(grad_kernel, count),
        grid_spec=pltpu.PrefetchScalarGridSpec(
            num_scalar_prefetch=1,
            grid=(4 * count,),
            in_specs=[pl.BlockSpec((1, 2 * HALF, tile), lambda i, p: ((i + 2) % 4, 0, 0))]
            + WEIGHT_SPECS,
            out_specs=[
                pl.BlockSpec(
                    (1, 1, 1024, tile), lambda i, p: (i // 4, jnp.maximum(i % 4 - 2, 0), 0, 0)
                ),
                pl.BlockSpec((1, 1, 1024, tile), lambda i, p: (i // 4, jnp.minimum(i % 4, 1), 0, 0)),
            ],
            scratch_shapes=weight_scratch(count),
        ),
        out_shape=[
            jax.ShapeDtypeStruct((count, 2, 1024, tile), dtype),
            jax.ShapeDtypeStruct((count, 2, 1024, tile), BF),
        ],
        compiler_params=params(20),
        cost_estimate=HIDDEN,
    )(places, kvg, *weights)


def finish_kernel(place, base_ref, core_ref, up_top, up_low, down_top, down_low, out_ref):
    step = pl.program_id(0)
    total = base_ref[...] + core_ref[...].astype(F32)

    def write(up, down):
        whole = total + up[...].astype(F32) + down[...].astype(F32)
        for n in range(2):
            out_ref[n * 256 : (n + 1) * 256, :] = whole[n].T

    pl.when(step < 2)(lambda: write(up_top, down_top))
    pl.when(step >= 2)(lambda: write(up_low, down_low))


def finish(place, base, core_part, parts):
    shape = (2, CHUNK, ROWS // 2)
    block = pl.BlockSpec(shape, lambda n, p: (0, n, 0))
    top = pl.BlockSpec(shape, lambda n, p: (0, jnp.minimum(n, 1), 0))
    low = pl.BlockSpec(shape, lambda n, p: (0, jnp.maximum(n - 2, 0), 0))
    return pl.pallas_call(
        finish_kernel,
        grid_spec=pltpu.PrefetchScalarGridSpec(
            num_scalar_prefetch=1,
            grid=(4,),
            in_specs=[block, block, top, low, top, low],
            out_specs=pl.BlockSpec((ROWS, CHUNK), lambda n, p: (0, p[n])),
        ),
        out_shape=jax.ShapeDtypeStruct((ROWS, 4 * CHUNK), F32),
        compiler_params=params(16),
        cost_estimate=HIDDEN,
    )(place, base, core_part, *parts)


def body(enc_rows, key_weight, value_weight, queries, ctx_grad, passage_len, passage_question):
    z, x, core, y = (lax.axis_index(a) for a in ("z", "x", "core", "dec"))
    four = jnp.arange(4, dtype=jnp.int32)
    zs, xs = (z + four) % 4, (x + four) % 4
    places = ((y + four - z) % 4).astype(jnp.int32)
    near_places, base_place = places[1::2], places[0:1]
    pos = jnp.stack([z, x, places[2]]).astype(jnp.int32)

    cat = jnp.concatenate([key_weight, value_weight, queries[0], ctx_grad[0]], axis=0)
    mine = lax.dynamic_slice_in_dim(cat, core * HALF, HALF, 1)
    theirs = lax.dynamic_slice_in_dim(cat, (1 - core) * HALF, HALF, 1)
    got = perm(theirs, "core", 1)
    numbers = jnp.concatenate([passage_len[0], passage_question[:, 0]])
    other_numbers = perm(numbers, "core", 1)
    enc_other = perm(enc_rows, "core", 1)
    first = jnp.where(core == 0, mine, got)
    second = jnp.where(core == 0, got, mine)
    chip = jnp.concatenate(
        [v[a:b] for a, b in ((0, 128), (128, 256), (256, 272), (272, 288)) for v in (first, second)],
        axis=0,
    )
    a_chip, b_chip, enc_other, other_numbers, pos, near_places, base_place, xs = phase(
        chip[:, :CHUNK],
        chip[:, CHUNK:],
        enc_other,
        other_numbers,
        pos,
        near_places,
        base_place,
        xs.astype(jnp.int32),
    )

    ax_up, ax_down = perm(a_chip, "x", -1), perm(a_chip, "x", 1)
    bz_up, bz_down = perm(b_chip, "z", -1), perm(b_chip, "z", 1)
    ax_up, ax_down, bz_up, bz_down = phase(ax_up, ax_down, bz_up, bz_down)
    mid = PIECE // 2
    far = phase(
        perm(ax_up[:mid], "x", -1),
        perm(ax_down[mid:], "x", 1),
        perm(bz_up[:mid], "z", -1),
        perm(bz_down[mid:], "z", 1),
    )
    a_first = [a_chip, ax_up, far[0], far[1], ax_down]
    b_first = [b_chip, bz_up, far[2], far[3], bz_down]
    a_own, b_own = phase(*first_blocks(a_first + b_first))

    a_up, a_down = perm(a_own, "z", -1), perm(a_own, "z", 1)
    b_up, b_down = perm(b_own, "x", -1), perm(b_own, "x", 1)
    a_own, b_own, a_up, a_down, b_up, b_down = phase(a_own, b_own, a_up, a_down, b_up, b_down)
    give = phase(*take_halves(a_up, a_down, b_up, b_down))
    far = [perm(v, a, t) for v, a, t in zip(give, ("z", "z", "x", "x"), (-1, 1, -1, 1))]
    acc, enc_far, qa, qb = project_near(
        pos, enc_rows, enc_other, [a_own, a_up, a_down, b_own, b_up, b_down]
    )
    far, acc, enc_far, qa, qb = phase(far, acc, enc_far, qa, qb)
    meta = (pos, numbers, other_numbers)
    keys, values, qa, qb, stats, numer = project_far(meta, enc_far, acc, far, qa, qb)
    stats_x = jnp.stack(phase(*gather4(stats, "x")))
    stats_all = jnp.concatenate(gather4(stats_x, "z"), axis=0)
    weights = [a_own, a_up, far[0], far[1], a_down, b_own, b_up, far[2], far[3], b_down]
    kvg, far_own, far_other, *dense = backward(
        meta, (keys, values, qa, qb, stats_all, numer), weights
    )

    def add(*values):
        return sum(v.astype(F32) for v in values).astype(BF)

    kvg, far_other, dense = phase(kvg, far_other, dense)
    far_got = perm(far_other, "core", 1)
    by_z = [dense[0]] + [perm(dense[o], "z", o) for o in (1, 2, 3)]
    near_own, near_other = grad_blocks(near_places, kvg, weights, BF)
    far_got, by_z, kvg, near_own, near_other = phase(far_got, by_z, kvg, near_own, near_other)

    from_below = perm(add(far_own[:, :512], far_got[:, :512]), "dec", 1)
    from_above = perm(add(far_own[:, 512:], far_got[:, 512:]), "dec", -1)
    near_got = perm(near_other, "core", 1)
    base, base_other = grad_blocks(base_place, kvg, weights, F32)
    base, base_other = base[0], base_other[0]
    by_z = sum(v.astype(F32) for v in by_z).reshape(4, 2, DEC, HALF)
    from_below, from_above, near_got, base, base_other, by_z = phase(
        from_below, from_above, near_got, base, base_other, by_z
    )

    low_below = perm(add(near_own[0, :, 512:], near_got[0, :, 512:]), "dec", 1)
    top_above = perm(add(near_own[1, :, :512], near_got[1, :, :512]), "dec", -1)
    up_top = add(near_own[0, :, :512], near_got[0, :, :512], from_below)
    down_low = add(near_own[1, :, 512:], near_got[1, :, 512:], from_above)
    by_x = [by_z[0]] + [perm(by_z[o], "x", o) for o in (1, 2, 3)]
    base_got = perm(base_other, "core", 1)
    low_below, top_above, up_top, down_low, base_got, by_x = phase(
        low_below, top_above, up_top, down_low, base_got, by_x
    )

    top_below = perm(up_top, "dec", 1)
    low_above = perm(down_low, "dec", -1)
    by_x = sum(by_x)
    keep = lax.dynamic_index_in_dim(by_x, core, 0, keepdims=False)
    give = lax.dynamic_index_in_dim(by_x, 1 - core, 0, keepdims=False)
    come = perm(give, "core", 1)
    ctx = jnp.where(
        core == 0,
        jnp.concatenate([keep, come], axis=1),
        jnp.concatenate([come, keep], axis=1),
    )[None]
    enc_grad = finish(xs, base, base_got, (top_below, low_below, top_above, low_above))
    return ctx, enc_grad


def solution(mesh):
    grid = Mesh(mesh.devices.reshape(NZ, NX, NC, NY), ("z", "x", "core", "dec"))
    return jax.shard_map(
        body,
        mesh=grid,
        in_specs=(
            P(ENC, None),
            P(ENC, "dec"),
            P(ENC, "dec"),
            P(ENC, None, "dec"),
            P(ENC, None, "dec"),
            P(ENC, None),
            P(ENC, None),
        ),
        out_specs=(P(ENC, None, "dec"), P(ENC, "dec")),
        check_vma=False,
    )
```

```python
import functools

import jax
import jax.numpy as jnp
from jax import lax
from jax.experimental import pallas as pl
from jax.experimental.pallas import tpu as pltpu
from jax.sharding import Mesh, PartitionSpec as P

BF = jnp.bfloat16
F32 = jnp.float32
NZ, NX, NC, NY = 4, 4, 2, 4
ENC = ("z", "x", "core")
ROWS = 512
D = 4096
HALF = 512
CHUNK = 256
PIECE = 576
DEC = 16
NPASS = 4
PAIRS = 4
LOW = -1e30
HIDDEN = pl.CostEstimate(flops=200_000_000, bytes_accessed=0, transcendentals=0)
NT = (((1,), (1,)), ((), ()))
TN = (((0,), (0,)), ((), ()))


def perm(v, axis, shift):
    n = {"z": NZ, "x": NX, "core": NC, "dec": NY}[axis]
    return lax.ppermute(v, axis, [(i, (i + shift) % n) for i in range(n)])


def phase(*values):
    return lax.optimization_barrier(values)


def params(mib):
    return pltpu.CompilerParams(vmem_limit_bytes=mib * 1024 * 1024)


def pair_perm(v, axis, odd):
    turn = (lambda i: i + 1 - 2 * (i % 2)) if not odd else (lambda i: i - 1 + 2 * (i % 2))
    return lax.ppermute(v, axis, [(i, turn(i) % 4) for i in range(4)])


def join_kernel(*refs):
    outs = refs[8:]
    rows = PIECE // 2
    for k, out in enumerate(outs):
        out[:rows] = refs[2 * k][...]
        out[rows:] = refs[2 * k + 1][...]


def join(pairs):
    return pl.pallas_call(
        join_kernel,
        out_shape=[jax.ShapeDtypeStruct((PIECE, CHUNK), BF)] * 4,
        compiler_params=params(16),
        cost_estimate=HIDDEN,
    )(*[v for p in pairs for v in p])


def first_kernel(place, joined0, second0, joined1, second1, out):
    mid = PIECE // 2
    odd = place[0] % 2

    def slot(o, h, value):
        at = (o % 2) * PIECE + h * mid
        out[o // 2, at : at + mid, :] = value

    for h, joined, second in ((0, joined0, second0), (1, joined1, second1)):
        slot(0, h, joined[:mid])
        slot(2, h, second[mid:])
        for parity in range(2):
            @pl.when(odd == parity)
            def near():
                one = 1 if h == parity else 3
                slot(one, h, joined[mid:])
                slot(4 - one, h, second[:mid])


def first_block(place, pieces):
    def whole(p):
        return pl.BlockSpec(p.shape, lambda i, o: (0, 0))

    return pl.pallas_call(
        first_kernel,
        grid_spec=pltpu.PrefetchScalarGridSpec(
            num_scalar_prefetch=1,
            grid=(1,),
            in_specs=[whole(p) for p in pieces],
            out_specs=pl.BlockSpec((2, 2 * PIECE, CHUNK), lambda i, o: (0, 0, 0)),
        ),
        out_shape=jax.ShapeDtypeStruct((2, 2 * PIECE, CHUNK), BF),
        compiler_params=params(16),
        cost_estimate=HIDDEN,
    )(place, *pieces)


def halves_kernel(up_ref, down_ref, first_ref, second_ref):
    first_ref[...] = up_ref[0]
    second_ref[...] = down_ref[0]


def take_halves(up, down):
    half = (1, 2 * PIECE, CHUNK)
    return pl.pallas_call(
        halves_kernel,
        grid=(1,),
        in_specs=[pl.BlockSpec(half, lambda i: (0, 0, 0)), pl.BlockSpec(half, lambda i: (1, 0, 0))],
        out_specs=[pl.BlockSpec(half[1:], lambda i: (0, 0))] * 2,
        out_shape=[jax.ShapeDtypeStruct(half[1:], BF)] * 2,
        compiler_params=params(16),
        cost_estimate=HIDDEN,
    )(up, down)


def near_kernel(pos, own_ref, oth_ref, *refs):
    blocks, (acc_ref, enc_ref, qa_ref, qb_ref) = refs[:6], refs[6:]
    z, x = pos[0], pos[1]
    step = pl.program_id(0)

    def columns(ref, side, outer, inners):
        parts = []
        for inner in inners:
            zo, xo = (outer, inner) if side == 0 else (inner, outer)
            chip = ((z + zo) & 3) * 4 + ((x + xo) & 3)
            parts.append(ref[:, pl.ds(pl.multiple_of(chip * CHUNK, CHUNK), CHUNK)])
        return jnp.concatenate(parts, axis=1)

    def run(ref):
        for side in range(2):
            totals = [None, None]
            for b, outer in enumerate((0, 1, 3)):
                for h in range(2):
                    lhs = columns(ref, side, outer, (h * 2, h * 2 + 1))
                    block = blocks[side * 3 + b].at[h]
                    for t in range(2):
                        rhs = jnp.concatenate(
                            [block[at + t * 256 : at + t * 256 + 256] for at in (0, PIECE)], axis=0
                        )
                        term = jnp.dot(lhs, rhs, preferred_element_type=F32)
                        totals[t] = term if totals[t] is None else totals[t] + term
            for t in range(2):
                at = t * HALF + side * CHUNK
                acc_ref[0, :, at : at + CHUNK] = totals[t]
            enc_ref[0, :, side * 1024 : (side + 1) * 1024] = columns(ref, side, 2, range(4))

    pl.when(step < 2)(lambda: run(own_ref))
    pl.when(step >= 2)(lambda: run(oth_ref))

    @pl.when(step == 0)
    def questions():
        for side, out in ((0, qa_ref), (1, qb_ref)):
            for b, outer in enumerate((0, 1, 3)):
                for inner in range(4):
                    row = (inner % 2) * PIECE + 512
                    at = (outer * 4 + inner) * 64
                    out[at : at + 64, :] = blocks[side * 3 + b][inner // 2, row : row + 64]
            out[512:768, :] = jnp.zeros((256, CHUNK), BF)


def project_near(pos, own, other, blocks):
    tile = ROWS // 2
    fixed = pl.BlockSpec((1024, CHUNK), lambda i, o: (0, 0))
    return pl.pallas_call(
        near_kernel,
        grid_spec=pltpu.PrefetchScalarGridSpec(
            num_scalar_prefetch=1,
            grid=(4,),
            in_specs=[
                pl.BlockSpec((tile, D), lambda i, o: (jnp.minimum(i, 1), 0)),
                pl.BlockSpec((tile, D), lambda i, o: (jnp.maximum(i - 2, 0), 0)),
            ]
            + [pl.BlockSpec(b.shape, lambda i, o: (0, 0, 0)) for b in blocks],
            out_specs=[
                pl.BlockSpec((1, tile, 2 * HALF), lambda i, o: (i // 2, i % 2, 0)),
                pl.BlockSpec((1, tile, 2048), lambda i, o: (i // 2, i % 2, 0)),
                fixed,
                fixed,
            ],
        ),
        out_shape=[
            jax.ShapeDtypeStruct((2, ROWS, 2 * HALF), F32),
            jax.ShapeDtypeStruct((2, ROWS, 2048), BF),
            jax.ShapeDtypeStruct((1024, CHUNK), BF),
            jax.ShapeDtypeStruct((1024, CHUNK), BF),
        ],
        compiler_params=params(26),
        cost_estimate=HIDDEN,
    )(pos, own, other, *blocks)


class Passages:
    def __init__(self, pos, own, other):
        self.z, self.x = pos[0], pos[1]
        self.numbers = (own, other)

    def question(self, side, p):
        return self.numbers[side][NPASS + p]

    def start(self, side, p):
        at = 0
        for k in range(p):
            at = at + self.numbers[side][k]
        return at

    def chip(self, side, p):
        q = self.question(side, p)
        return ((q >> 3) - self.z) & 3, ((q >> 1) - self.x) & 3, q & 1

    def row(self, half, side, p):
        zo, xo, core = self.chip(side, p)
        outer, inner = (zo, xo) if half == 0 else (xo, zo)
        return (outer * 4 + inner) * 64 + core * 16


def pair_matrix(meta, qg_refs, side, pair, which):
    low = lax.broadcasted_iota(jnp.int32, (DEC, 128), 1) < 64
    half, lane = pair // 2, pair % 2
    parts = []
    for p in range(NPASS):
        row = pl.multiple_of(meta.row(half, side, p) + which * 32, 16)
        tile = qg_refs[half][pl.ds(row, DEC), lane * 128 : (lane + 1) * 128]
        zero = jnp.zeros_like(tile)
        parts += [jnp.where(low, tile, zero), jnp.where(low, zero, tile)]
    return jnp.concatenate(parts, axis=0)


def lane_value(numbers):
    lane = lax.broadcasted_iota(jnp.int32, (1, 128), 1) // 32
    value = jnp.zeros((1, 128), jnp.int32)
    for p in range(NPASS):
        value = jnp.where(lane == p, numbers[p], value)
    return value


def inside_mask(meta, side):
    row = lax.broadcasted_iota(jnp.int32, (ROWS, 128), 0)
    starts = [meta.start(side, p) for p in range(NPASS + 1)]
    return (row >= lane_value(starts[:NPASS])) & (row < lane_value(starts[1:]))


def dot_nt(a, b):
    return lax.dot_general(a, b, NT, preferred_element_type=F32)


def forward_side(side, meta, k, v, qg, st_ref, num_ref):
    n = st_ref.shape[0]

    def put(row, value):
        st_ref[:, row : row + 1, :] = jnp.broadcast_to(value[None], (n, 1, 128))

    inside = inside_mask(meta, side)
    question = lane_value([meta.question(side, p) for p in range(NPASS)]).astype(F32)
    for pair in range(PAIRS):
        cols = slice(pair * 128, (pair + 1) * 128)
        scores = dot_nt(k[side, :, cols], pair_matrix(meta, qg, side, pair, 0))
        scores = jnp.where(inside, scores, LOW)
        top = jnp.max(scores, axis=0, keepdims=True)
        unnorm = jnp.exp(scores - top)
        unnorm_b = unnorm.astype(BF)
        values = v[side, :, cols]
        dprob = dot_nt(values, pair_matrix(meta, qg, side, pair, 1))
        at = side * PAIRS + pair
        put(at, top)
        put(8 + at, jnp.sum(unnorm, axis=0, keepdims=True))
        put(16 + at, jnp.sum(unnorm_b.astype(F32) * dprob, axis=0, keepdims=True))
        put(24 + at, question)
        num_ref[side, pair] = lax.dot_general(values, unnorm_b, TN, preferred_element_type=F32)


def far_kernel(
    pos, own_numbers, other_numbers, enc_ref, acc_ref, a_top, a_low, b_top, b_low, qa_in, qb_in,
    k_ref, v_ref, qa_ref, qb_ref, st_ref, num_ref,
):
    meta = Passages(pos, own_numbers, other_numbers)
    step = pl.program_id(0)
    far = ((a_top, a_low), (b_top, b_low))

    @pl.when(step == 0)
    def questions():
        for side, source, out in ((0, qa_in, qa_ref), (1, qb_in, qb_ref)):
            out[...] = source[...]
            for inner in range(4):
                row = (inner % 2) * PIECE + 512
                at = (8 + inner) * 64
                out[at : at + 64, :] = far[side][inner // 2][row : row + 64, :]

    row0 = pl.multiple_of((step % 2) * (ROWS // 2), ROWS // 2)
    for side in range(2):
        lhs = enc_ref[0, :, side * 1024 : (side + 1) * 1024]
        for t, out in ((0, k_ref), (1, v_ref)):
            rhs = jnp.concatenate(
                [
                    far[side][inner // 2][(inner % 2) * PIECE + t * 256 : (inner % 2) * PIECE + t * 256 + 256]
                    for inner in range(4)
                ],
                axis=0,
            )
            at = t * HALF + side * CHUNK
            total = acc_ref[0, :, at : at + CHUNK] + jnp.dot(
                lhs, rhs, preferred_element_type=F32
            )
            out[step // 2, pl.ds(row0, ROWS // 2), side * CHUNK : (side + 1) * CHUNK] = total.astype(BF)
    for side in range(2):
        @pl.when(step == side * 2 + 1)
        def attend():
            forward_side(side, meta, k_ref, v_ref, (qa_ref, qb_ref), st_ref, num_ref)


def project_far(meta, enc_far, acc, blocks, qa, qb):
    tile = ROWS // 2

    def whole(shape):
        return pl.BlockSpec(shape, lambda i, *m: (0,) * len(shape))

    shapes = [
        jax.ShapeDtypeStruct((2, ROWS, HALF), BF),
        jax.ShapeDtypeStruct((2, ROWS, HALF), BF),
        jax.ShapeDtypeStruct((1024, CHUNK), BF),
        jax.ShapeDtypeStruct((1024, CHUNK), BF),
        jax.ShapeDtypeStruct((NZ * NX, 32, 128), F32),
        jax.ShapeDtypeStruct((2, PAIRS, 128, 128), F32),
    ]
    return pl.pallas_call(
        far_kernel,
        grid_spec=pltpu.PrefetchScalarGridSpec(
            num_scalar_prefetch=3,
            grid=(4,),
            in_specs=[
                pl.BlockSpec((1, tile, 2048), lambda i, *m: (i // 2, i % 2, 0)),
                pl.BlockSpec((1, tile, 2 * HALF), lambda i, *m: (i // 2, i % 2, 0)),
            ]
            + [whole(b.shape) for b in blocks]
            + [whole((1024, CHUNK))] * 2,
            out_specs=[whole(s.shape) for s in shapes],
        ),
        out_shape=shapes,
        compiler_params=params(24),
        cost_estimate=HIDDEN,
    )(*meta, enc_far, acc, *blocks, qa, qb)


def combine(meta, st_ref):
    n = st_ref.shape[0]
    own_question = [
        lane_value([meta.question(s, p) for p in range(NPASS)]).astype(F32) for s in range(2)
    ]

    def turned(value, k):
        return pltpu.roll(value, 32 * k, 1) if k else value

    tops = [None, None]
    for d in range(n):
        for k in range(NPASS):
            q, m = turned(st_ref[d, 24:32], k), turned(st_ref[d, 0:8], k)
            for s in range(2):
                term = jnp.where(q == own_question[s], m, LOW)
                tops[s] = term if tops[s] is None else jnp.maximum(tops[s], term)
    tops = [jnp.maximum(t[0:PAIRS], t[PAIRS:]) for t in tops]
    both = [jnp.concatenate([t, t], axis=0) for t in tops]
    totals, deltas = [0.0, 0.0], [0.0, 0.0]
    for d in range(n):
        for k in range(NPASS):
            q, m = turned(st_ref[d, 24:32], k), turned(st_ref[d, 0:8], k)
            l, e = turned(st_ref[d, 8:16], k), turned(st_ref[d, 16:24], k)
            for s in range(2):
                hit = q == own_question[s]
                scale = jnp.where(hit, jnp.exp(jnp.where(hit, m - both[s], 0.0)), 0.0)
                totals[s] = totals[s] + scale * l
                deltas[s] = deltas[s] + scale * e
    inverse = [1.0 / (t[0:PAIRS] + t[PAIRS:]) for t in totals]
    deltas = [(t[0:PAIRS] + t[PAIRS:]) * i for t, i in zip(deltas, inverse)]
    return tops, inverse, deltas


def weight_copy(ref, row, w_ref, sems, side, n):
    return pltpu.make_async_copy(
        ref.at[pl.ds(row, 2 * CHUNK)], w_ref.at[side, n], sems.at[side, n]
    )


def wait_copies(sources, w_ref, sems):
    for side in range(2):
        for n in range(4):
            weight_copy(sources[2], 0, w_ref, sems, side, n).wait()


def start_copies(place, sources, w_ref, sems):
    a_own, a_up, a_top, a_low, a_down, b_own, b_up, b_top, b_low, b_down = sources

    def copy(ref, row, side, n):
        return weight_copy(ref, row, w_ref, sems, side, n)

    for outer in range(4):
        @pl.when(place == outer)
        def start_a():
            for n in range(4):
                half = {
                    0: a_own.at[n // 2],
                    1: a_up.at[n // 2],
                    2: (a_top, a_low)[n // 2],
                    3: a_down.at[n // 2],
                }[outer]
                copy(half, (n % 2) * PIECE, 0, n).start()

    upper = place // 2
    row = pl.multiple_of((place % 2) * PIECE, 64)
    for n, ref in ((0, b_own), (1, b_up), (3, b_down)):
        copy(ref.at[upper], row, 1, n).start()
    for h, ref in ((0, b_top), (1, b_low)):
        pl.when(upper == h)(copy(ref, row, 1, 2).start)


def weights_tile(w_ref):
    rows = [
        jnp.concatenate(
            [w_ref[side, n, t * CHUNK : (t + 1) * CHUNK] for t in range(2) for side in range(2)],
            axis=1,
        )
        for n in range(4)
    ]
    return jnp.concatenate(rows, axis=0)


WEIGHT_SPECS = [pl.BlockSpec(memory_space=pltpu.HBM)] * 10


def weight_scratch(count):
    return [
        pltpu.VMEM((count, 2, 4, 2 * CHUNK, CHUNK), BF),
        pltpu.SemaphoreType.DMA((count, 2, 4)),
    ]


def backward_kernel(
    pos, own_numbers, other_numbers, k_ref, v_ref, qa_ref, qb_ref, st_ref, num_ref, *refs
):
    sources, outs = refs[:10], refs[10:]
    kvg_ref, own_ref, oth_ref, dense_ref, ctx_ref, w_ref, sems = outs
    w_ref = w_ref.at[0]
    sems = sems.at[0]
    start_copies(pos[2], sources, w_ref, sems)
    meta = Passages(pos, own_numbers, other_numbers)
    qg = (qa_ref, qb_ref)
    tops, inverses, deltas = combine(meta, st_ref)
    here = meta.z * 4 + meta.x
    ctx_ref[...] = jnp.zeros_like(ctx_ref)
    low = lax.broadcasted_iota(jnp.int32, (DEC, 128), 1) < 64
    for side in (1, 0):
        inside = inside_mask(meta, side)
        for pair in range(PAIRS):
            cols = slice(pair * 128, (pair + 1) * 128)
            at = side * PAIRS + pair
            top, inverse = tops[side][pair : pair + 1], inverses[side][pair : pair + 1]
            queries = pair_matrix(meta, qg, side, pair, 0)
            grads = pair_matrix(meta, qg, side, pair, 1)
            scores = dot_nt(k_ref[side, :, cols], queries)
            unnorm = jnp.where(inside, jnp.exp(jnp.where(inside, scores - top, 0.0)), 0.0)
            probs = unnorm * inverse
            dprob = dot_nt(v_ref[side, :, cols], grads)
            ds = (probs * (dprob - deltas[side][pair : pair + 1])).astype(BF)
            for t, lanes, weight in ((0, queries, ds), (1, grads, probs.astype(BF))):
                turned = lax.dot_general(
                    lanes, weight, (((0,), (1,)), ((), ())), preferred_element_type=F32
                ).astype(BF)
                for n in range(2):
                    kvg_ref[
                        side * 2 + n, t * HALF + pair * 128 : t * HALF + (pair + 1) * 128, :
                    ] = turned[:, n * 256 : (n + 1) * 256]
            scale = jnp.exp(st_ref[here, at : at + 1, :] - top) * inverse
            context = (num_ref[side, pair] * scale).T
            for p in range(NPASS):
                ctx_ref[meta.question(side, p), :, cols] += jnp.where(
                    low, context[p * 32 : p * 32 + 16], context[p * 32 + 16 : p * 32 + 32]
                )
        if side == 1:
            wait_copies(sources, w_ref, sems)
        out = (own_ref, oth_ref)[side]
        for n in range(2):
            out[n] = jnp.dot(
                weights_tile(w_ref), kvg_ref[side * 2 + n], preferred_element_type=F32
            ).astype(BF)
    dense_ref[...] = ctx_ref[...].astype(BF)


def backward(meta, args, weights):
    def whole(shape):
        return pl.BlockSpec(shape, lambda i, *m: (0,) * len(shape))

    shapes = [
        jax.ShapeDtypeStruct((4, 2 * HALF, ROWS // 2), BF),
        jax.ShapeDtypeStruct((2, 1024, ROWS // 2), BF),
        jax.ShapeDtypeStruct((2, 1024, ROWS // 2), BF),
        jax.ShapeDtypeStruct((32, DEC, HALF), BF),
    ]
    return pl.pallas_call(
        backward_kernel,
        grid_spec=pltpu.PrefetchScalarGridSpec(
            num_scalar_prefetch=3,
            grid=(1,),
            in_specs=[whole(a.shape) for a in args]
            + WEIGHT_SPECS,
            out_specs=[whole(s.shape) for s in shapes],
            scratch_shapes=[pltpu.VMEM((32, DEC, HALF), F32)] + weight_scratch(1),
        ),
        out_shape=shapes,
        compiler_params=params(24),
        cost_estimate=HIDDEN,
    )(*meta, *args, *weights)


def grad_kernel(count, places, kvg_ref, *refs):
    sources, (own_ref, oth_ref, w_ref, sems) = refs[:10], refs[10:]
    step = pl.program_id(0)
    for k in range(count):
        @pl.when(step == 4 * k)
        def load():
            first = range(count) if k == 0 else ()
            for n in first:
                start_copies(places[n], sources, w_ref.at[n], sems.at[n])
            wait_copies(sources, w_ref.at[k], sems.at[k])

    total = jnp.dot(weights_tile(w_ref.at[step // 4]), kvg_ref[0], preferred_element_type=F32)

    @pl.when(step % 4 < 2)
    def other():
        oth_ref[0, 0] = total.astype(oth_ref.dtype)

    @pl.when(step % 4 >= 2)
    def own():
        own_ref[0, 0] = total.astype(own_ref.dtype)


def grad_blocks(places, kvg, weights, dtype):
    tile = ROWS // 2
    count = places.shape[0]
    return pl.pallas_call(
        functools.partial(grad_kernel, count),
        grid_spec=pltpu.PrefetchScalarGridSpec(
            num_scalar_prefetch=1,
            grid=(4 * count,),
            in_specs=[pl.BlockSpec((1, 2 * HALF, tile), lambda i, p: ((i + 2) % 4, 0, 0))]
            + WEIGHT_SPECS,
            out_specs=[
                pl.BlockSpec(
                    (1, 1, 1024, tile), lambda i, p: (i // 4, jnp.maximum(i % 4 - 2, 0), 0, 0)
                ),
                pl.BlockSpec((1, 1, 1024, tile), lambda i, p: (i // 4, jnp.minimum(i % 4, 1), 0, 0)),
            ],
            scratch_shapes=weight_scratch(count),
        ),
        out_shape=[
            jax.ShapeDtypeStruct((count, 2, 1024, tile), dtype),
            jax.ShapeDtypeStruct((count, 2, 1024, tile), BF),
        ],
        compiler_params=params(20),
        cost_estimate=HIDDEN,
    )(places, kvg, *weights)


def sums_kernel(own_ref, got_ref, below_ref, above_ref, *outs):
    for out, k, h, more in zip(outs, (0, 1, 0, 1), (1, 0, 0, 1), (None, None, below_ref, above_ref)):
        rows = slice(h * 512, (h + 1) * 512)
        total = own_ref[k, :, rows].astype(F32) + got_ref[k, :, rows].astype(F32)
        if more is not None:
            total = total + more[...].astype(F32)
        out[...] = total.astype(BF)


def near_sums(own, got, below, above):
    return pl.pallas_call(
        sums_kernel,
        out_shape=[jax.ShapeDtypeStruct((2, 512, ROWS // 2), BF)] * 4,
        compiler_params=params(16),
        cost_estimate=HIDDEN,
    )(own, got, below, above)


def finish_kernel(place, base_ref, core_ref, up_top, up_low, down_top, down_low, out_ref):
    step = pl.program_id(0)
    total = base_ref[...] + core_ref[...].astype(F32)

    def write(up, down):
        whole = total + up[...].astype(F32) + down[...].astype(F32)
        for n in range(2):
            out_ref[n * 256 : (n + 1) * 256, :] = whole[n].T

    pl.when(step < 2)(lambda: write(up_top, down_top))
    pl.when(step >= 2)(lambda: write(up_low, down_low))


def finish(place, base, core_part, parts):
    shape = (2, CHUNK, ROWS // 2)
    block = pl.BlockSpec(shape, lambda n, p: (0, n, 0))
    top = pl.BlockSpec(shape, lambda n, p: (0, jnp.minimum(n, 1), 0))
    low = pl.BlockSpec(shape, lambda n, p: (0, jnp.maximum(n - 2, 0), 0))
    return pl.pallas_call(
        finish_kernel,
        grid_spec=pltpu.PrefetchScalarGridSpec(
            num_scalar_prefetch=1,
            grid=(4,),
            in_specs=[block, block, top, low, top, low],
            out_specs=pl.BlockSpec((ROWS, CHUNK), lambda n, p: (0, p[n])),
        ),
        out_shape=jax.ShapeDtypeStruct((ROWS, 4 * CHUNK), F32),
        compiler_params=params(16),
        cost_estimate=HIDDEN,
    )(place, base, core_part, *parts)


def body(enc_rows, key_weight, value_weight, queries, ctx_grad, passage_len, passage_question):
    z, x, core, y = (lax.axis_index(a) for a in ("z", "x", "core", "dec"))
    four = jnp.arange(4, dtype=jnp.int32)
    zs, xs = (z + four) % 4, (x + four) % 4
    places = ((y + four - z) % 4).astype(jnp.int32)
    near_places, base_place = places[1::2], places[0:1]
    pos = jnp.stack([z, x, places[2]]).astype(jnp.int32)

    cat = jnp.concatenate([key_weight, value_weight, queries[0], ctx_grad[0]], axis=0)
    mine = lax.dynamic_slice_in_dim(cat, core * HALF, HALF, 1)
    theirs = lax.dynamic_slice_in_dim(cat, (1 - core) * HALF, HALF, 1)
    got = perm(theirs, "core", 1)
    numbers = jnp.concatenate([passage_len[0], passage_question[:, 0]])
    other_numbers = perm(numbers, "core", 1)
    enc_after, got = phase(enc_rows, got)
    enc_other = perm(enc_after, "core", 1)
    first = jnp.where(core == 0, mine, got)
    second = jnp.where(core == 0, got, mine)
    chip = jnp.concatenate(
        [v[a:b] for a, b in ((0, 128), (128, 256), (256, 272), (272, 288)) for v in (first, second)],
        axis=0,
    )
    mid = PIECE // 2
    halves = phase(
        *[chip[h * mid : (h + 1) * mid, c : c + CHUNK] for c in (0, CHUNK) for h in (0, 1)]
    )

    steps = [(v, a, h) for v, (a, h) in zip(halves, (("x", 0), ("x", 1), ("z", 0), ("z", 1)))]
    met, pos, near_places, base_place, x_place, xs = phase(
        [pair_perm(v, a, h) for v, a, h in steps],
        pos,
        near_places,
        base_place,
        x.astype(jnp.int32).reshape(1),
        xs.astype(jnp.int32),
    )
    joined = phase(*join(list(zip(halves, met))))
    second = [pair_perm(v, a, 1 - h) for v, (_, a, h) in zip(joined, steps)]
    a_own = first_block(x_place, (joined[0], second[0], joined[1], second[1]))
    b_own = first_block(pos[0:1], (joined[2], second[2], joined[3], second[3]))
    enc_other, other_numbers, a_own, b_own = phase(enc_other, other_numbers, a_own, b_own)

    a_up, a_down = phase(perm(a_own, "z", -1), perm(a_own, "z", 1))
    b_up, b_down = phase(perm(b_own, "x", -1), perm(b_own, "x", 1))
    a_first, a_second = phase(*take_halves(a_up, a_down))
    b_first, b_second = phase(*take_halves(b_up, b_down))
    far = [
        perm(a_first, "z", -1),
        perm(a_second, "z", 1),
        perm(b_first, "x", -1),
        perm(b_second, "x", 1),
    ]
    acc, enc_far, qa, qb = project_near(
        pos, enc_rows, enc_other, [a_own, a_up, a_down, b_own, b_up, b_down]
    )
    far, acc, enc_far, qa, qb = phase(far, acc, enc_far, qa, qb)
    meta = (pos, numbers, other_numbers)
    keys, values, qa, qb, stats, numer = project_far(meta, enc_far, acc, far, qa, qb)
    stats_all = lax.all_to_all(stats, ("z", "x"), 0, 0, tiled=True)
    weights = [a_own, a_up, far[0], far[1], a_down, b_own, b_up, far[2], far[3], b_down]
    kvg, far_own, far_other, dense = backward(
        meta, (keys, values, qa, qb, stats_all, numer), weights
    )

    def add(*values):
        return sum(v.astype(F32) for v in values).astype(BF)

    far_got = perm(far_other, "core", 1)
    near_own, near_other = grad_blocks(near_places, kvg, weights, BF)
    far_got, near_own, near_other, kvg, dense = phase(far_got, near_own, near_other, kvg, dense)

    far_top = add(far_own[:, :512], far_got[:, :512])
    far_low = add(far_own[:, 512:], far_got[:, 512:])
    far_top, far_low, near_other, kvg, dense = phase(far_top, far_low, near_other, kvg, dense)
    from_below = perm(far_top, "dec", 1)
    from_above = perm(far_low, "dec", -1)
    near_got = perm(near_other, "core", 1)
    base, base_other = grad_blocks(base_place, kvg, weights, F32)
    from_below, from_above, near_got, base, base_other, dense = phase(
        from_below, from_above, near_got, base[0], base_other[0], dense
    )

    *sums, dense, base_other = phase(
        *near_sums(near_own, near_got, from_below, from_above), dense, base_other
    )
    low_below = perm(sums[0], "dec", 1)
    top_above = perm(sums[1], "dec", -1)
    top_below = perm(sums[2], "dec", 1)
    low_above = perm(sums[3], "dec", -1)
    base_got = perm(base_other, "core", 1)
    parts = lax.all_to_all(dense.reshape(NZ * NX, 2, DEC, HALF), ("z", "x"), 0, 0, tiled=True)
    low_below, top_above, top_below, low_above, base_got, parts = phase(
        low_below, top_above, top_below, low_above, base_got, parts
    )
    chip_ctx = jnp.sum(parts.astype(F32), axis=0)
    keep = lax.dynamic_index_in_dim(chip_ctx, core, 0, keepdims=False)
    give = lax.dynamic_index_in_dim(chip_ctx, 1 - core, 0, keepdims=False)
    come = perm(give, "core", 1)
    ctx = jnp.where(
        core == 0,
        jnp.concatenate([keep, come], axis=1),
        jnp.concatenate([come, keep], axis=1),
    )[None]
    enc_grad = finish(xs, base, base_got, (top_below, low_below, top_above, low_above))
    return ctx, enc_grad


def solution(mesh):
    grid = Mesh(mesh.devices.reshape(NZ, NX, NC, NY), ("z", "x", "core", "dec"))
    return jax.shard_map(
        body,
        mesh=grid,
        in_specs=(
            P(ENC, None),
            P(ENC, "dec"),
            P(ENC, "dec"),
            P(ENC, None, "dec"),
            P(ENC, None, "dec"),
            P(ENC, None),
            P(ENC, None),
        ),
        out_specs=(P(ENC, None, "dec"), P(ENC, "dec")),
        check_vma=False,
    )
```

```python
import jax
import jax.numpy as jnp
from jax import lax
from jax.experimental import pallas as pl
from jax.experimental.pallas import tpu as pltpu
from jax.sharding import Mesh, PartitionSpec as P

BF = jnp.bfloat16
F32 = jnp.float32
NZ, NX, NC, NY = 4, 4, 2, 4
ENC = ("z", "x", "core")
ROWS = 512
D = 4096
HALF = 512
CHUNK = 256
PIECE = 576
DEC = 16
NPASS = 4
PAIRS = 4
LOW = -1e30
HIDDEN = pl.CostEstimate(flops=200_000_000, bytes_accessed=0, transcendentals=0)
NT = (((1,), (1,)), ((), ()))
TN = (((0,), (0,)), ((), ()))


def perm(v, axis, shift):
    n = {"z": NZ, "x": NX, "core": NC, "dec": NY}[axis]
    return lax.ppermute(v, axis, [(i, (i + shift) % n) for i in range(n)])


def phase(*values):
    return lax.optimization_barrier(values)


def params(mib):
    return pltpu.CompilerParams(vmem_limit_bytes=mib * 1024 * 1024)


def pair_perm(v, axis, odd):
    turn = (lambda i: i + 1 - 2 * (i % 2)) if not odd else (lambda i: i - 1 + 2 * (i % 2))
    return lax.ppermute(v, axis, [(i, turn(i) % 4) for i in range(4)])


def join_kernel(*refs):
    outs = refs[8:]
    rows = PIECE // 2
    for k, out in enumerate(outs):
        out[:rows] = refs[2 * k][...]
        out[rows:] = refs[2 * k + 1][...]


def join(pairs):
    return pl.pallas_call(
        join_kernel,
        out_shape=[jax.ShapeDtypeStruct((PIECE, CHUNK), BF)] * 4,
        compiler_params=params(16),
        cost_estimate=HIDDEN,
    )(*[v for p in pairs for v in p])


def first_kernel(place, joined0, second0, joined1, second1, out):
    mid = PIECE // 2
    odd = place[0] % 2

    def slot(o, h, value):
        at = (o % 2) * PIECE + h * mid
        out[o // 2, at : at + mid, :] = value

    for h, joined, second in ((0, joined0, second0), (1, joined1, second1)):
        slot(0, h, joined[:mid])
        slot(2, h, second[mid:])
        for parity in range(2):
            @pl.when(odd == parity)
            def near():
                one = 1 if h == parity else 3
                slot(one, h, joined[mid:])
                slot(4 - one, h, second[:mid])


def first_block(place, pieces):
    def whole(p):
        return pl.BlockSpec(p.shape, lambda i, o: (0, 0))

    return pl.pallas_call(
        first_kernel,
        grid_spec=pltpu.PrefetchScalarGridSpec(
            num_scalar_prefetch=1,
            grid=(1,),
            in_specs=[whole(p) for p in pieces],
            out_specs=pl.BlockSpec((2, 2 * PIECE, CHUNK), lambda i, o: (0, 0, 0)),
        ),
        out_shape=jax.ShapeDtypeStruct((2, 2 * PIECE, CHUNK), BF),
        compiler_params=params(16),
        cost_estimate=HIDDEN,
    )(place, *pieces)


def halves_kernel(up_ref, down_ref, first_ref, second_ref):
    first_ref[...] = up_ref[0]
    second_ref[...] = down_ref[0]


def take_halves(up, down):
    half = (1, 2 * PIECE, CHUNK)
    return pl.pallas_call(
        halves_kernel,
        grid=(1,),
        in_specs=[pl.BlockSpec(half, lambda i: (0, 0, 0)), pl.BlockSpec(half, lambda i: (1, 0, 0))],
        out_specs=[pl.BlockSpec(half[1:], lambda i: (0, 0))] * 2,
        out_shape=[jax.ShapeDtypeStruct(half[1:], BF)] * 2,
        compiler_params=params(16),
        cost_estimate=HIDDEN,
    )(up, down)


def key_value(halves):
    rows = []
    for half in halves:
        for at in (0, PIECE):
            rows.append(
                jnp.concatenate(
                    [half[at : at + CHUNK, :], half[at + CHUNK : at + 2 * CHUNK, :]], axis=1
                )
            )
    return jnp.concatenate(rows, axis=0)


def near_kernel(pos, own_ref, oth_ref, *refs):
    blocks, (acc_ref, enc_ref, qa_ref, qb_ref) = refs[:6], refs[6:]
    z, x = pos[0], pos[1]
    step = pl.program_id(0)

    def columns(ref, side, outer, inners):
        parts = []
        for inner in inners:
            zo, xo = (outer, inner) if side == 0 else (inner, outer)
            chip = ((z + zo) & 3) * 4 + ((x + xo) & 3)
            parts.append(ref[:, pl.ds(pl.multiple_of(chip * CHUNK, CHUNK), CHUNK)])
        return jnp.concatenate(parts, axis=1)

    def run(ref):
        for side in range(2):
            total = None
            for b, outer in enumerate((0, 1, 3)):
                block = blocks[side * 3 + b]
                rhs = key_value([block.at[h] for h in range(2)])
                lhs = columns(ref, side, outer, range(4))
                term = jnp.dot(lhs, rhs, preferred_element_type=F32)
                total = term if total is None else total + term
            for t in range(2):
                at = t * HALF + side * CHUNK
                acc_ref[0, :, at : at + CHUNK] = total[:, t * CHUNK : (t + 1) * CHUNK]
            enc_ref[0, :, side * 1024 : (side + 1) * 1024] = columns(ref, side, 2, range(4))

    pl.when(step < 2)(lambda: run(own_ref))
    pl.when(step >= 2)(lambda: run(oth_ref))

    @pl.when(step == 0)
    def questions():
        for side, out in ((0, qa_ref), (1, qb_ref)):
            for b, outer in enumerate((0, 1, 3)):
                for inner in range(4):
                    row = (inner % 2) * PIECE + 512
                    at = (outer * 4 + inner) * 64
                    out[at : at + 64, :] = blocks[side * 3 + b][inner // 2, row : row + 64]
            out[512:768, :] = jnp.zeros((256, CHUNK), BF)


def project_near(pos, own, other, blocks):
    tile = ROWS // 2
    fixed = pl.BlockSpec((1024, CHUNK), lambda i, o: (0, 0))
    return pl.pallas_call(
        near_kernel,
        grid_spec=pltpu.PrefetchScalarGridSpec(
            num_scalar_prefetch=1,
            grid=(4,),
            in_specs=[
                pl.BlockSpec((tile, D), lambda i, o: (jnp.minimum(i, 1), 0)),
                pl.BlockSpec((tile, D), lambda i, o: (jnp.maximum(i - 2, 0), 0)),
            ]
            + [pl.BlockSpec(b.shape, lambda i, o: (0, 0, 0)) for b in blocks],
            out_specs=[
                pl.BlockSpec((1, tile, 2 * HALF), lambda i, o: (i // 2, i % 2, 0)),
                pl.BlockSpec((1, tile, 2048), lambda i, o: (i // 2, i % 2, 0)),
                fixed,
                fixed,
            ],
        ),
        out_shape=[
            jax.ShapeDtypeStruct((2, ROWS, 2 * HALF), F32),
            jax.ShapeDtypeStruct((2, ROWS, 2048), BF),
            jax.ShapeDtypeStruct((1024, CHUNK), BF),
            jax.ShapeDtypeStruct((1024, CHUNK), BF),
        ],
        compiler_params=params(26),
        cost_estimate=HIDDEN,
    )(pos, own, other, *blocks)


class Passages:
    def __init__(self, pos, own, other):
        self.z, self.x = pos[0], pos[1]
        self.numbers = (own, other)

    def question(self, side, p):
        return self.numbers[side][NPASS + p]

    def start(self, side, p):
        at = 0
        for k in range(p):
            at = at + self.numbers[side][k]
        return at

    def chip(self, side, p):
        q = self.question(side, p)
        return ((q >> 3) - self.z) & 3, ((q >> 1) - self.x) & 3, q & 1

    def row(self, half, side, p):
        zo, xo, core = self.chip(side, p)
        outer, inner = (zo, xo) if half == 0 else (xo, zo)
        return (outer * 4 + inner) * 64 + core * 16


def pair_matrix(meta, qg_refs, side, pair, which):
    low = lax.broadcasted_iota(jnp.int32, (DEC, 128), 1) < 64
    half, lane = pair // 2, pair % 2
    parts = []
    for p in range(NPASS):
        row = pl.multiple_of(meta.row(half, side, p) + which * 32, 16)
        tile = qg_refs[half][pl.ds(row, DEC), lane * 128 : (lane + 1) * 128]
        zero = jnp.zeros_like(tile)
        parts += [jnp.where(low, tile, zero), jnp.where(low, zero, tile)]
    return jnp.concatenate(parts, axis=0)


def lane_value(numbers):
    lane = lax.broadcasted_iota(jnp.int32, (1, 128), 1) // 32
    value = jnp.zeros((1, 128), jnp.int32)
    for p in range(NPASS):
        value = jnp.where(lane == p, numbers[p], value)
    return value


def inside_mask(meta, side):
    row = lax.broadcasted_iota(jnp.int32, (ROWS, 128), 0)
    starts = [meta.start(side, p) for p in range(NPASS + 1)]
    return (row >= lane_value(starts[:NPASS])) & (row < lane_value(starts[1:]))


def dot_nt(a, b):
    return lax.dot_general(a, b, NT, preferred_element_type=F32)


def forward_side(side, meta, k, v, qg, st_ref, num_ref):
    n = st_ref.shape[0]

    def put(row, value):
        st_ref[:, row : row + 1, :] = jnp.broadcast_to(value[None], (n, 1, 128))

    inside = inside_mask(meta, side)
    question = lane_value([meta.question(side, p) for p in range(NPASS)]).astype(F32)
    for pair in range(PAIRS):
        cols = slice(pair * 128, (pair + 1) * 128)
        scores = dot_nt(k[side, :, cols], pair_matrix(meta, qg, side, pair, 0))
        scores = jnp.where(inside, scores, LOW)
        top = jnp.max(scores, axis=0, keepdims=True)
        unnorm = jnp.exp(scores - top)
        unnorm_b = unnorm.astype(BF)
        values = v[side, :, cols]
        dprob = dot_nt(values, pair_matrix(meta, qg, side, pair, 1))
        at = side * PAIRS + pair
        put(at, top)
        put(8 + at, jnp.sum(unnorm, axis=0, keepdims=True))
        put(16 + at, jnp.sum(unnorm_b.astype(F32) * dprob, axis=0, keepdims=True))
        put(24 + at, question)
        num_ref[side, pair] = lax.dot_general(values, unnorm_b, TN, preferred_element_type=F32)


def far_kernel(
    pos, own_numbers, other_numbers, enc_ref, acc_ref, a_top, a_low, b_top, b_low, qa_in, qb_in,
    k_ref, v_ref, qa_ref, qb_ref, st_ref, num_ref,
):
    meta = Passages(pos, own_numbers, other_numbers)
    step = pl.program_id(0)
    far = ((a_top, a_low), (b_top, b_low))

    @pl.when(step == 0)
    def questions():
        for side, source, out in ((0, qa_in, qa_ref), (1, qb_in, qb_ref)):
            out[...] = source[...]
            for inner in range(4):
                row = (inner % 2) * PIECE + 512
                at = (8 + inner) * 64
                out[at : at + 64, :] = far[side][inner // 2][row : row + 64, :]

    for side in range(2):
        lhs = enc_ref[0, :, side * 1024 : (side + 1) * 1024]
        total = jnp.dot(lhs, key_value(far[side]), preferred_element_type=F32)
        for t, out in ((0, k_ref), (1, v_ref)):
            at = t * HALF + side * CHUNK
            part = total[:, t * CHUNK : (t + 1) * CHUNK] + acc_ref[0, :, at : at + CHUNK]
            out[step, :, side * CHUNK : (side + 1) * CHUNK] = part.astype(BF)
    for side in range(2):
        @pl.when(step == side)
        def attend():
            forward_side(side, meta, k_ref, v_ref, (qa_ref, qb_ref), st_ref, num_ref)


def project_far(meta, enc_far, acc, blocks, qa, qb):
    def whole(shape):
        return pl.BlockSpec(shape, lambda i, *m: (0,) * len(shape))

    shapes = [
        jax.ShapeDtypeStruct((2, ROWS, HALF), BF),
        jax.ShapeDtypeStruct((2, ROWS, HALF), BF),
        jax.ShapeDtypeStruct((1024, CHUNK), BF),
        jax.ShapeDtypeStruct((1024, CHUNK), BF),
        jax.ShapeDtypeStruct((NZ * NX, 32, 128), F32),
        jax.ShapeDtypeStruct((2, PAIRS, 128, 128), F32),
    ]
    return pl.pallas_call(
        far_kernel,
        grid_spec=pltpu.PrefetchScalarGridSpec(
            num_scalar_prefetch=3,
            grid=(2,),
            in_specs=[
                pl.BlockSpec((1, ROWS, 2048), lambda i, *m: (i, 0, 0)),
                pl.BlockSpec((1, ROWS, 2 * HALF), lambda i, *m: (i, 0, 0)),
            ]
            + [whole(b.shape) for b in blocks]
            + [whole((1024, CHUNK))] * 2,
            out_specs=[whole(s.shape) for s in shapes],
        ),
        out_shape=shapes,
        compiler_params=params(24),
        cost_estimate=HIDDEN,
    )(*meta, enc_far, acc, *blocks, qa, qb)


def combine(meta, st_ref):
    n = st_ref.shape[0]
    own_question = [
        lane_value([meta.question(s, p) for p in range(NPASS)]).astype(F32) for s in range(2)
    ]

    def turned(value, k):
        return pltpu.roll(value, 32 * k, 1) if k else value

    tops = [None, None]
    for d in range(n):
        for k in range(NPASS):
            q, m = turned(st_ref[d, 24:32], k), turned(st_ref[d, 0:8], k)
            for s in range(2):
                term = jnp.where(q == own_question[s], m, LOW)
                tops[s] = term if tops[s] is None else jnp.maximum(tops[s], term)
    tops = [jnp.maximum(t[0:PAIRS], t[PAIRS:]) for t in tops]
    both = [jnp.concatenate([t, t], axis=0) for t in tops]
    totals, deltas = [0.0, 0.0], [0.0, 0.0]
    for d in range(n):
        for k in range(NPASS):
            q, m = turned(st_ref[d, 24:32], k), turned(st_ref[d, 0:8], k)
            l, e = turned(st_ref[d, 8:16], k), turned(st_ref[d, 16:24], k)
            for s in range(2):
                hit = q == own_question[s]
                scale = jnp.where(hit, jnp.exp(jnp.where(hit, m - both[s], 0.0)), 0.0)
                totals[s] = totals[s] + scale * l
                deltas[s] = deltas[s] + scale * e
    inverse = [1.0 / (t[0:PAIRS] + t[PAIRS:]) for t in totals]
    deltas = [(t[0:PAIRS] + t[PAIRS:]) * i for t, i in zip(deltas, inverse)]
    return tops, inverse, deltas


def take_weights(place, sources, w_ref):
    a_own, a_up, a_top, a_low, a_down, b_own, b_up, b_top, b_low, b_down = sources
    both = 2 * CHUNK
    for outer in range(4):
        @pl.when(place == outer)
        def take_a():
            for n in range(4):
                rows = pl.ds((n % 2) * PIECE, both)
                if outer == 2:
                    w_ref[0, n] = (a_top, a_low)[n // 2][rows, :]
                else:
                    w_ref[0, n] = (a_own, a_up, None, a_down)[outer][n // 2, rows, :]

    upper = place // 2
    rows = pl.ds(pl.multiple_of((place % 2) * PIECE, 64), both)
    for n, ref in ((0, b_own), (1, b_up), (3, b_down)):
        w_ref[1, n] = ref[upper, rows, :]
    for h, ref in ((0, b_top), (1, b_low)):
        @pl.when(upper == h)
        def take_b():
            w_ref[1, 2] = ref[rows, :]


def weights_tile(w_ref):
    rows = [
        jnp.concatenate(
            [w_ref[side, n, t * CHUNK : (t + 1) * CHUNK] for t in range(2) for side in range(2)],
            axis=1,
        )
        for n in range(4)
    ]
    return jnp.concatenate(rows, axis=0)


def weight_specs():
    shape = (2, 2 * PIECE, CHUNK)
    block = pl.BlockSpec(shape, lambda i, *p: (0, 0, 0), pipeline_mode=pl.Buffered(1))
    half = pl.BlockSpec(shape[1:], lambda i, *p: (0, 0), pipeline_mode=pl.Buffered(1))
    return [block, block, half, half, block] * 2


WEIGHT_SCRATCH = pltpu.VMEM((2, 4, 2 * CHUNK, CHUNK), BF)


def backward_kernel(
    pos, own_numbers, other_numbers, k_ref, v_ref, qa_ref, qb_ref, st_ref, num_ref, *refs
):
    sources, outs = refs[:10], refs[10:]
    kvg_ref, own_ref, oth_ref, dense_ref, ctx_ref, w_ref = outs
    take_weights(pos[2], sources, w_ref)
    meta = Passages(pos, own_numbers, other_numbers)
    qg = (qa_ref, qb_ref)
    tops, inverses, deltas = combine(meta, st_ref)
    here = meta.z * 4 + meta.x
    ctx_ref[...] = jnp.zeros_like(ctx_ref)
    low = lax.broadcasted_iota(jnp.int32, (DEC, 128), 1) < 64
    for side in (1, 0):
        inside = inside_mask(meta, side)
        for pair in range(PAIRS):
            cols = slice(pair * 128, (pair + 1) * 128)
            at = side * PAIRS + pair
            top, inverse = tops[side][pair : pair + 1], inverses[side][pair : pair + 1]
            queries = pair_matrix(meta, qg, side, pair, 0)
            grads = pair_matrix(meta, qg, side, pair, 1)
            scores = dot_nt(k_ref[side, :, cols], queries)
            unnorm = jnp.where(inside, jnp.exp(jnp.where(inside, scores - top, 0.0)), 0.0)
            probs = unnorm * inverse
            dprob = dot_nt(v_ref[side, :, cols], grads)
            ds = (probs * (dprob - deltas[side][pair : pair + 1])).astype(BF)
            for t, lanes, weight in ((0, queries, ds), (1, grads, probs.astype(BF))):
                turned = lax.dot_general(
                    lanes, weight, (((0,), (1,)), ((), ())), preferred_element_type=F32
                ).astype(BF)
                first = t * HALF + pair * 128
                kvg_ref[first : first + 128, side * ROWS : (side + 1) * ROWS] = turned
            scale = jnp.exp(st_ref[here, at : at + 1, :] - top) * inverse
            context = (num_ref[side, pair] * scale).T
            for p in range(NPASS):
                ctx_ref[meta.question(side, p), :, cols] += jnp.where(
                    low, context[p * 32 : p * 32 + 16], context[p * 32 + 16 : p * 32 + 32]
                )
    total = jnp.dot(weights_tile(w_ref), kvg_ref[...], preferred_element_type=F32)
    own_ref[...] = total[:, :ROWS].astype(BF)
    oth_ref[...] = total[:, ROWS:].astype(BF)
    dense_ref[...] = ctx_ref[...].astype(BF)


def backward(meta, args, weights):
    def whole(shape):
        return pl.BlockSpec(shape, lambda i, *m: (0,) * len(shape))

    shapes = [
        jax.ShapeDtypeStruct((2 * HALF, 2 * ROWS), BF),
        jax.ShapeDtypeStruct((1024, ROWS), BF),
        jax.ShapeDtypeStruct((1024, ROWS), BF),
        jax.ShapeDtypeStruct((32, DEC, HALF), BF),
    ]
    return pl.pallas_call(
        backward_kernel,
        grid_spec=pltpu.PrefetchScalarGridSpec(
            num_scalar_prefetch=3,
            grid=(1,),
            in_specs=[whole(a.shape) for a in args]
            + weight_specs(),
            out_specs=[whole(s.shape) for s in shapes],
            scratch_shapes=[pltpu.VMEM((32, DEC, HALF), F32), WEIGHT_SCRATCH],
        ),
        out_shape=shapes,
        compiler_params=params(34),
        cost_estimate=HIDDEN,
    )(*meta, *args, *weights)


def grad_kernel(places, kvg_ref, *refs):
    sources, (own_ref, oth_ref, w_ref) = refs[:10], refs[10:]
    take_weights(places[pl.program_id(0)], sources, w_ref)
    total = jnp.dot(weights_tile(w_ref), kvg_ref[...], preferred_element_type=F32)
    own_ref[0] = total[:, :ROWS].astype(own_ref.dtype)
    oth_ref[0] = total[:, ROWS:].astype(oth_ref.dtype)


def grad_blocks(places, kvg, weights, dtype):
    count = places.shape[0]
    out = pl.BlockSpec((1, 1024, ROWS), lambda i, p: (i, 0, 0))
    return pl.pallas_call(
        grad_kernel,
        grid_spec=pltpu.PrefetchScalarGridSpec(
            num_scalar_prefetch=1,
            grid=(count,),
            in_specs=[pl.BlockSpec(kvg.shape, lambda i, p: (0, 0))] + weight_specs(),
            out_specs=[out, out],
            scratch_shapes=[WEIGHT_SCRATCH],
        ),
        out_shape=[
            jax.ShapeDtypeStruct((count, 1024, ROWS), dtype),
            jax.ShapeDtypeStruct((count, 1024, ROWS), BF),
        ],
        compiler_params=params(34),
        cost_estimate=HIDDEN,
    )(places, kvg, *weights)


def sums_kernel(own_ref, got_ref, below_ref, above_ref, *outs):
    for out, k, h, more in zip(outs, (0, 1, 0, 1), (1, 0, 0, 1), (None, None, below_ref, above_ref)):
        rows = slice(h * 512, (h + 1) * 512)
        total = own_ref[k, rows].astype(F32) + got_ref[k, rows].astype(F32)
        if more is not None:
            total = total + more[...].astype(F32)
        out[...] = total.astype(BF)


def near_sums(own, got, below, above):
    return pl.pallas_call(
        sums_kernel,
        out_shape=[jax.ShapeDtypeStruct((512, ROWS), BF)] * 4,
        compiler_params=params(16),
        cost_estimate=HIDDEN,
    )(own, got, below, above)


def finish_kernel(
    place, base_ref, core_ref, up_top, up_low, down_top, down_low, parts_ref, out_ref, ctx_ref
):
    step = pl.program_id(0)

    @pl.when(step == 0)
    def context():
        for core in range(2):
            total = parts_ref[0, core].astype(F32)
            for n in range(1, NZ * NX):
                total = total + parts_ref[n, core].astype(F32)
            ctx_ref[0, :, core * HALF : (core + 1) * HALF] = total

    total = base_ref[...] + core_ref[...].astype(F32)

    def write(up, down):
        whole = total + up[...].astype(F32) + down[...].astype(F32)
        out_ref[...] = whole.T

    pl.when(step < 2)(lambda: write(up_top, down_top))
    pl.when(step >= 2)(lambda: write(up_low, down_low))


def finish(place, base, core_part, parts, ctx_parts):
    shape = (CHUNK, ROWS)
    block = pl.BlockSpec(shape, lambda n, p: (n, 0))
    top = pl.BlockSpec(shape, lambda n, p: (jnp.minimum(n, 1), 0))
    low = pl.BlockSpec(shape, lambda n, p: (jnp.maximum(n - 2, 0), 0))
    return pl.pallas_call(
        finish_kernel,
        grid_spec=pltpu.PrefetchScalarGridSpec(
            num_scalar_prefetch=1,
            grid=(4,),
            in_specs=[block, block, top, low, top, low]
            + [pl.BlockSpec(ctx_parts.shape, lambda n, p: (0, 0, 0, 0))],
            out_specs=[
                pl.BlockSpec((ROWS, CHUNK), lambda n, p: (0, p[n])),
                pl.BlockSpec((1, DEC, 2 * HALF), lambda n, p: (0, 0, 0)),
            ],
        ),
        out_shape=[
            jax.ShapeDtypeStruct((ROWS, 4 * CHUNK), F32),
            jax.ShapeDtypeStruct((1, DEC, 2 * HALF), F32),
        ],
        compiler_params=params(16),
        cost_estimate=HIDDEN,
    )(place, base, core_part, *parts, ctx_parts)


def body(enc_rows, key_weight, value_weight, queries, ctx_grad, passage_len, passage_question):
    z, x, core, y = (lax.axis_index(a) for a in ("z", "x", "core", "dec"))
    four = jnp.arange(4, dtype=jnp.int32)
    zs, xs = (z + four) % 4, (x + four) % 4
    places = ((y + four - z) % 4).astype(jnp.int32)
    near_places, base_place = places[1::2], places[0:1]
    pos = jnp.stack([z, x, places[2]]).astype(jnp.int32)

    cat = jnp.concatenate([key_weight, value_weight, queries[0], ctx_grad[0]], axis=0)
    mine = lax.dynamic_slice_in_dim(cat, core * HALF, HALF, 1)
    theirs = lax.dynamic_slice_in_dim(cat, (1 - core) * HALF, HALF, 1)
    got = perm(theirs, "core", 1)
    numbers = jnp.concatenate([passage_len[0], passage_question[:, 0]])
    other_numbers = perm(numbers, "core", 1)
    enc_after, got = phase(enc_rows, got)
    enc_other = perm(enc_after, "core", 1)
    first = jnp.where(core == 0, mine, got)
    second = jnp.where(core == 0, got, mine)
    chip = jnp.concatenate(
        [v[a:b] for a, b in ((0, 128), (128, 256), (256, 272), (272, 288)) for v in (first, second)],
        axis=0,
    )
    mid = PIECE // 2
    halves = phase(
        *[chip[h * mid : (h + 1) * mid, c : c + CHUNK] for c in (0, CHUNK) for h in (0, 1)]
    )

    steps = [(v, a, h) for v, (a, h) in zip(halves, (("x", 0), ("x", 1), ("z", 0), ("z", 1)))]
    met, pos, near_places, base_place, x_place, xs = phase(
        [pair_perm(v, a, h) for v, a, h in steps],
        pos,
        near_places,
        base_place,
        x.astype(jnp.int32).reshape(1),
        xs.astype(jnp.int32),
    )
    joined = phase(*join(list(zip(halves, met))))
    second = [pair_perm(v, a, 1 - h) for v, (_, a, h) in zip(joined, steps)]
    a_own = first_block(x_place, (joined[0], second[0], joined[1], second[1]))
    b_own = first_block(pos[0:1], (joined[2], second[2], joined[3], second[3]))
    enc_other, other_numbers, a_own, b_own = phase(enc_other, other_numbers, a_own, b_own)

    a_up, a_down = phase(perm(a_own, "z", -1), perm(a_own, "z", 1))
    b_up, b_down = phase(perm(b_own, "x", -1), perm(b_own, "x", 1))
    a_first, a_second = phase(*take_halves(a_up, a_down))
    b_first, b_second = phase(*take_halves(b_up, b_down))
    far = [
        perm(a_first, "z", -1),
        perm(a_second, "z", 1),
        perm(b_first, "x", -1),
        perm(b_second, "x", 1),
    ]
    acc, enc_far, qa, qb = project_near(
        pos, enc_rows, enc_other, [a_own, a_up, a_down, b_own, b_up, b_down]
    )
    far, acc, enc_far, qa, qb = phase(far, acc, enc_far, qa, qb)
    meta = (pos, numbers, other_numbers)
    keys, values, qa, qb, stats, numer = project_far(meta, enc_far, acc, far, qa, qb)
    stats_all = lax.all_to_all(stats, ("z", "x"), 0, 0, tiled=True)
    weights = [a_own, a_up, far[0], far[1], a_down, b_own, b_up, far[2], far[3], b_down]
    kvg, far_own, far_other, dense = backward(
        meta, (keys, values, qa, qb, stats_all, numer), weights
    )

    def add(*values):
        return sum(v.astype(F32) for v in values).astype(BF)

    far_got = perm(far_other, "core", 1)
    near_own, near_other = grad_blocks(near_places, kvg, weights, BF)
    far_got, near_own, near_other, kvg, dense = phase(far_got, near_own, near_other, kvg, dense)

    far_top, far_low = add(far_own[:512], far_got[:512]), add(far_own[512:], far_got[512:])
    far_top, far_low, near_other, kvg, dense = phase(far_top, far_low, near_other, kvg, dense)
    from_below = perm(far_top, "dec", 1)
    from_above = perm(far_low, "dec", -1)
    near_got = perm(near_other, "core", 1)
    base, base_other = grad_blocks(base_place, kvg, weights, F32)
    from_below, from_above, near_got, base, base_other, dense = phase(
        from_below, from_above, near_got, base[0], base_other[0], dense
    )

    *sums, dense, base_other = phase(
        *near_sums(near_own, near_got, from_below, from_above), dense, base_other
    )
    low_below = perm(sums[0], "dec", 1)
    top_above = perm(sums[1], "dec", -1)
    top_below = perm(sums[2], "dec", 1)
    low_above = perm(sums[3], "dec", -1)
    base_got = perm(base_other, "core", 1)
    parts = lax.all_to_all(dense, ENC, 0, 0, tiled=True).reshape(NZ * NX, NC, DEC, HALF)
    low_below, top_above, top_below, low_above, base_got, parts = phase(
        low_below, top_above, top_below, low_above, base_got, parts
    )
    enc_grad, ctx = finish(
        xs, base, base_got, (top_below, low_below, top_above, low_above), parts
    )
    return ctx, enc_grad


def solution(mesh):
    grid = Mesh(mesh.devices.reshape(NZ, NX, NC, NY), ("z", "x", "core", "dec"))
    return jax.shard_map(
        body,
        mesh=grid,
        in_specs=(
            P(ENC, None),
            P(ENC, "dec"),
            P(ENC, "dec"),
            P(ENC, None, "dec"),
            P(ENC, None, "dec"),
            P(ENC, None),
            P(ENC, None),
        ),
        out_specs=(P(ENC, None, "dec"), P(ENC, "dec")),
        check_vma=False,
    )
```

```python
import jax
import jax.numpy as jnp
from jax import lax
from jax.experimental import pallas as pl
from jax.experimental.pallas import tpu as pltpu
from jax.sharding import Mesh, PartitionSpec as P

BF = jnp.bfloat16
F32 = jnp.float32
NZ, NX, NC, NY = 4, 4, 2, 4
ENC = ("z", "x", "core")
ROWS = 512
D = 4096
HALF = 512
CHUNK = 256
PIECE = 576
DEC = 16
NPASS = 4
QUADS = 2
LANES = 256
LOW = -1e30
HIDDEN = pl.CostEstimate(flops=200_000_000, bytes_accessed=0, transcendentals=0)
NT = (((1,), (1,)), ((), ()))
TN = (((0,), (0,)), ((), ()))


def perm(v, axis, shift):
    n = {"z": NZ, "x": NX, "core": NC, "dec": NY}[axis]
    return lax.ppermute(v, axis, [(i, (i + shift) % n) for i in range(n)])


def phase(*values):
    return lax.optimization_barrier(values)


def params(mib):
    return pltpu.CompilerParams(vmem_limit_bytes=mib * 1024 * 1024)


def pair_perm(v, axis, odd):
    turn = (lambda i: i + 1 - 2 * (i % 2)) if not odd else (lambda i: i - 1 + 2 * (i % 2))
    return lax.ppermute(v, axis, [(i, turn(i) % 4) for i in range(4)])


def join_kernel(*refs):
    outs = refs[8:]
    rows = PIECE // 2
    for k, out in enumerate(outs):
        out[:rows] = refs[2 * k][...]
        out[rows:] = refs[2 * k + 1][...]


def join(pairs):
    return pl.pallas_call(
        join_kernel,
        out_shape=[jax.ShapeDtypeStruct((PIECE, CHUNK), BF)] * 4,
        compiler_params=params(16),
        cost_estimate=HIDDEN,
    )(*[v for p in pairs for v in p])


def first_kernel(place, joined0, second0, joined1, second1, out):
    mid = PIECE // 2
    odd = place[0] % 2

    def slot(o, h, value):
        at = (o % 2) * PIECE + h * mid
        out[o // 2, at : at + mid, :] = value

    for h, joined, second in ((0, joined0, second0), (1, joined1, second1)):
        slot(0, h, joined[:mid])
        slot(2, h, second[mid:])
        for parity in range(2):
            @pl.when(odd == parity)
            def near():
                one = 1 if h == parity else 3
                slot(one, h, joined[mid:])
                slot(4 - one, h, second[:mid])


def first_block(place, pieces):
    def whole(p):
        return pl.BlockSpec(p.shape, lambda i, o: (0, 0))

    return pl.pallas_call(
        first_kernel,
        grid_spec=pltpu.PrefetchScalarGridSpec(
            num_scalar_prefetch=1,
            grid=(1,),
            in_specs=[whole(p) for p in pieces],
            out_specs=pl.BlockSpec((2, 2 * PIECE, CHUNK), lambda i, o: (0, 0, 0)),
        ),
        out_shape=jax.ShapeDtypeStruct((2, 2 * PIECE, CHUNK), BF),
        compiler_params=params(16),
        cost_estimate=HIDDEN,
    )(place, *pieces)


def halves_kernel(up_ref, down_ref, first_ref, second_ref):
    first_ref[...] = up_ref[0]
    second_ref[...] = down_ref[0]


def take_halves(up, down):
    half = (1, 2 * PIECE, CHUNK)
    return pl.pallas_call(
        halves_kernel,
        grid=(1,),
        in_specs=[pl.BlockSpec(half, lambda i: (0, 0, 0)), pl.BlockSpec(half, lambda i: (1, 0, 0))],
        out_specs=[pl.BlockSpec(half[1:], lambda i: (0, 0))] * 2,
        out_shape=[jax.ShapeDtypeStruct(half[1:], BF)] * 2,
        compiler_params=params(16),
        cost_estimate=HIDDEN,
    )(up, down)


def key_value(halves):
    rows = []
    for half in halves:
        for at in (0, PIECE):
            rows.append(
                jnp.concatenate(
                    [half[at : at + CHUNK, :], half[at + CHUNK : at + 2 * CHUNK, :]], axis=1
                )
            )
    return jnp.concatenate(rows, axis=0)


def near_kernel(pos, own_ref, oth_ref, *refs):
    blocks, (acc_ref, enc_ref, qa_ref, qb_ref) = refs[:6], refs[6:]
    z, x = pos[0], pos[1]
    step = pl.program_id(0)

    def columns(ref, side, outer, inners):
        parts = []
        for inner in inners:
            zo, xo = (outer, inner) if side == 0 else (inner, outer)
            chip = ((z + zo) & 3) * 4 + ((x + xo) & 3)
            parts.append(ref[:, pl.ds(pl.multiple_of(chip * CHUNK, CHUNK), CHUNK)])
        return jnp.concatenate(parts, axis=1)

    def run(ref):
        for side in range(2):
            total = None
            for b, outer in enumerate((0, 1, 3)):
                block = blocks[side * 3 + b]
                rhs = key_value([block.at[h] for h in range(2)])
                lhs = columns(ref, side, outer, range(4))
                term = jnp.dot(lhs, rhs, preferred_element_type=F32)
                total = term if total is None else total + term
            for t in range(2):
                at = t * HALF + side * CHUNK
                acc_ref[0, :, at : at + CHUNK] = total[:, t * CHUNK : (t + 1) * CHUNK]
            enc_ref[0, :, side * 1024 : (side + 1) * 1024] = columns(ref, side, 2, range(4))

    pl.when(step < 2)(lambda: run(own_ref))
    pl.when(step >= 2)(lambda: run(oth_ref))

    @pl.when(step == 0)
    def questions():
        for side, out in ((0, qa_ref), (1, qb_ref)):
            for b, outer in enumerate((0, 1, 3)):
                for inner in range(4):
                    row = (inner % 2) * PIECE + 512
                    at = (outer * 4 + inner) * 64
                    out[at : at + 64, :] = blocks[side * 3 + b][inner // 2, row : row + 64]
            out[512:768, :] = jnp.zeros((256, CHUNK), BF)


def project_near(pos, own, other, blocks):
    tile = ROWS // 2
    fixed = pl.BlockSpec((1024, CHUNK), lambda i, o: (0, 0))
    return pl.pallas_call(
        near_kernel,
        grid_spec=pltpu.PrefetchScalarGridSpec(
            num_scalar_prefetch=1,
            grid=(4,),
            in_specs=[
                pl.BlockSpec((tile, D), lambda i, o: (jnp.minimum(i, 1), 0)),
                pl.BlockSpec((tile, D), lambda i, o: (jnp.maximum(i - 2, 0), 0)),
            ]
            + [pl.BlockSpec(b.shape, lambda i, o: (0, 0, 0)) for b in blocks],
            out_specs=[
                pl.BlockSpec((1, tile, 2 * HALF), lambda i, o: (i // 2, i % 2, 0)),
                pl.BlockSpec((1, tile, 2048), lambda i, o: (i // 2, i % 2, 0)),
                fixed,
                fixed,
            ],
        ),
        out_shape=[
            jax.ShapeDtypeStruct((2, ROWS, 2 * HALF), F32),
            jax.ShapeDtypeStruct((2, ROWS, 2048), BF),
            jax.ShapeDtypeStruct((1024, CHUNK), BF),
            jax.ShapeDtypeStruct((1024, CHUNK), BF),
        ],
        compiler_params=params(26),
        cost_estimate=HIDDEN,
    )(pos, own, other, *blocks)


class Passages:
    def __init__(self, pos, own, other):
        self.z, self.x = pos[0], pos[1]
        self.numbers = (own, other)

    def question(self, side, p):
        return self.numbers[side][NPASS + p]

    def start(self, side, p):
        at = 0
        for k in range(p):
            at = at + self.numbers[side][k]
        return at

    def chip(self, side, p):
        q = self.question(side, p)
        return ((q >> 3) - self.z) & 3, ((q >> 1) - self.x) & 3, q & 1

    def row(self, half, side, p):
        zo, xo, core = self.chip(side, p)
        outer, inner = (zo, xo) if half == 0 else (xo, zo)
        return (outer * 4 + inner) * 64 + core * 16


def head_of_column(rows):
    return lax.broadcasted_iota(jnp.int32, (rows, LANES), 1) // 64


def head_matrix(meta, qg_refs, side, quad, which):
    head = head_of_column(DEC)
    parts = []
    for p in range(NPASS):
        row = pl.multiple_of(meta.row(quad, side, p) + which * 32, 16)
        tile = qg_refs[quad][pl.ds(row, DEC), :]
        parts += [jnp.where(head == a, tile, jnp.zeros_like(tile)) for a in range(4)]
    return jnp.concatenate(parts, axis=0)


def lane_value(numbers):
    lane = lax.broadcasted_iota(jnp.int32, (1, LANES), 1) // 64
    value = jnp.zeros((1, LANES), jnp.int32)
    for p in range(NPASS):
        value = jnp.where(lane == p, numbers[p], value)
    return value


def inside_mask(meta, side):
    row = lax.broadcasted_iota(jnp.int32, (ROWS, LANES), 0)
    starts = [meta.start(side, p) for p in range(NPASS + 1)]
    return (row >= lane_value(starts[:NPASS])) & (row < lane_value(starts[1:]))


def dot_nt(a, b):
    return lax.dot_general(a, b, NT, preferred_element_type=F32)


def forward_side(side, meta, k, v, qg, st_ref, num_ref):
    n = st_ref.shape[0]

    def put(row, value):
        st_ref[:, row : row + 1, :] = jnp.broadcast_to(value[None], (n, 1, LANES))

    inside = inside_mask(meta, side)
    question = lane_value([meta.question(side, p) for p in range(NPASS)]).astype(F32)
    for quad in range(QUADS):
        cols = slice(quad * CHUNK, (quad + 1) * CHUNK)
        scores = dot_nt(k[side, :, cols], head_matrix(meta, qg, side, quad, 0))
        scores = jnp.where(inside, scores, LOW)
        top = jnp.max(scores, axis=0, keepdims=True)
        unnorm = jnp.exp(scores - top)
        unnorm_b = unnorm.astype(BF)
        values = v[side, :, cols]
        dprob = dot_nt(values, head_matrix(meta, qg, side, quad, 1))
        at = side * QUADS + quad
        put(at, top)
        put(4 + at, jnp.sum(unnorm, axis=0, keepdims=True))
        put(8 + at, jnp.sum(unnorm_b.astype(F32) * dprob, axis=0, keepdims=True))
        put(12 + at, question)
        num_ref[side, quad] = lax.dot_general(values, unnorm_b, TN, preferred_element_type=F32)


def far_kernel(
    pos, own_numbers, other_numbers, enc_ref, acc_ref, a_top, a_low, b_top, b_low, qa_in, qb_in,
    k_ref, v_ref, qa_ref, qb_ref, st_ref, num_ref,
):
    meta = Passages(pos, own_numbers, other_numbers)
    step = pl.program_id(0)
    far = ((a_top, a_low), (b_top, b_low))

    @pl.when(step == 0)
    def questions():
        for side, source, out in ((0, qa_in, qa_ref), (1, qb_in, qb_ref)):
            out[...] = source[...]
            for inner in range(4):
                row = (inner % 2) * PIECE + 512
                at = (8 + inner) * 64
                out[at : at + 64, :] = far[side][inner // 2][row : row + 64, :]

    for side in range(2):
        lhs = enc_ref[0, :, side * 1024 : (side + 1) * 1024]
        total = jnp.dot(lhs, key_value(far[side]), preferred_element_type=F32)
        for t, out in ((0, k_ref), (1, v_ref)):
            at = t * HALF + side * CHUNK
            part = total[:, t * CHUNK : (t + 1) * CHUNK] + acc_ref[0, :, at : at + CHUNK]
            out[step, :, side * CHUNK : (side + 1) * CHUNK] = part.astype(BF)
    for side in range(2):
        @pl.when(step == side)
        def attend():
            forward_side(side, meta, k_ref, v_ref, (qa_ref, qb_ref), st_ref, num_ref)


def project_far(meta, enc_far, acc, blocks, qa, qb):
    def whole(shape):
        return pl.BlockSpec(shape, lambda i, *m: (0,) * len(shape))

    shapes = [
        jax.ShapeDtypeStruct((2, ROWS, HALF), BF),
        jax.ShapeDtypeStruct((2, ROWS, HALF), BF),
        jax.ShapeDtypeStruct((1024, CHUNK), BF),
        jax.ShapeDtypeStruct((1024, CHUNK), BF),
        jax.ShapeDtypeStruct((NZ * NX, 16, LANES), F32),
        jax.ShapeDtypeStruct((2, QUADS, LANES, CHUNK), F32),
    ]
    return pl.pallas_call(
        far_kernel,
        grid_spec=pltpu.PrefetchScalarGridSpec(
            num_scalar_prefetch=3,
            grid=(2,),
            in_specs=[
                pl.BlockSpec((1, ROWS, 2048), lambda i, *m: (i, 0, 0)),
                pl.BlockSpec((1, ROWS, 2 * HALF), lambda i, *m: (i, 0, 0)),
            ]
            + [whole(b.shape) for b in blocks]
            + [whole((1024, CHUNK))] * 2,
            out_specs=[whole(s.shape) for s in shapes],
        ),
        out_shape=shapes,
        compiler_params=params(24),
        cost_estimate=HIDDEN,
    )(*meta, enc_far, acc, *blocks, qa, qb)


def combine(meta, st_ref):
    n = st_ref.shape[0]
    own_question = [
        lane_value([meta.question(s, p) for p in range(NPASS)]).astype(F32) for s in range(2)
    ]

    def turned(value, k):
        return pltpu.roll(value, 64 * k, 1) if k else value

    tops = [None, None]
    for d in range(n):
        for k in range(NPASS):
            q, m = turned(st_ref[d, 12:16], k), turned(st_ref[d, 0:4], k)
            for s in range(2):
                term = jnp.where(q == own_question[s], m, LOW)
                tops[s] = term if tops[s] is None else jnp.maximum(tops[s], term)
    tops = [jnp.maximum(t[0:QUADS], t[QUADS:]) for t in tops]
    both = [jnp.concatenate([t, t], axis=0) for t in tops]
    totals, deltas = [0.0, 0.0], [0.0, 0.0]
    for d in range(n):
        for k in range(NPASS):
            q, m = turned(st_ref[d, 12:16], k), turned(st_ref[d, 0:4], k)
            l, e = turned(st_ref[d, 4:8], k), turned(st_ref[d, 8:12], k)
            for s in range(2):
                hit = q == own_question[s]
                scale = jnp.where(hit, jnp.exp(jnp.where(hit, m - both[s], 0.0)), 0.0)
                totals[s] = totals[s] + scale * l
                deltas[s] = deltas[s] + scale * e
    inverse = [1.0 / (t[0:QUADS] + t[QUADS:]) for t in totals]
    deltas = [(t[0:QUADS] + t[QUADS:]) * i for t, i in zip(deltas, inverse)]
    return tops, inverse, deltas


def take_weights(place, sources, w_ref):
    a_own, a_up, a_top, a_low, a_down, b_own, b_up, b_top, b_low, b_down = sources
    both = 2 * CHUNK
    for outer in range(4):
        @pl.when(place == outer)
        def take_a():
            for n in range(4):
                rows = pl.ds((n % 2) * PIECE, both)
                if outer == 2:
                    w_ref[0, n] = (a_top, a_low)[n // 2][rows, :]
                else:
                    w_ref[0, n] = (a_own, a_up, None, a_down)[outer][n // 2, rows, :]

    upper = place // 2
    rows = pl.ds(pl.multiple_of((place % 2) * PIECE, 64), both)
    for n, ref in ((0, b_own), (1, b_up), (3, b_down)):
        w_ref[1, n] = ref[upper, rows, :]
    for h, ref in ((0, b_top), (1, b_low)):
        @pl.when(upper == h)
        def take_b():
            w_ref[1, 2] = ref[rows, :]


def weights_tile(w_ref):
    rows = [
        jnp.concatenate(
            [w_ref[side, n, t * CHUNK : (t + 1) * CHUNK] for t in range(2) for side in range(2)],
            axis=1,
        )
        for n in range(4)
    ]
    return jnp.concatenate(rows, axis=0)


def weight_specs():
    shape = (2, 2 * PIECE, CHUNK)
    block = pl.BlockSpec(shape, lambda i, *p: (0, 0, 0), pipeline_mode=pl.Buffered(1))
    half = pl.BlockSpec(shape[1:], lambda i, *p: (0, 0), pipeline_mode=pl.Buffered(1))
    return [block, block, half, half, block] * 2


WEIGHT_SCRATCH = pltpu.VMEM((2, 4, 2 * CHUNK, CHUNK), BF)


def backward_kernel(
    pos, own_numbers, other_numbers, k_ref, v_ref, qa_ref, qb_ref, st_ref, num_ref, *refs
):
    sources, outs = refs[:10], refs[10:]
    kvg_ref, oth_ref, dense_ref, ctx_ref, w_ref = outs
    take_weights(pos[2], sources, w_ref)
    meta = Passages(pos, own_numbers, other_numbers)
    qg = (qa_ref, qb_ref)
    tops, inverses, deltas = combine(meta, st_ref)
    here = meta.z * 4 + meta.x
    ctx_ref[...] = jnp.zeros_like(ctx_ref)
    head = head_of_column(DEC)
    for side in (1, 0):
        inside = inside_mask(meta, side)
        for quad in range(QUADS):
            cols = slice(quad * CHUNK, (quad + 1) * CHUNK)
            at = side * QUADS + quad
            top, inverse = tops[side][quad : quad + 1], inverses[side][quad : quad + 1]
            queries = head_matrix(meta, qg, side, quad, 0)
            grads = head_matrix(meta, qg, side, quad, 1)
            scores = dot_nt(k_ref[side, :, cols], queries)
            unnorm = jnp.where(inside, jnp.exp(jnp.where(inside, scores - top, 0.0)), 0.0)
            probs = unnorm * inverse
            dprob = dot_nt(v_ref[side, :, cols], grads)
            ds = (probs * (dprob - deltas[side][quad : quad + 1])).astype(BF)
            for t, lanes, weight in ((0, queries, ds), (1, grads, probs.astype(BF))):
                turned = lax.dot_general(
                    lanes, weight, (((0,), (1,)), ((), ())), preferred_element_type=F32
                ).astype(BF)
                first = t * HALF + quad * CHUNK
                kvg_ref[first : first + CHUNK, side * ROWS : (side + 1) * ROWS] = turned
            scale = jnp.exp(st_ref[here, at : at + 1, :] - top) * inverse
            context = (num_ref[side, quad] * scale).T
            for p in range(NPASS):
                part = jnp.zeros((DEC, CHUNK), F32)
                for a in range(4):
                    first = p * 64 + a * DEC
                    part = jnp.where(head == a, context[first : first + DEC], part)
                ctx_ref[meta.question(side, p), :, cols] += part
    oth_ref[...] = jnp.dot(
        weights_tile(w_ref), kvg_ref[:, ROWS:], preferred_element_type=F32
    ).astype(BF)
    dense_ref[...] = ctx_ref[...].astype(BF)


def backward(meta, args, weights):
    def whole(shape):
        return pl.BlockSpec(shape, lambda i, *m: (0,) * len(shape))

    shapes = [
        jax.ShapeDtypeStruct((2 * HALF, 2 * ROWS), BF),
        jax.ShapeDtypeStruct((1024, ROWS), BF),
        jax.ShapeDtypeStruct((32, DEC, HALF), BF),
    ]
    return pl.pallas_call(
        backward_kernel,
        grid_spec=pltpu.PrefetchScalarGridSpec(
            num_scalar_prefetch=3,
            grid=(1,),
            in_specs=[whole(a.shape) for a in args]
            + weight_specs(),
            out_specs=[whole(s.shape) for s in shapes],
            scratch_shapes=[pltpu.VMEM((32, DEC, HALF), F32), WEIGHT_SCRATCH],
        ),
        out_shape=shapes,
        compiler_params=params(34),
        cost_estimate=HIDDEN,
    )(*meta, *args, *weights)


def own_kernel(places, kvg_ref, *refs):
    sources, (far_ref, base_ref, other_ref, w_ref) = refs[:10], refs[10:]
    take_weights(places[0], sources, w_ref)
    far_ref[...] = jnp.dot(
        weights_tile(w_ref), kvg_ref[:, :ROWS], preferred_element_type=F32
    ).astype(BF)
    take_weights(places[1], sources, w_ref)
    total = jnp.dot(weights_tile(w_ref), kvg_ref[...], preferred_element_type=F32)
    base_ref[...] = total[:, :ROWS]
    other_ref[...] = total[:, ROWS:].astype(BF)


def own_blocks(places, kvg, weights):
    out = pl.BlockSpec((1024, ROWS), lambda i, p: (0, 0))
    return pl.pallas_call(
        own_kernel,
        grid_spec=pltpu.PrefetchScalarGridSpec(
            num_scalar_prefetch=1,
            grid=(1,),
            in_specs=[pl.BlockSpec(kvg.shape, lambda i, p: (0, 0))] + weight_specs(),
            out_specs=[out] * 3,
            scratch_shapes=[WEIGHT_SCRATCH],
        ),
        out_shape=[jax.ShapeDtypeStruct((1024, ROWS), t) for t in (BF, F32, BF)],
        compiler_params=params(34),
        cost_estimate=HIDDEN,
    )(places, kvg, *weights)


def far_sums_kernel(own_ref, got_ref, top_ref, low_ref):
    for h, out in enumerate((top_ref, low_ref)):
        rows = slice(h * 512, (h + 1) * 512)
        out[...] = (own_ref[rows].astype(F32) + got_ref[rows].astype(F32)).astype(BF)


def far_sums(own, got):
    return pl.pallas_call(
        far_sums_kernel,
        out_shape=[jax.ShapeDtypeStruct((512, ROWS), BF)] * 2,
        compiler_params=params(16),
        cost_estimate=HIDDEN,
    )(own, got)


def near_grad_kernel(places, kvg_ref, *refs):
    sources, (out_ref, w_ref) = refs[:10], refs[10:]
    take_weights(places[pl.program_id(0)], sources, w_ref)
    total = jnp.dot(weights_tile(w_ref), kvg_ref[...], preferred_element_type=F32)
    core = places[2]
    out_ref[core, 0] = total[:, :ROWS].astype(BF)
    out_ref[1 - core, 0] = total[:, ROWS:].astype(BF)


def near_blocks(places, kvg, weights):
    return pl.pallas_call(
        near_grad_kernel,
        grid_spec=pltpu.PrefetchScalarGridSpec(
            num_scalar_prefetch=1,
            grid=(2,),
            in_specs=[pl.BlockSpec(kvg.shape, lambda i, p: (0, 0))] + weight_specs(),
            out_specs=pl.BlockSpec((2, 1, 1024, ROWS), lambda i, p: (0, i, 0, 0)),
            scratch_shapes=[WEIGHT_SCRATCH],
        ),
        out_shape=jax.ShapeDtypeStruct((2, 2, 1024, ROWS), BF),
        compiler_params=params(34),
        cost_estimate=HIDDEN,
    )(places, kvg, *weights)


def sums_kernel(near_ref, below_ref, above_ref, *outs):
    for out, k, h, more in zip(outs, (0, 1, 0, 1), (1, 0, 0, 1), (None, None, below_ref, above_ref)):
        rows = slice(h * 512, (h + 1) * 512)
        total = near_ref[0, k, rows].astype(F32) + near_ref[1, k, rows].astype(F32)
        if more is not None:
            total = total + more[...].astype(F32)
        out[...] = total.astype(BF)


def near_sums(near, below, above):
    return pl.pallas_call(
        sums_kernel,
        out_shape=[jax.ShapeDtypeStruct((512, ROWS), BF)] * 4,
        compiler_params=params(16),
        cost_estimate=HIDDEN,
    )(near, below, above)


def finish_kernel(
    place, base_ref, core_ref, up_top, up_low, down_top, down_low, parts_ref, out_ref, ctx_ref
):
    step = pl.program_id(0)

    @pl.when(step == 0)
    def context():
        for core in range(2):
            total = parts_ref[0, core].astype(F32)
            for n in range(1, NZ * NX):
                total = total + parts_ref[n, core].astype(F32)
            ctx_ref[0, :, core * HALF : (core + 1) * HALF] = total

    total = base_ref[...] + core_ref[...].astype(F32)

    def write(up, down):
        whole = total + up[...].astype(F32) + down[...].astype(F32)
        out_ref[...] = whole.T

    pl.when(step < 2)(lambda: write(up_top, down_top))
    pl.when(step >= 2)(lambda: write(up_low, down_low))


def finish(place, base, core_part, parts, ctx_parts):
    shape = (CHUNK, ROWS)
    block = pl.BlockSpec(shape, lambda n, p: (n, 0))
    top = pl.BlockSpec(shape, lambda n, p: (jnp.minimum(n, 1), 0))
    low = pl.BlockSpec(shape, lambda n, p: (jnp.maximum(n - 2, 0), 0))
    return pl.pallas_call(
        finish_kernel,
        grid_spec=pltpu.PrefetchScalarGridSpec(
            num_scalar_prefetch=1,
            grid=(4,),
            in_specs=[block, block, top, low, top, low]
            + [pl.BlockSpec(ctx_parts.shape, lambda n, p: (0, 0, 0, 0))],
            out_specs=[
                pl.BlockSpec((ROWS, CHUNK), lambda n, p: (0, p[n])),
                pl.BlockSpec((1, DEC, 2 * HALF), lambda n, p: (0, 0, 0)),
            ],
        ),
        out_shape=[
            jax.ShapeDtypeStruct((ROWS, 4 * CHUNK), F32),
            jax.ShapeDtypeStruct((1, DEC, 2 * HALF), F32),
        ],
        compiler_params=params(16),
        cost_estimate=HIDDEN,
    )(place, base, core_part, *parts, ctx_parts)


def body(enc_rows, key_weight, value_weight, queries, ctx_grad, passage_len, passage_question):
    z, x, core, y = (lax.axis_index(a) for a in ("z", "x", "core", "dec"))
    four = jnp.arange(4, dtype=jnp.int32)
    zs, xs = (z + four) % 4, (x + four) % 4
    places = ((y + four - z) % 4).astype(jnp.int32)
    near_places = jnp.stack([places[1], places[3], core.astype(jnp.int32)])
    own_places = jnp.stack([places[2], places[0]])
    pos = jnp.stack([z, x, places[2]]).astype(jnp.int32)

    cat = jnp.concatenate([key_weight, value_weight, queries[0], ctx_grad[0]], axis=0)
    mine = lax.dynamic_slice_in_dim(cat, core * HALF, HALF, 1)
    theirs = lax.dynamic_slice_in_dim(cat, (1 - core) * HALF, HALF, 1)
    got = perm(theirs, "core", 1)
    numbers = jnp.concatenate([passage_len[0], passage_question[:, 0]])
    other_numbers = perm(numbers, "core", 1)
    enc_after, got = phase(enc_rows, got)
    enc_other = perm(enc_after, "core", 1)
    first = jnp.where(core == 0, mine, got)
    second = jnp.where(core == 0, got, mine)
    chip = jnp.concatenate(
        [v[a:b] for a, b in ((0, 128), (128, 256), (256, 272), (272, 288)) for v in (first, second)],
        axis=0,
    )
    mid = PIECE // 2
    halves = phase(
        *[chip[h * mid : (h + 1) * mid, c : c + CHUNK] for c in (0, CHUNK) for h in (0, 1)]
    )

    steps = [(v, a, h) for v, (a, h) in zip(halves, (("x", 0), ("x", 1), ("z", 0), ("z", 1)))]
    met, pos, near_places, own_places, x_place, xs = phase(
        [pair_perm(v, a, h) for v, a, h in steps],
        pos,
        near_places,
        own_places,
        x.astype(jnp.int32).reshape(1),
        xs.astype(jnp.int32),
    )
    joined = phase(*join(list(zip(halves, met))))
    second = [pair_perm(v, a, 1 - h) for v, (_, a, h) in zip(joined, steps)]
    a_own = first_block(x_place, (joined[0], second[0], joined[1], second[1]))
    b_own = first_block(pos[0:1], (joined[2], second[2], joined[3], second[3]))
    enc_other, other_numbers, a_own, b_own = phase(enc_other, other_numbers, a_own, b_own)

    a_up, a_down = phase(perm(a_own, "z", -1), perm(a_own, "z", 1))
    b_up, b_down = phase(perm(b_own, "x", -1), perm(b_own, "x", 1))
    a_first, a_second = phase(*take_halves(a_up, a_down))
    b_first, b_second = phase(*take_halves(b_up, b_down))
    far = [
        perm(a_first, "z", -1),
        perm(a_second, "z", 1),
        perm(b_first, "x", -1),
        perm(b_second, "x", 1),
    ]
    acc, enc_far, qa, qb = project_near(
        pos, enc_rows, enc_other, [a_own, a_up, a_down, b_own, b_up, b_down]
    )
    far, acc, enc_far, qa, qb = phase(far, acc, enc_far, qa, qb)
    meta = (pos, numbers, other_numbers)
    keys, values, qa, qb, stats, numer = project_far(meta, enc_far, acc, far, qa, qb)
    stats_all = lax.all_to_all(stats, ("z", "x"), 0, 0, tiled=True)
    weights = [a_own, a_up, far[0], far[1], a_down, b_own, b_up, far[2], far[3], b_down]
    kvg, far_other, dense = backward(
        meta, (keys, values, qa, qb, stats_all, numer), weights
    )

    far_got = perm(far_other, "core", 1)
    far_own, base, base_other = own_blocks(own_places, kvg, weights)
    far_got, far_own, base, base_other, kvg, dense = phase(
        far_got, far_own, base, base_other, kvg, dense
    )

    far_top, far_low, base, base_other, kvg, dense = phase(
        *far_sums(far_own, far_got), base, base_other, kvg, dense
    )
    from_below = perm(far_top, "dec", 1)
    from_above = perm(far_low, "dec", -1)
    near = lax.all_to_all(near_blocks(near_places, kvg, weights), "core", 0, 0, tiled=True)
    from_below, from_above, near, base, base_other, dense = phase(
        from_below, from_above, near, base, base_other, dense
    )

    *sums, dense, base_other = phase(
        *near_sums(near, from_below, from_above), dense, base_other
    )
    low_below = perm(sums[0], "dec", 1)
    top_above = perm(sums[1], "dec", -1)
    top_below = perm(sums[2], "dec", 1)
    low_above = perm(sums[3], "dec", -1)
    base_got = perm(base_other, "core", 1)
    parts = lax.all_to_all(dense, ENC, 0, 0, tiled=True).reshape(NZ * NX, NC, DEC, HALF)
    low_below, top_above, top_below, low_above, base_got, parts = phase(
        low_below, top_above, top_below, low_above, base_got, parts
    )
    enc_grad, ctx = finish(
        xs, base, base_got, (top_below, low_below, top_above, low_above), parts
    )
    return ctx, enc_grad


def solution(mesh):
    grid = Mesh(mesh.devices.reshape(NZ, NX, NC, NY), ("z", "x", "core", "dec"))
    return jax.shard_map(
        body,
        mesh=grid,
        in_specs=(
            P(ENC, None),
            P(ENC, "dec"),
            P(ENC, "dec"),
            P(ENC, None, "dec"),
            P(ENC, None, "dec"),
            P(ENC, None),
            P(ENC, None),
        ),
        out_specs=(P(ENC, None, "dec"), P(ENC, "dec")),
        check_vma=False,
    )
```

```python
import functools

import jax
import jax.numpy as jnp
from jax import lax
from jax.experimental import pallas as pl
from jax.experimental.pallas import tpu as pltpu
from jax.sharding import Mesh, PartitionSpec as P

BF = jnp.bfloat16
F32 = jnp.float32
NZ, NX, NC, NY = 4, 4, 2, 4
ENC = ("z", "x", "core")
ROWS = 512
D = 4096
HALF = 512
CHUNK = 256
PIECE = 576
DEC = 16
NPASS = 4
QUADS = 2
LANES = 256
LOW = -1e30
HIDDEN = pl.CostEstimate(flops=200_000_000, bytes_accessed=0, transcendentals=0)
NT = (((1,), (1,)), ((), ()))
TN = (((0,), (0,)), ((), ()))


def perm(v, axis, shift):
    n = {"z": NZ, "x": NX, "core": NC, "dec": NY}[axis]
    return lax.ppermute(v, axis, [(i, (i + shift) % n) for i in range(n)])


def phase(*values):
    return lax.optimization_barrier(values)


def params(mib):
    return pltpu.CompilerParams(vmem_limit_bytes=mib * 1024 * 1024)


def pair_perm(v, axis, odd):
    turn = (lambda i: i + 1 - 2 * (i % 2)) if not odd else (lambda i: i - 1 + 2 * (i % 2))
    return lax.ppermute(v, axis, [(i, turn(i) % 4) for i in range(4)])


def join_kernel(*refs):
    outs = refs[8:]
    rows = PIECE // 2
    for k, out in enumerate(outs):
        out[:rows] = refs[2 * k][...]
        out[rows:] = refs[2 * k + 1][...]


def join(pairs):
    return pl.pallas_call(
        join_kernel,
        out_shape=[jax.ShapeDtypeStruct((PIECE, CHUNK), BF)] * 4,
        compiler_params=params(16),
        cost_estimate=HIDDEN,
    )(*[v for p in pairs for v in p])


def first_kernel(place, joined0, second0, joined1, second1, out):
    mid = PIECE // 2
    odd = place[0] % 2

    def slot(o, h, value):
        at = (o % 2) * PIECE + h * mid
        out[o // 2, at : at + mid, :] = value

    for h, joined, second in ((0, joined0, second0), (1, joined1, second1)):
        slot(0, h, joined[:mid])
        slot(2, h, second[mid:])
        for parity in range(2):
            @pl.when(odd == parity)
            def near():
                one = 1 if h == parity else 3
                slot(one, h, joined[mid:])
                slot(4 - one, h, second[:mid])


def first_block(place, pieces):
    def whole(p):
        return pl.BlockSpec(p.shape, lambda i, o: (0, 0))

    return pl.pallas_call(
        first_kernel,
        grid_spec=pltpu.PrefetchScalarGridSpec(
            num_scalar_prefetch=1,
            grid=(1,),
            in_specs=[whole(p) for p in pieces],
            out_specs=pl.BlockSpec((2, 2 * PIECE, CHUNK), lambda i, o: (0, 0, 0)),
        ),
        out_shape=jax.ShapeDtypeStruct((2, 2 * PIECE, CHUNK), BF),
        compiler_params=params(16),
        cost_estimate=HIDDEN,
    )(place, *pieces)


def halves_kernel(up_ref, down_ref, first_ref, second_ref):
    first_ref[...] = up_ref[0]
    second_ref[...] = down_ref[0]


def take_halves(up, down):
    half = (1, 2 * PIECE, CHUNK)
    return pl.pallas_call(
        halves_kernel,
        grid=(1,),
        in_specs=[pl.BlockSpec(half, lambda i: (0, 0, 0)), pl.BlockSpec(half, lambda i: (1, 0, 0))],
        out_specs=[pl.BlockSpec(half[1:], lambda i: (0, 0))] * 2,
        out_shape=[jax.ShapeDtypeStruct(half[1:], BF)] * 2,
        compiler_params=params(16),
        cost_estimate=HIDDEN,
    )(up, down)


def key_value(halves):
    rows = []
    for half in halves:
        for at in (0, PIECE):
            rows.append(
                jnp.concatenate(
                    [half[at : at + CHUNK, :], half[at + CHUNK : at + 2 * CHUNK, :]], axis=1
                )
            )
    return jnp.concatenate(rows, axis=0)


def near_kernel(pos, own_ref, oth_ref, *refs):
    blocks, (acc_refs, enc_refs, (qa_ref, qb_ref)) = refs[:6], (refs[6:8], refs[8:10], refs[10:])
    z, x = pos[0], pos[1]
    step = pl.program_id(0)

    def columns(ref, side, outer, inners):
        parts = []
        for inner in inners:
            zo, xo = (outer, inner) if side == 0 else (inner, outer)
            chip = ((z + zo) & 3) * 4 + ((x + xo) & 3)
            parts.append(ref[:, pl.ds(pl.multiple_of(chip * CHUNK, CHUNK), CHUNK)])
        return jnp.concatenate(parts, axis=1)

    def run(ref):
        for side in range(2):
            total = None
            for b, outer in enumerate((0, 1, 3)):
                block = blocks[side * 3 + b]
                rhs = key_value([block.at[h] for h in range(2)])
                lhs = columns(ref, side, outer, range(4))
                term = jnp.dot(lhs, rhs, preferred_element_type=F32)
                total = term if total is None else total + term
            acc_refs[side][0] = total
            enc_refs[side][0] = columns(ref, side, 2, range(4))

    pl.when(step < 2)(lambda: run(own_ref))
    pl.when(step >= 2)(lambda: run(oth_ref))

    @pl.when(step == 0)
    def questions():
        for side, out in ((0, qa_ref), (1, qb_ref)):
            for b, outer in enumerate((0, 1, 3)):
                for inner in range(4):
                    row = (inner % 2) * PIECE + 512
                    at = (outer * 4 + inner) * 64
                    out[at : at + 64, :] = blocks[side * 3 + b][inner // 2, row : row + 64]
            out[512:768, :] = jnp.zeros((256, CHUNK), BF)


def project_near(pos, own, other, blocks):
    tile = ROWS // 2
    fixed = pl.BlockSpec((1024, CHUNK), lambda i, o: (0, 0))
    return pl.pallas_call(
        near_kernel,
        grid_spec=pltpu.PrefetchScalarGridSpec(
            num_scalar_prefetch=1,
            grid=(4,),
            in_specs=[
                pl.BlockSpec((tile, D), lambda i, o: (jnp.minimum(i, 1), 0)),
                pl.BlockSpec((tile, D), lambda i, o: (jnp.maximum(i - 2, 0), 0)),
            ]
            + [pl.BlockSpec(b.shape, lambda i, o: (0, 0, 0)) for b in blocks],
            out_specs=[
                pl.BlockSpec((1, tile, HALF), lambda i, o: (i // 2, i % 2, 0)),
                pl.BlockSpec((1, tile, HALF), lambda i, o: (i // 2, i % 2, 0)),
                pl.BlockSpec((1, tile, 1024), lambda i, o: (i // 2, i % 2, 0)),
                pl.BlockSpec((1, tile, 1024), lambda i, o: (i // 2, i % 2, 0)),
                fixed,
                fixed,
            ],
        ),
        out_shape=[
            jax.ShapeDtypeStruct((2, ROWS, HALF), F32),
            jax.ShapeDtypeStruct((2, ROWS, HALF), F32),
            jax.ShapeDtypeStruct((2, ROWS, 1024), BF),
            jax.ShapeDtypeStruct((2, ROWS, 1024), BF),
            jax.ShapeDtypeStruct((1024, CHUNK), BF),
            jax.ShapeDtypeStruct((1024, CHUNK), BF),
        ],
        compiler_params=params(26),
        cost_estimate=HIDDEN,
    )(pos, own, other, *blocks)


class Passages:
    def __init__(self, pos, own, other):
        self.z, self.x = pos[0], pos[1]
        self.numbers = (own, other)

    def question(self, side, p):
        return self.numbers[side][NPASS + p]

    def start(self, side, p):
        at = 0
        for k in range(p):
            at = at + self.numbers[side][k]
        return at

    def chip(self, side, p):
        q = self.question(side, p)
        return ((q >> 3) - self.z) & 3, ((q >> 1) - self.x) & 3, q & 1

    def row(self, half, side, p):
        zo, xo, core = self.chip(side, p)
        outer, inner = (zo, xo) if half == 0 else (xo, zo)
        return (outer * 4 + inner) * 64 + core * 16


def head_of_column(rows):
    return lax.broadcasted_iota(jnp.int32, (rows, LANES), 1) // 64


def head_matrix(meta, q_ref, side, quad, which):
    head = head_of_column(DEC)
    parts = []
    for p in range(NPASS):
        row = pl.multiple_of(meta.row(quad, side, p) + which * 32, 16)
        tile = q_ref[pl.ds(row, DEC), :]
        parts += [jnp.where(head == a, tile, jnp.zeros_like(tile)) for a in range(4)]
    return jnp.concatenate(parts, axis=0)


def lane_value(numbers):
    lane = lax.broadcasted_iota(jnp.int32, (1, LANES), 1) // 64
    value = jnp.zeros((1, LANES), jnp.int32)
    for p in range(NPASS):
        value = jnp.where(lane == p, numbers[p], value)
    return value


def inside_mask(meta, side):
    row = lax.broadcasted_iota(jnp.int32, (ROWS, LANES), 0)
    starts = [meta.start(side, p) for p in range(NPASS + 1)]
    return (row >= lane_value(starts[:NPASS])) & (row < lane_value(starts[1:]))


def dot_nt(a, b):
    return lax.dot_general(a, b, NT, preferred_element_type=F32)


def forward_side(side, quad, meta, k, v, q_ref, put, num_ref):
    inside = inside_mask(meta, side)
    scores = dot_nt(k, head_matrix(meta, q_ref, side, quad, 0))
    scores = jnp.where(inside, scores, LOW)
    top = jnp.max(scores, axis=0, keepdims=True)
    unnorm = jnp.exp(scores - top)
    unnorm_b = unnorm.astype(BF)
    dprob = dot_nt(v, head_matrix(meta, q_ref, side, quad, 1))
    put(0, top)
    put(1, jnp.sum(unnorm, axis=0, keepdims=True))
    put(2, jnp.sum(unnorm_b.astype(F32) * dprob, axis=0, keepdims=True))
    num_ref[side] = lax.dot_general(v, unnorm_b, TN, preferred_element_type=F32)


def far_kernel(quad, pos, own_numbers, other_numbers, *refs):
    meta = Passages(pos, own_numbers, other_numbers)
    enc_ref, acc_ref, top, low, q_in = refs[:5]
    before_ref = refs[5] if quad else None
    k_ref, v_ref, q_ref, st_ref, num_ref = refs[-5:]
    step = pl.program_id(0)

    @pl.when(step == 0)
    def questions():
        q_ref[...] = q_in[...]
        for inner in range(4):
            row = (inner % 2) * PIECE + 512
            at = (8 + inner) * 64
            q_ref[at : at + 64, :] = (top, low)[inner // 2][row : row + 64, :]

    total = acc_ref[0] + jnp.dot(
        enc_ref[0], key_value((top, low)), preferred_element_type=F32
    )
    keys, values = total[:, :CHUNK].astype(BF), total[:, CHUNK:].astype(BF)
    k_ref[step] = keys
    v_ref[step] = values

    def put_all(row, value):
        st_ref[:, row : row + 1, :] = jnp.broadcast_to(value[None], (NZ * NX, 1, LANES))

    for side in range(2):
        def put(r, value):
            if quad:
                put_all(4 * r + side * 2 + 1, value)
            else:
                st_ref[r * 2 + side : r * 2 + side + 1, :] = value

        @pl.when(step == side)
        def attend():
            forward_side(side, quad, meta, k_ref[side], v_ref[side], q_ref, put, num_ref)
            if quad:
                question = lane_value([meta.question(side, p) for p in range(NPASS)]).astype(F32)
                for r in range(3):
                    put_all(4 * r + side * 2, before_ref[r * 2 + side : r * 2 + side + 1, :])
                for q in range(QUADS):
                    put_all(12 + side * 2 + q, question)


def project_far(quad, meta, enc_far, acc, blocks, q, before):
    def whole(shape):
        return pl.BlockSpec(shape, lambda i, *m: (0,) * len(shape))

    stats = (NZ * NX, 16, LANES) if quad else (8, LANES)
    shapes = [
        jax.ShapeDtypeStruct((2, ROWS, CHUNK), BF),
        jax.ShapeDtypeStruct((2, ROWS, CHUNK), BF),
        jax.ShapeDtypeStruct((1024, CHUNK), BF),
        jax.ShapeDtypeStruct(stats, F32),
        jax.ShapeDtypeStruct((2, LANES, CHUNK), F32),
    ]
    extra = [before] if quad else []
    return pl.pallas_call(
        functools.partial(far_kernel, quad),
        grid_spec=pltpu.PrefetchScalarGridSpec(
            num_scalar_prefetch=3,
            grid=(2,),
            in_specs=[
                pl.BlockSpec((1, ROWS, 1024), lambda i, *m: (i, 0, 0)),
                pl.BlockSpec((1, ROWS, HALF), lambda i, *m: (i, 0, 0)),
            ]
            + [whole(b.shape) for b in blocks + [q] + extra],
            out_specs=[whole(s.shape) for s in shapes],
        ),
        out_shape=shapes,
        compiler_params=params(20),
        cost_estimate=HIDDEN,
    )(*meta, enc_far, acc, *blocks, q, *extra)


def combine(meta, st_ref):
    n = st_ref.shape[0]
    own_question = [
        lane_value([meta.question(s, p) for p in range(NPASS)]).astype(F32) for s in range(2)
    ]

    def turned(value, k):
        return pltpu.roll(value, 64 * k, 1) if k else value

    tops = [None, None]
    for d in range(n):
        for k in range(NPASS):
            q, m = turned(st_ref[d, 12:16], k), turned(st_ref[d, 0:4], k)
            for s in range(2):
                term = jnp.where(q == own_question[s], m, LOW)
                tops[s] = term if tops[s] is None else jnp.maximum(tops[s], term)
    tops = [jnp.maximum(t[0:QUADS], t[QUADS:]) for t in tops]
    both = [jnp.concatenate([t, t], axis=0) for t in tops]
    totals, deltas = [0.0, 0.0], [0.0, 0.0]
    for d in range(n):
        for k in range(NPASS):
            q, m = turned(st_ref[d, 12:16], k), turned(st_ref[d, 0:4], k)
            l, e = turned(st_ref[d, 4:8], k), turned(st_ref[d, 8:12], k)
            for s in range(2):
                hit = q == own_question[s]
                scale = jnp.where(hit, jnp.exp(jnp.where(hit, m - both[s], 0.0)), 0.0)
                totals[s] = totals[s] + scale * l
                deltas[s] = deltas[s] + scale * e
    inverse = [1.0 / (t[0:QUADS] + t[QUADS:]) for t in totals]
    deltas = [(t[0:QUADS] + t[QUADS:]) * i for t, i in zip(deltas, inverse)]
    return tops, inverse, deltas


def take_weights(place, sources, w_ref):
    a_own, a_up, a_top, a_low, a_down, b_own, b_up, b_top, b_low, b_down = sources
    both = 2 * CHUNK
    for outer in range(4):
        @pl.when(place == outer)
        def take_a():
            for n in range(4):
                rows = pl.ds((n % 2) * PIECE, both)
                if outer == 2:
                    w_ref[0, n] = (a_top, a_low)[n // 2][rows, :]
                else:
                    w_ref[0, n] = (a_own, a_up, None, a_down)[outer][n // 2, rows, :]

    upper = place // 2
    rows = pl.ds(pl.multiple_of((place % 2) * PIECE, 64), both)
    for n, ref in ((0, b_own), (1, b_up), (3, b_down)):
        w_ref[1, n] = ref[upper, rows, :]
    for h, ref in ((0, b_top), (1, b_low)):
        @pl.when(upper == h)
        def take_b():
            w_ref[1, 2] = ref[rows, :]


def weights_tile(w_ref):
    rows = [
        jnp.concatenate(
            [w_ref[side, n, t * CHUNK : (t + 1) * CHUNK] for t in range(2) for side in range(2)],
            axis=1,
        )
        for n in range(4)
    ]
    return jnp.concatenate(rows, axis=0)


def weight_specs():
    shape = (2, 2 * PIECE, CHUNK)
    block = pl.BlockSpec(shape, lambda i, *p: (0, 0, 0), pipeline_mode=pl.Buffered(1))
    half = pl.BlockSpec(shape[1:], lambda i, *p: (0, 0), pipeline_mode=pl.Buffered(1))
    return [block, block, half, half, block] * 2


WEIGHT_SCRATCH = pltpu.VMEM((2, 4, 2 * CHUNK, CHUNK), BF)


def backward_kernel(
    pos, own_numbers, other_numbers, ka_ref, va_ref, qa_ref, na_ref, kb_ref, vb_ref, qb_ref, nb_ref,
    st_ref, *refs
):
    sources, outs = refs[:10], refs[10:]
    kvg_ref, own_ref, oth_ref, dense_ref, ctx_ref, w_ref = outs
    take_weights(pos[2], sources, w_ref)
    meta = Passages(pos, own_numbers, other_numbers)
    halves = ((ka_ref, va_ref, qa_ref, na_ref), (kb_ref, vb_ref, qb_ref, nb_ref))
    tops, inverses, deltas = combine(meta, st_ref)
    here = meta.z * 4 + meta.x
    ctx_ref[...] = jnp.zeros_like(ctx_ref)
    head = head_of_column(DEC)
    for side in (1, 0):
        inside = inside_mask(meta, side)
        for quad in range(QUADS):
            cols = slice(quad * CHUNK, (quad + 1) * CHUNK)
            at = side * QUADS + quad
            top, inverse = tops[side][quad : quad + 1], inverses[side][quad : quad + 1]
            k_ref, v_ref, q_ref, num_ref = halves[quad]
            queries = head_matrix(meta, q_ref, side, quad, 0)
            grads = head_matrix(meta, q_ref, side, quad, 1)
            scores = dot_nt(k_ref[side], queries)
            unnorm = jnp.where(inside, jnp.exp(jnp.where(inside, scores - top, 0.0)), 0.0)
            probs = unnorm * inverse
            dprob = dot_nt(v_ref[side], grads)
            ds = (probs * (dprob - deltas[side][quad : quad + 1])).astype(BF)
            for t, lanes, weight in ((0, queries, ds), (1, grads, probs.astype(BF))):
                turned = lax.dot_general(
                    lanes, weight, (((0,), (1,)), ((), ())), preferred_element_type=F32
                ).astype(BF)
                first = t * HALF + quad * CHUNK
                kvg_ref[first : first + CHUNK, side * ROWS : (side + 1) * ROWS] = turned
            scale = jnp.exp(st_ref[here, at : at + 1, :] - top) * inverse
            context = (num_ref[side] * scale).T
            for p in range(NPASS):
                part = jnp.zeros((DEC, CHUNK), F32)
                for a in range(4):
                    first = p * 64 + a * DEC
                    part = jnp.where(head == a, context[first : first + DEC], part)
                ctx_ref[meta.question(side, p), :, cols] += part
    total = jnp.dot(weights_tile(w_ref), kvg_ref[...], preferred_element_type=F32)
    own_ref[...] = total[:, :ROWS].astype(BF)
    oth_ref[...] = total[:, ROWS:].astype(BF)
    dense_ref[...] = ctx_ref[...].astype(BF)


def backward(meta, args, weights):
    def whole(shape):
        return pl.BlockSpec(shape, lambda i, *m: (0,) * len(shape))

    shapes = [
        jax.ShapeDtypeStruct((2 * HALF, 2 * ROWS), BF),
        jax.ShapeDtypeStruct((1024, ROWS), BF),
        jax.ShapeDtypeStruct((1024, ROWS), BF),
        jax.ShapeDtypeStruct((32, DEC, HALF), BF),
    ]
    return pl.pallas_call(
        backward_kernel,
        grid_spec=pltpu.PrefetchScalarGridSpec(
            num_scalar_prefetch=3,
            grid=(1,),
            in_specs=[whole(a.shape) for a in args]
            + weight_specs(),
            out_specs=[whole(s.shape) for s in shapes],
            scratch_shapes=[pltpu.VMEM((32, DEC, HALF), F32), WEIGHT_SCRATCH],
        ),
        out_shape=shapes,
        compiler_params=params(34),
        cost_estimate=HIDDEN,
    )(*meta, *args, *weights)


def base_kernel(places, kvg_ref, *refs):
    sources, (base_ref, other_ref, w_ref) = refs[:10], refs[10:]
    take_weights(places[0], sources, w_ref)
    total = jnp.dot(weights_tile(w_ref), kvg_ref[...], preferred_element_type=F32)
    base_ref[...] = total[:, :ROWS]
    other_ref[...] = total[:, ROWS:].astype(BF)


def base_blocks(places, kvg, weights):
    out = pl.BlockSpec((1024, ROWS), lambda i, p: (0, 0))
    return pl.pallas_call(
        base_kernel,
        grid_spec=pltpu.PrefetchScalarGridSpec(
            num_scalar_prefetch=1,
            grid=(1,),
            in_specs=[pl.BlockSpec(kvg.shape, lambda i, p: (0, 0))] + weight_specs(),
            out_specs=[out] * 2,
            scratch_shapes=[WEIGHT_SCRATCH],
        ),
        out_shape=[jax.ShapeDtypeStruct((1024, ROWS), t) for t in (F32, BF)],
        compiler_params=params(34),
        cost_estimate=HIDDEN,
    )(places, kvg, *weights)


def far_sums_kernel(own_ref, got_ref, top_ref, low_ref):
    for h, out in enumerate((top_ref, low_ref)):
        rows = slice(h * 512, (h + 1) * 512)
        out[...] = (own_ref[rows].astype(F32) + got_ref[rows].astype(F32)).astype(BF)


def far_sums(own, got):
    return pl.pallas_call(
        far_sums_kernel,
        out_shape=[jax.ShapeDtypeStruct((512, ROWS), BF)] * 2,
        compiler_params=params(16),
        cost_estimate=HIDDEN,
    )(own, got)


def near_grad_kernel(places, kvg_ref, *refs):
    sources, (out_ref, w_ref) = refs[:10], refs[10:]
    take_weights(places[pl.program_id(0)], sources, w_ref)
    total = jnp.dot(weights_tile(w_ref), kvg_ref[...], preferred_element_type=F32)
    core = places[2]
    out_ref[core, 0] = total[:, :ROWS].astype(BF)
    out_ref[1 - core, 0] = total[:, ROWS:].astype(BF)


def near_blocks(places, kvg, weights):
    return pl.pallas_call(
        near_grad_kernel,
        grid_spec=pltpu.PrefetchScalarGridSpec(
            num_scalar_prefetch=1,
            grid=(2,),
            in_specs=[pl.BlockSpec(kvg.shape, lambda i, p: (0, 0))] + weight_specs(),
            out_specs=pl.BlockSpec((2, 1, 1024, ROWS), lambda i, p: (0, i, 0, 0)),
            scratch_shapes=[WEIGHT_SCRATCH],
        ),
        out_shape=jax.ShapeDtypeStruct((2, 2, 1024, ROWS), BF),
        compiler_params=params(34),
        cost_estimate=HIDDEN,
    )(places, kvg, *weights)


def sums_kernel(near_ref, below_ref, above_ref, *outs):
    for out, k, h, more in zip(outs, (0, 1, 0, 1), (1, 0, 0, 1), (None, None, below_ref, above_ref)):
        rows = slice(h * 512, (h + 1) * 512)
        total = near_ref[0, k, rows].astype(F32) + near_ref[1, k, rows].astype(F32)
        if more is not None:
            total = total + more[...].astype(F32)
        out[...] = total.astype(BF)


def near_sums(near, below, above):
    return pl.pallas_call(
        sums_kernel,
        out_shape=[jax.ShapeDtypeStruct((512, ROWS), BF)] * 4,
        compiler_params=params(16),
        cost_estimate=HIDDEN,
    )(near, below, above)


def finish_kernel(
    place, base_ref, core_ref, up_top, up_low, down_top, down_low, parts_ref, out_ref, ctx_ref
):
    step = pl.program_id(0)

    @pl.when(step == 0)
    def context():
        for core in range(2):
            total = parts_ref[0, core].astype(F32)
            for n in range(1, NZ * NX):
                total = total + parts_ref[n, core].astype(F32)
            ctx_ref[0, :, core * HALF : (core + 1) * HALF] = total

    total = base_ref[...] + core_ref[...].astype(F32)

    def write(up, down):
        whole = total + up[...].astype(F32) + down[...].astype(F32)
        out_ref[...] = whole.T

    pl.when(step < 2)(lambda: write(up_top, down_top))
    pl.when(step >= 2)(lambda: write(up_low, down_low))


def finish(place, base, core_part, parts, ctx_parts):
    shape = (CHUNK, ROWS)
    block = pl.BlockSpec(shape, lambda n, p: (n, 0))
    top = pl.BlockSpec(shape, lambda n, p: (jnp.minimum(n, 1), 0))
    low = pl.BlockSpec(shape, lambda n, p: (jnp.maximum(n - 2, 0), 0))
    return pl.pallas_call(
        finish_kernel,
        grid_spec=pltpu.PrefetchScalarGridSpec(
            num_scalar_prefetch=1,
            grid=(4,),
            in_specs=[block, block, top, low, top, low]
            + [pl.BlockSpec(ctx_parts.shape, lambda n, p: (0, 0, 0, 0))],
            out_specs=[
                pl.BlockSpec((ROWS, CHUNK), lambda n, p: (0, p[n])),
                pl.BlockSpec((1, DEC, 2 * HALF), lambda n, p: (0, 0, 0)),
            ],
        ),
        out_shape=[
            jax.ShapeDtypeStruct((ROWS, 4 * CHUNK), F32),
            jax.ShapeDtypeStruct((1, DEC, 2 * HALF), F32),
        ],
        compiler_params=params(16),
        cost_estimate=HIDDEN,
    )(place, base, core_part, *parts, ctx_parts)


def body(enc_rows, key_weight, value_weight, queries, ctx_grad, passage_len, passage_question):
    z, x, core, y = (lax.axis_index(a) for a in ("z", "x", "core", "dec"))
    four = jnp.arange(4, dtype=jnp.int32)
    zs, xs = (z + four) % 4, (x + four) % 4
    places = ((y + four - z) % 4).astype(jnp.int32)
    near_places = jnp.stack([places[1], places[3], core.astype(jnp.int32)])
    base_place = places[0:1]
    pos = jnp.stack([z, x, places[2]]).astype(jnp.int32)

    cat = jnp.concatenate([key_weight, value_weight, queries[0], ctx_grad[0]], axis=0)
    mine = lax.dynamic_slice_in_dim(cat, core * HALF, HALF, 1)
    theirs = lax.dynamic_slice_in_dim(cat, (1 - core) * HALF, HALF, 1)
    got = perm(theirs, "core", 1)
    numbers = jnp.concatenate([passage_len[0], passage_question[:, 0]])
    other_numbers = perm(numbers, "core", 1)
    enc_after, got = phase(enc_rows, got)
    enc_other = perm(enc_after, "core", 1)
    first = jnp.where(core == 0, mine, got)
    second = jnp.where(core == 0, got, mine)
    chip = jnp.concatenate(
        [v[a:b] for a, b in ((0, 128), (128, 256), (256, 272), (272, 288)) for v in (first, second)],
        axis=0,
    )
    mid = PIECE // 2
    halves = phase(
        *[chip[h * mid : (h + 1) * mid, c : c + CHUNK] for c in (0, CHUNK) for h in (0, 1)]
    )

    steps = [(v, a, h) for v, (a, h) in zip(halves, (("x", 0), ("x", 1), ("z", 0), ("z", 1)))]
    met, pos, near_places, base_place, x_place, xs = phase(
        [pair_perm(v, a, h) for v, a, h in steps],
        pos,
        near_places,
        base_place,
        x.astype(jnp.int32).reshape(1),
        xs.astype(jnp.int32),
    )
    joined = phase(*join(list(zip(halves, met))))
    second = [pair_perm(v, a, 1 - h) for v, (_, a, h) in zip(joined, steps)]
    a_own = first_block(x_place, (joined[0], second[0], joined[1], second[1]))
    b_own = first_block(pos[0:1], (joined[2], second[2], joined[3], second[3]))
    enc_other, other_numbers, a_own, b_own = phase(enc_other, other_numbers, a_own, b_own)

    a_up, a_down = phase(perm(a_own, "z", -1), perm(a_own, "z", 1))
    b_up, b_down = phase(perm(b_own, "x", -1), perm(b_own, "x", 1))
    a_first, a_second = phase(*take_halves(a_up, a_down))
    b_first, b_second = phase(*take_halves(b_up, b_down))
    far = [
        perm(a_first, "z", -1),
        perm(a_second, "z", 1),
        perm(b_first, "x", -1),
        perm(b_second, "x", 1),
    ]
    acc_a, acc_b, enc_a, enc_b, qa, qb = project_near(
        pos, enc_rows, enc_other, [a_own, a_up, a_down, b_own, b_up, b_down]
    )
    meta = (pos, numbers, other_numbers)
    acc_a, acc_b, enc_a, enc_b, qa, qb, far[0], far[1] = phase(
        acc_a, acc_b, enc_a, enc_b, qa, qb, *far[:2]
    )
    ka, va, qa, stats_a, numer_a = project_far(0, meta, enc_a, acc_a, far[:2], qa, None)
    stats_a, far[2], far[3] = phase(stats_a, far[2], far[3])
    kb, vb, qb, stats, numer_b = project_far(1, meta, enc_b, acc_b, far[2:], qb, stats_a)
    stats_all = lax.all_to_all(stats, ("z", "x"), 0, 0, tiled=True)
    weights = [a_own, a_up, far[0], far[1], a_down, b_own, b_up, far[2], far[3], b_down]
    kvg, far_own, far_other, dense = backward(
        meta, (ka, va, qa, numer_a, kb, vb, qb, numer_b, stats_all), weights
    )

    far_got = perm(far_other, "core", 1)
    base, base_other = base_blocks(base_place, kvg, weights)
    far_got, far_own, base, base_other, kvg, dense = phase(
        far_got, far_own, base, base_other, kvg, dense
    )

    far_top, far_low, base, base_other, kvg, dense = phase(
        *far_sums(far_own, far_got), base, base_other, kvg, dense
    )
    from_below = perm(far_top, "dec", 1)
    from_above = perm(far_low, "dec", -1)
    near = lax.all_to_all(near_blocks(near_places, kvg, weights), "core", 0, 0, tiled=True)
    from_below, from_above, near, base, base_other, dense = phase(
        from_below, from_above, near, base, base_other, dense
    )

    *sums, dense, base_other = phase(
        *near_sums(near, from_below, from_above), dense, base_other
    )
    low_below = perm(sums[0], "dec", 1)
    top_above = perm(sums[1], "dec", -1)
    top_below = perm(sums[2], "dec", 1)
    low_above = perm(sums[3], "dec", -1)
    base_got = perm(base_other, "core", 1)
    parts = lax.all_to_all(dense, ENC, 0, 0, tiled=True).reshape(NZ * NX, NC, DEC, HALF)
    low_below, top_above, top_below, low_above, base_got, parts = phase(
        low_below, top_above, top_below, low_above, base_got, parts
    )
    enc_grad, ctx = finish(
        xs, base, base_got, (top_below, low_below, top_above, low_above), parts
    )
    return ctx, enc_grad


def solution(mesh):
    grid = Mesh(mesh.devices.reshape(NZ, NX, NC, NY), ("z", "x", "core", "dec"))
    return jax.shard_map(
        body,
        mesh=grid,
        in_specs=(
            P(ENC, None),
            P(ENC, "dec"),
            P(ENC, "dec"),
            P(ENC, None, "dec"),
            P(ENC, None, "dec"),
            P(ENC, None),
            P(ENC, None),
        ),
        out_specs=(P(ENC, None, "dec"), P(ENC, "dec")),
        check_vma=False,
    )
```

```python
import functools

import jax
import jax.numpy as jnp
from jax import lax
from jax.experimental import pallas as pl
from jax.experimental.pallas import tpu as pltpu
from jax.sharding import Mesh, PartitionSpec as P

BF = jnp.bfloat16
F32 = jnp.float32
NZ, NX, NC, NY = 4, 4, 2, 4
ENC = ("z", "x", "core")
ROWS = 512
D = 4096
HALF = 512
CHUNK = 256
PIECE = 576
DEC = 16
NPASS = 4
QUADS = 2
LANES = 256
LOW = -1e30
HIDDEN = pl.CostEstimate(flops=200_000_000, bytes_accessed=0, transcendentals=0)
NT = (((1,), (1,)), ((), ()))
TN = (((0,), (0,)), ((), ()))


def perm(v, axis, shift):
    n = {"z": NZ, "x": NX, "core": NC, "dec": NY}[axis]
    return lax.ppermute(v, axis, [(i, (i + shift) % n) for i in range(n)])


def phase(*values):
    return lax.optimization_barrier(values)


def params(mib):
    return pltpu.CompilerParams(vmem_limit_bytes=mib * 1024 * 1024)


def pair_perm(v, axis, odd):
    turn = (lambda i: i + 1 - 2 * (i % 2)) if not odd else (lambda i: i - 1 + 2 * (i % 2))
    return lax.ppermute(v, axis, [(i, turn(i) % 4) for i in range(4)])


def join_kernel(*refs):
    outs = refs[8:]
    rows = PIECE // 2
    for k, out in enumerate(outs):
        out[:rows] = refs[2 * k][...]
        out[rows:] = refs[2 * k + 1][...]


def join(pairs):
    return pl.pallas_call(
        join_kernel,
        out_shape=[jax.ShapeDtypeStruct((PIECE, CHUNK), BF)] * 4,
        compiler_params=params(16),
        cost_estimate=HIDDEN,
    )(*[v for p in pairs for v in p])


def first_kernel(place, joined0, second0, joined1, second1, out):
    mid = PIECE // 2
    odd = place[0] % 2

    def slot(o, h, value):
        at = (o % 2) * PIECE + h * mid
        out[o // 2, at : at + mid, :] = value

    for h, joined, second in ((0, joined0, second0), (1, joined1, second1)):
        slot(0, h, joined[:mid])
        slot(2, h, second[mid:])
        for parity in range(2):
            @pl.when(odd == parity)
            def near():
                one = 1 if h == parity else 3
                slot(one, h, joined[mid:])
                slot(4 - one, h, second[:mid])


def first_block(place, pieces):
    def whole(p):
        return pl.BlockSpec(p.shape, lambda i, o: (0, 0))

    return pl.pallas_call(
        first_kernel,
        grid_spec=pltpu.PrefetchScalarGridSpec(
            num_scalar_prefetch=1,
            grid=(1,),
            in_specs=[whole(p) for p in pieces],
            out_specs=pl.BlockSpec((2, 2 * PIECE, CHUNK), lambda i, o: (0, 0, 0)),
        ),
        out_shape=jax.ShapeDtypeStruct((2, 2 * PIECE, CHUNK), BF),
        compiler_params=params(16),
        cost_estimate=HIDDEN,
    )(place, *pieces)


def halves_kernel(up_ref, down_ref, first_ref, second_ref):
    first_ref[...] = up_ref[0]
    second_ref[...] = down_ref[0]


def take_halves(up, down):
    half = (1, 2 * PIECE, CHUNK)
    return pl.pallas_call(
        halves_kernel,
        grid=(1,),
        in_specs=[pl.BlockSpec(half, lambda i: (0, 0, 0)), pl.BlockSpec(half, lambda i: (1, 0, 0))],
        out_specs=[pl.BlockSpec(half[1:], lambda i: (0, 0))] * 2,
        out_shape=[jax.ShapeDtypeStruct(half[1:], BF)] * 2,
        compiler_params=params(16),
        cost_estimate=HIDDEN,
    )(up, down)


def key_value(halves):
    rows = []
    for half in halves:
        for at in (0, PIECE):
            rows.append(
                jnp.concatenate(
                    [half[at : at + CHUNK, :], half[at + CHUNK : at + 2 * CHUNK, :]], axis=1
                )
            )
    return jnp.concatenate(rows, axis=0)


def near_kernel(pos, own_ref, oth_ref, *refs):
    blocks, (acc_refs, enc_refs, (qa_ref, qb_ref)) = refs[:6], (refs[6:8], refs[8:10], refs[10:])
    z, x = pos[0], pos[1]
    step = pl.program_id(0)

    def columns(ref, side, outer, inners):
        parts = []
        for inner in inners:
            zo, xo = (outer, inner) if side == 0 else (inner, outer)
            chip = ((z + zo) & 3) * 4 + ((x + xo) & 3)
            parts.append(ref[:, pl.ds(pl.multiple_of(chip * CHUNK, CHUNK), CHUNK)])
        return jnp.concatenate(parts, axis=1)

    def run(ref):
        for side in range(2):
            total = None
            for b, outer in enumerate((0, 1, 3)):
                block = blocks[side * 3 + b]
                rhs = key_value([block.at[h] for h in range(2)])
                lhs = columns(ref, side, outer, range(4))
                term = jnp.dot(lhs, rhs, preferred_element_type=F32)
                total = term if total is None else total + term
            acc_refs[side][0] = total
            enc_refs[side][0] = columns(ref, side, 2, range(4))

    pl.when(step < 2)(lambda: run(own_ref))
    pl.when(step >= 2)(lambda: run(oth_ref))

    @pl.when(step == 0)
    def questions():
        for side, out in ((0, qa_ref), (1, qb_ref)):
            for b, outer in enumerate((0, 1, 3)):
                for inner in range(4):
                    row = (inner % 2) * PIECE + 512
                    at = (outer * 4 + inner) * 64
                    out[at : at + 64, :] = blocks[side * 3 + b][inner // 2, row : row + 64]
            out[512:768, :] = jnp.zeros((256, CHUNK), BF)


def project_near(pos, own, other, blocks):
    tile = ROWS // 2
    fixed = pl.BlockSpec((1024, CHUNK), lambda i, o: (0, 0))
    return pl.pallas_call(
        near_kernel,
        grid_spec=pltpu.PrefetchScalarGridSpec(
            num_scalar_prefetch=1,
            grid=(4,),
            in_specs=[
                pl.BlockSpec((tile, D), lambda i, o: (jnp.minimum(i, 1), 0)),
                pl.BlockSpec((tile, D), lambda i, o: (jnp.maximum(i - 2, 0), 0)),
            ]
            + [pl.BlockSpec(b.shape, lambda i, o: (0, 0, 0)) for b in blocks],
            out_specs=[
                pl.BlockSpec((1, tile, HALF), lambda i, o: (i // 2, i % 2, 0)),
                pl.BlockSpec((1, tile, HALF), lambda i, o: (i // 2, i % 2, 0)),
                pl.BlockSpec((1, tile, 1024), lambda i, o: (i // 2, i % 2, 0)),
                pl.BlockSpec((1, tile, 1024), lambda i, o: (i // 2, i % 2, 0)),
                fixed,
                fixed,
            ],
        ),
        out_shape=[
            jax.ShapeDtypeStruct((2, ROWS, HALF), F32),
            jax.ShapeDtypeStruct((2, ROWS, HALF), F32),
            jax.ShapeDtypeStruct((2, ROWS, 1024), BF),
            jax.ShapeDtypeStruct((2, ROWS, 1024), BF),
            jax.ShapeDtypeStruct((1024, CHUNK), BF),
            jax.ShapeDtypeStruct((1024, CHUNK), BF),
        ],
        compiler_params=params(26),
        cost_estimate=HIDDEN,
    )(pos, own, other, *blocks)


class Passages:
    def __init__(self, pos, own, other):
        self.z, self.x = pos[0], pos[1]
        self.numbers = (own, other)

    def question(self, side, p):
        return self.numbers[side][NPASS + p]

    def start(self, side, p):
        at = 0
        for k in range(p):
            at = at + self.numbers[side][k]
        return at

    def chip(self, side, p):
        q = self.question(side, p)
        return ((q >> 3) - self.z) & 3, ((q >> 1) - self.x) & 3, q & 1

    def row(self, half, side, p):
        zo, xo, core = self.chip(side, p)
        outer, inner = (zo, xo) if half == 0 else (xo, zo)
        return (outer * 4 + inner) * 64 + core * 16


def head_of_column(rows):
    return lax.broadcasted_iota(jnp.int32, (rows, LANES), 1) // 64


def head_matrix(meta, q_ref, side, quad, which):
    head = head_of_column(DEC)
    parts = []
    for p in range(NPASS):
        row = pl.multiple_of(meta.row(quad, side, p) + which * 32, 16)
        tile = q_ref[pl.ds(row, DEC), :]
        parts += [jnp.where(head == a, tile, jnp.zeros_like(tile)) for a in range(4)]
    return jnp.concatenate(parts, axis=0)


def lane_value(numbers):
    lane = lax.broadcasted_iota(jnp.int32, (1, LANES), 1) // 64
    value = jnp.zeros((1, LANES), jnp.int32)
    for p in range(NPASS):
        value = jnp.where(lane == p, numbers[p], value)
    return value


def inside_mask(meta, side):
    row = lax.broadcasted_iota(jnp.int32, (ROWS, LANES), 0)
    starts = [meta.start(side, p) for p in range(NPASS + 1)]
    return (row >= lane_value(starts[:NPASS])) & (row < lane_value(starts[1:]))


def dot_nt(a, b):
    return lax.dot_general(a, b, NT, preferred_element_type=F32)


def forward_side(side, quad, meta, k, v, q_ref, put, num_ref):
    inside = inside_mask(meta, side)
    scores = dot_nt(k, head_matrix(meta, q_ref, side, quad, 0))
    scores = jnp.where(inside, scores, LOW)
    top = jnp.max(scores, axis=0, keepdims=True)
    unnorm = jnp.exp(scores - top)
    unnorm_b = unnorm.astype(BF)
    dprob = dot_nt(v, head_matrix(meta, q_ref, side, quad, 1))
    put(0, top)
    put(1, jnp.sum(unnorm, axis=0, keepdims=True))
    put(2, jnp.sum(unnorm_b.astype(F32) * dprob, axis=0, keepdims=True))
    num_ref[side] = lax.dot_general(v, unnorm_b, TN, preferred_element_type=F32)


def far_kernel(quad, pos, own_numbers, other_numbers, *refs):
    meta = Passages(pos, own_numbers, other_numbers)
    enc_ref, acc_ref, top, low, q_in = refs[:5]
    before_ref = refs[5] if quad else None
    k_ref, v_ref, q_ref, st_ref, num_ref = refs[-5:]
    step = pl.program_id(0)

    @pl.when(step == 0)
    def questions():
        q_ref[...] = q_in[...]
        for inner in range(4):
            row = (inner % 2) * PIECE + 512
            at = (8 + inner) * 64
            q_ref[at : at + 64, :] = (top, low)[inner // 2][row : row + 64, :]

    total = acc_ref[0] + jnp.dot(
        enc_ref[0], key_value((top, low)), preferred_element_type=F32
    )
    keys, values = total[:, :CHUNK].astype(BF), total[:, CHUNK:].astype(BF)
    k_ref[step] = keys
    v_ref[step] = values

    def put_all(row, value):
        st_ref[:, row : row + 1, :] = jnp.broadcast_to(value[None], (NZ * NX, 1, LANES))

    for side in range(2):
        def put(r, value):
            if quad:
                put_all(4 * r + side * 2 + 1, value)
            else:
                st_ref[r * 2 + side : r * 2 + side + 1, :] = value

        @pl.when(step == side)
        def attend():
            forward_side(side, quad, meta, k_ref[side], v_ref[side], q_ref, put, num_ref)
            if quad:
                question = lane_value([meta.question(side, p) for p in range(NPASS)]).astype(F32)
                for r in range(3):
                    put_all(4 * r + side * 2, before_ref[r * 2 + side : r * 2 + side + 1, :])
                for q in range(QUADS):
                    put_all(12 + side * 2 + q, question)


def project_far(quad, meta, enc_far, acc, blocks, q, before):
    def whole(shape):
        return pl.BlockSpec(shape, lambda i, *m: (0,) * len(shape))

    stats = (NZ * NX, 16, LANES) if quad else (8, LANES)
    shapes = [
        jax.ShapeDtypeStruct((2, ROWS, CHUNK), BF),
        jax.ShapeDtypeStruct((2, ROWS, CHUNK), BF),
        jax.ShapeDtypeStruct((1024, CHUNK), BF),
        jax.ShapeDtypeStruct(stats, F32),
        jax.ShapeDtypeStruct((2, LANES, CHUNK), F32),
    ]
    extra = [before] if quad else []
    return pl.pallas_call(
        functools.partial(far_kernel, quad),
        grid_spec=pltpu.PrefetchScalarGridSpec(
            num_scalar_prefetch=3,
            grid=(2,),
            in_specs=[
                pl.BlockSpec((1, ROWS, 1024), lambda i, *m: (i, 0, 0)),
                pl.BlockSpec((1, ROWS, HALF), lambda i, *m: (i, 0, 0)),
            ]
            + [whole(b.shape) for b in blocks + [q] + extra],
            out_specs=[whole(s.shape) for s in shapes],
        ),
        out_shape=shapes,
        compiler_params=params(20),
        cost_estimate=HIDDEN,
    )(*meta, enc_far, acc, *blocks, q, *extra)


def combine(meta, st_ref):
    n = st_ref.shape[0]
    own_question = [
        lane_value([meta.question(s, p) for p in range(NPASS)]).astype(F32) for s in range(2)
    ]

    def turned(value, k):
        return pltpu.roll(value, 64 * k, 1) if k else value

    tops = [None, None]
    for d in range(n):
        for k in range(NPASS):
            q, m = turned(st_ref[d, 12:16], k), turned(st_ref[d, 0:4], k)
            for s in range(2):
                term = jnp.where(q == own_question[s], m, LOW)
                tops[s] = term if tops[s] is None else jnp.maximum(tops[s], term)
    tops = [jnp.maximum(t[0:QUADS], t[QUADS:]) for t in tops]
    both = [jnp.concatenate([t, t], axis=0) for t in tops]
    totals, deltas = [0.0, 0.0], [0.0, 0.0]
    for d in range(n):
        for k in range(NPASS):
            q, m = turned(st_ref[d, 12:16], k), turned(st_ref[d, 0:4], k)
            l, e = turned(st_ref[d, 4:8], k), turned(st_ref[d, 8:12], k)
            for s in range(2):
                hit = q == own_question[s]
                scale = jnp.where(hit, jnp.exp(jnp.where(hit, m - both[s], 0.0)), 0.0)
                totals[s] = totals[s] + scale * l
                deltas[s] = deltas[s] + scale * e
    inverse = [1.0 / (t[0:QUADS] + t[QUADS:]) for t in totals]
    deltas = [(t[0:QUADS] + t[QUADS:]) * i for t, i in zip(deltas, inverse)]
    return tops, inverse, deltas


def take_weights(place, sources, w_ref):
    a_own, a_up, a_top, a_low, a_down, b_own, b_up, b_top, b_low, b_down = sources
    both = 2 * CHUNK
    for outer in range(4):
        @pl.when(place == outer)
        def take_a():
            for n in range(4):
                rows = pl.ds((n % 2) * PIECE, both)
                if outer == 2:
                    w_ref[0, n] = (a_top, a_low)[n // 2][rows, :]
                else:
                    w_ref[0, n] = (a_own, a_up, None, a_down)[outer][n // 2, rows, :]

    upper = place // 2
    rows = pl.ds(pl.multiple_of((place % 2) * PIECE, 64), both)
    for h, ref in ((0, b_top), (1, b_low)):
        @pl.when(upper == h)
        def take_b():
            w_ref[1, 2] = ref[rows, :]


def weights_tile(place, sources, w_ref):
    b_own, b_up, b_down = sources[5], sources[6], sources[9]

    def piece(side, n, t):
        if side == 0 or n == 2:
            return w_ref[side, n, t * CHUNK : (t + 1) * CHUNK]
        row = pl.multiple_of((place % 2) * PIECE + t * CHUNK, 64)
        return {0: b_own, 1: b_up, 3: b_down}[n][place // 2, pl.ds(row, CHUNK), :]

    rows = [
        jnp.concatenate([piece(side, n, t) for t in range(2) for side in range(2)], axis=1)
        for n in range(4)
    ]
    return jnp.concatenate(rows, axis=0)


def weight_specs():
    shape = (2, 2 * PIECE, CHUNK)
    block = pl.BlockSpec(shape, lambda i, *p: (0, 0, 0), pipeline_mode=pl.Buffered(1))
    half = pl.BlockSpec(shape[1:], lambda i, *p: (0, 0), pipeline_mode=pl.Buffered(1))
    return [block, block, half, half, block] * 2


WEIGHT_SCRATCH = pltpu.VMEM((2, 4, 2 * CHUNK, CHUNK), BF)


def backward_kernel(
    pos, own_numbers, other_numbers, ka_ref, va_ref, qa_ref, na_ref, kb_ref, vb_ref, qb_ref, nb_ref,
    st_ref, *refs
):
    sources, outs = refs[:10], refs[10:]
    kvg_ref, own_ref, oth_ref, dense_ref, ctx_ref, w_ref = outs
    take_weights(pos[2], sources, w_ref)
    meta = Passages(pos, own_numbers, other_numbers)
    halves = ((ka_ref, va_ref, qa_ref, na_ref), (kb_ref, vb_ref, qb_ref, nb_ref))
    tops, inverses, deltas = combine(meta, st_ref)
    here = meta.z * 4 + meta.x
    ctx_ref[...] = jnp.zeros_like(ctx_ref)
    head = head_of_column(DEC)
    for side in (1, 0):
        inside = inside_mask(meta, side)
        for quad in range(QUADS):
            cols = slice(quad * CHUNK, (quad + 1) * CHUNK)
            at = side * QUADS + quad
            top, inverse = tops[side][quad : quad + 1], inverses[side][quad : quad + 1]
            k_ref, v_ref, q_ref, num_ref = halves[quad]
            queries = head_matrix(meta, q_ref, side, quad, 0)
            grads = head_matrix(meta, q_ref, side, quad, 1)
            scores = dot_nt(k_ref[side], queries)
            unnorm = jnp.where(inside, jnp.exp(jnp.where(inside, scores - top, 0.0)), 0.0)
            probs = unnorm * inverse
            dprob = dot_nt(v_ref[side], grads)
            ds = (probs * (dprob - deltas[side][quad : quad + 1])).astype(BF)
            for t, lanes, weight in ((0, queries, ds), (1, grads, probs.astype(BF))):
                turned = lax.dot_general(
                    lanes, weight, (((0,), (1,)), ((), ())), preferred_element_type=F32
                ).astype(BF)
                first = t * HALF + quad * CHUNK
                kvg_ref[first : first + CHUNK, side * ROWS : (side + 1) * ROWS] = turned
            scale = jnp.exp(st_ref[here, at : at + 1, :] - top) * inverse
            context = (num_ref[side] * scale).T
            for p in range(NPASS):
                part = jnp.zeros((DEC, CHUNK), F32)
                for a in range(4):
                    first = p * 64 + a * DEC
                    part = jnp.where(head == a, context[first : first + DEC], part)
                ctx_ref[meta.question(side, p), :, cols] += part
    total = jnp.dot(weights_tile(pos[2], sources, w_ref), kvg_ref[...], preferred_element_type=F32)
    own_ref[...] = total[:, :ROWS].astype(BF)
    oth_ref[...] = total[:, ROWS:].astype(BF)
    dense_ref[...] = ctx_ref[...].astype(BF)


def backward(meta, args, weights):
    def whole(shape):
        return pl.BlockSpec(shape, lambda i, *m: (0,) * len(shape))

    shapes = [
        jax.ShapeDtypeStruct((2 * HALF, 2 * ROWS), BF),
        jax.ShapeDtypeStruct((1024, ROWS), BF),
        jax.ShapeDtypeStruct((1024, ROWS), BF),
        jax.ShapeDtypeStruct((32, DEC, HALF), BF),
    ]
    return pl.pallas_call(
        backward_kernel,
        grid_spec=pltpu.PrefetchScalarGridSpec(
            num_scalar_prefetch=3,
            grid=(1,),
            in_specs=[whole(a.shape) for a in args]
            + weight_specs(),
            out_specs=[whole(s.shape) for s in shapes],
            scratch_shapes=[pltpu.VMEM((32, DEC, HALF), F32), WEIGHT_SCRATCH],
        ),
        out_shape=shapes,
        compiler_params=params(34),
        cost_estimate=HIDDEN,
    )(*meta, *args, *weights)


def base_kernel(places, kvg_ref, *refs):
    sources, (base_ref, other_ref, w_ref) = refs[:10], refs[10:]
    take_weights(places[0], sources, w_ref)
    total = jnp.dot(weights_tile(places[0], sources, w_ref), kvg_ref[...], preferred_element_type=F32)
    base_ref[...] = total[:, :ROWS]
    other_ref[...] = total[:, ROWS:].astype(BF)


def base_blocks(places, kvg, weights):
    out = pl.BlockSpec((1024, ROWS), lambda i, p: (0, 0))
    return pl.pallas_call(
        base_kernel,
        grid_spec=pltpu.PrefetchScalarGridSpec(
            num_scalar_prefetch=1,
            grid=(1,),
            in_specs=[pl.BlockSpec(kvg.shape, lambda i, p: (0, 0))] + weight_specs(),
            out_specs=[out] * 2,
            scratch_shapes=[WEIGHT_SCRATCH],
        ),
        out_shape=[jax.ShapeDtypeStruct((1024, ROWS), t) for t in (F32, BF)],
        compiler_params=params(34),
        cost_estimate=HIDDEN,
    )(places, kvg, *weights)


def far_sums_kernel(own_ref, got_ref, top_ref, low_ref):
    for h, out in enumerate((top_ref, low_ref)):
        rows = slice(h * 512, (h + 1) * 512)
        out[...] = (own_ref[rows].astype(F32) + got_ref[rows].astype(F32)).astype(BF)


def far_sums(own, got):
    return pl.pallas_call(
        far_sums_kernel,
        out_shape=[jax.ShapeDtypeStruct((512, ROWS), BF)] * 2,
        compiler_params=params(16),
        cost_estimate=HIDDEN,
    )(own, got)


def near_grad_kernel(places, kvg_ref, *refs):
    sources, (out_ref, w_ref) = refs[:10], refs[10:]
    take_weights(places[pl.program_id(0)], sources, w_ref)
    total = jnp.dot(weights_tile(places[pl.program_id(0)], sources, w_ref), kvg_ref[...], preferred_element_type=F32)
    core = places[2]
    out_ref[core, 0] = total[:, :ROWS].astype(BF)
    out_ref[1 - core, 0] = total[:, ROWS:].astype(BF)


def near_blocks(places, kvg, weights):
    return pl.pallas_call(
        near_grad_kernel,
        grid_spec=pltpu.PrefetchScalarGridSpec(
            num_scalar_prefetch=1,
            grid=(2,),
            in_specs=[pl.BlockSpec(kvg.shape, lambda i, p: (0, 0))] + weight_specs(),
            out_specs=pl.BlockSpec((2, 1, 1024, ROWS), lambda i, p: (0, i, 0, 0)),
            scratch_shapes=[WEIGHT_SCRATCH],
        ),
        out_shape=jax.ShapeDtypeStruct((2, 2, 1024, ROWS), BF),
        compiler_params=params(34),
        cost_estimate=HIDDEN,
    )(places, kvg, *weights)


def sums_kernel(near_ref, below_ref, above_ref, *outs):
    for out, k, h, more in zip(outs, (0, 1, 0, 1), (1, 0, 0, 1), (None, None, below_ref, above_ref)):
        rows = slice(h * 512, (h + 1) * 512)
        total = near_ref[0, k, rows].astype(F32) + near_ref[1, k, rows].astype(F32)
        if more is not None:
            total = total + more[...].astype(F32)
        out[...] = total.astype(BF)


def near_sums(near, below, above):
    return pl.pallas_call(
        sums_kernel,
        out_shape=[jax.ShapeDtypeStruct((512, ROWS), BF)] * 4,
        compiler_params=params(16),
        cost_estimate=HIDDEN,
    )(near, below, above)


def finish_kernel(
    place, base_ref, core_ref, up_top, up_low, down_top, down_low, parts_ref, out_ref, ctx_ref
):
    step = pl.program_id(0)

    @pl.when(step == 0)
    def context():
        for core in range(2):
            total = parts_ref[0, core].astype(F32)
            for n in range(1, NZ * NX):
                total = total + parts_ref[n, core].astype(F32)
            ctx_ref[0, :, core * HALF : (core + 1) * HALF] = total

    total = base_ref[...] + core_ref[...].astype(F32)

    def write(up, down):
        whole = total + up[...].astype(F32) + down[...].astype(F32)
        out_ref[...] = whole.T

    pl.when(step < 2)(lambda: write(up_top, down_top))
    pl.when(step >= 2)(lambda: write(up_low, down_low))


def finish(place, base, core_part, parts, ctx_parts):
    shape = (CHUNK, ROWS)
    block = pl.BlockSpec(shape, lambda n, p: (n, 0))
    top = pl.BlockSpec(shape, lambda n, p: (jnp.minimum(n, 1), 0))
    low = pl.BlockSpec(shape, lambda n, p: (jnp.maximum(n - 2, 0), 0))
    return pl.pallas_call(
        finish_kernel,
        grid_spec=pltpu.PrefetchScalarGridSpec(
            num_scalar_prefetch=1,
            grid=(4,),
            in_specs=[block, block, top, low, top, low]
            + [pl.BlockSpec(ctx_parts.shape, lambda n, p: (0, 0, 0, 0))],
            out_specs=[
                pl.BlockSpec((ROWS, CHUNK), lambda n, p: (0, p[n])),
                pl.BlockSpec((1, DEC, 2 * HALF), lambda n, p: (0, 0, 0)),
            ],
        ),
        out_shape=[
            jax.ShapeDtypeStruct((ROWS, 4 * CHUNK), F32),
            jax.ShapeDtypeStruct((1, DEC, 2 * HALF), F32),
        ],
        compiler_params=params(16),
        cost_estimate=HIDDEN,
    )(place, base, core_part, *parts, ctx_parts)


def body(enc_rows, key_weight, value_weight, queries, ctx_grad, passage_len, passage_question):
    z, x, core, y = (lax.axis_index(a) for a in ("z", "x", "core", "dec"))
    four = jnp.arange(4, dtype=jnp.int32)
    zs, xs = (z + four) % 4, (x + four) % 4
    places = ((y + four - z) % 4).astype(jnp.int32)
    near_places = jnp.stack([places[1], places[3], core.astype(jnp.int32)])
    base_place = places[0:1]
    pos = jnp.stack([z, x, places[2]]).astype(jnp.int32)

    cat = jnp.concatenate([key_weight, value_weight, queries[0], ctx_grad[0]], axis=0)
    mine = lax.dynamic_slice_in_dim(cat, core * HALF, HALF, 1)
    theirs = lax.dynamic_slice_in_dim(cat, (1 - core) * HALF, HALF, 1)
    got = perm(theirs, "core", 1)
    numbers = jnp.concatenate([passage_len[0], passage_question[:, 0]])
    other_numbers = perm(numbers, "core", 1)
    enc_after, got = phase(enc_rows, got)
    enc_other = perm(enc_after, "core", 1)
    first = jnp.where(core == 0, mine, got)
    second = jnp.where(core == 0, got, mine)
    chip = jnp.concatenate(
        [v[a:b] for a, b in ((0, 128), (128, 256), (256, 272), (272, 288)) for v in (first, second)],
        axis=0,
    )
    mid = PIECE // 2
    halves = phase(
        *[chip[h * mid : (h + 1) * mid, c : c + CHUNK] for c in (0, CHUNK) for h in (0, 1)]
    )

    steps = [(v, a, h) for v, (a, h) in zip(halves, (("x", 0), ("x", 1), ("z", 0), ("z", 1)))]
    met, pos, near_places, base_place, x_place, xs = phase(
        [pair_perm(v, a, h) for v, a, h in steps],
        pos,
        near_places,
        base_place,
        x.astype(jnp.int32).reshape(1),
        xs.astype(jnp.int32),
    )
    joined = phase(*join(list(zip(halves, met))))
    second = [pair_perm(v, a, 1 - h) for v, (_, a, h) in zip(joined, steps)]
    a_own = first_block(x_place, (joined[0], second[0], joined[1], second[1]))
    b_own = first_block(pos[0:1], (joined[2], second[2], joined[3], second[3]))
    enc_other, other_numbers, a_own, b_own = phase(enc_other, other_numbers, a_own, b_own)

    a_up, a_down = phase(perm(a_own, "z", -1), perm(a_own, "z", 1))
    b_up, b_down = phase(perm(b_own, "x", -1), perm(b_own, "x", 1))
    a_first, a_second = phase(*take_halves(a_up, a_down))
    b_first, b_second = phase(*take_halves(b_up, b_down))
    far = [
        perm(a_first, "z", -1),
        perm(a_second, "z", 1),
        perm(b_first, "x", -1),
        perm(b_second, "x", 1),
    ]
    acc_a, acc_b, enc_a, enc_b, qa, qb = project_near(
        pos, enc_rows, enc_other, [a_own, a_up, a_down, b_own, b_up, b_down]
    )
    meta = (pos, numbers, other_numbers)
    acc_a, acc_b, enc_a, enc_b, qa, qb, far[0], far[1] = phase(
        acc_a, acc_b, enc_a, enc_b, qa, qb, *far[:2]
    )
    ka, va, qa, stats_a, numer_a = project_far(0, meta, enc_a, acc_a, far[:2], qa, None)
    stats_a, far[2], far[3] = phase(stats_a, far[2], far[3])
    kb, vb, qb, stats, numer_b = project_far(1, meta, enc_b, acc_b, far[2:], qb, stats_a)
    stats_all = lax.all_to_all(stats, ("z", "x"), 0, 0, tiled=True)
    weights = [a_own, a_up, far[0], far[1], a_down, b_own, b_up, far[2], far[3], b_down]
    kvg, far_own, far_other, dense = backward(
        meta, (ka, va, qa, numer_a, kb, vb, qb, numer_b, stats_all), weights
    )

    far_got = perm(far_other, "core", 1)
    base, base_other = base_blocks(base_place, kvg, weights)
    far_got, far_own, base, base_other, kvg, dense = phase(
        far_got, far_own, base, base_other, kvg, dense
    )

    far_top, far_low, base, base_other, kvg, dense = phase(
        *far_sums(far_own, far_got), base, base_other, kvg, dense
    )
    from_below = perm(far_top, "dec", 1)
    from_above = perm(far_low, "dec", -1)
    near = lax.all_to_all(near_blocks(near_places, kvg, weights), "core", 0, 0, tiled=True)
    from_below, from_above, near, base, base_other, dense = phase(
        from_below, from_above, near, base, base_other, dense
    )

    *sums, dense, base_other = phase(
        *near_sums(near, from_below, from_above), dense, base_other
    )
    low_below = perm(sums[0], "dec", 1)
    top_above = perm(sums[1], "dec", -1)
    top_below = perm(sums[2], "dec", 1)
    low_above = perm(sums[3], "dec", -1)
    base_got = perm(base_other, "core", 1)
    parts = lax.all_to_all(dense, ENC, 0, 0, tiled=True).reshape(NZ * NX, NC, DEC, HALF)
    low_below, top_above, top_below, low_above, base_got, parts = phase(
        low_below, top_above, top_below, low_above, base_got, parts
    )
    enc_grad, ctx = finish(
        xs, base, base_got, (top_below, low_below, top_above, low_above), parts
    )
    return ctx, enc_grad


def solution(mesh):
    grid = Mesh(mesh.devices.reshape(NZ, NX, NC, NY), ("z", "x", "core", "dec"))
    return jax.shard_map(
        body,
        mesh=grid,
        in_specs=(
            P(ENC, None),
            P(ENC, "dec"),
            P(ENC, "dec"),
            P(ENC, None, "dec"),
            P(ENC, None, "dec"),
            P(ENC, None),
            P(ENC, None),
        ),
        out_specs=(P(ENC, None, "dec"), P(ENC, "dec")),
        check_vma=False,
    )
```
